32 devices in a mesh: user: 4 (over x, core), tok: 8 (over z, y).
Axes of the slice: x: 2, y: 2, z: 4, core: 2. Of those that a mesh axis runs over, the one named last changes fastest.
Arguments:
- hidden: bfloat16 [4, 1024, 16384], P('user', 'tok'), may hold values from -256 to 256, as said below
- cotangent: bfloat16 [4, 1024, 2048], P('user', 'tok'), may hold values from -6 to 6
- lengths: int32 [4], P('user'), may hold values from 256 to 1024
Outputs:
- clipped_sum: float32 [16384, 2048], P('tok', 'user')
The draws below stay inside these ranges and needn't reach their ends.
Inputs may be any that keep to these rules, and one draw needn't show every extreme that they name: bfloat16 activations of mixed magnitudes across tokens and hidden units.
All inputs are finite; a program needn't handle non-finite values.
Results may differ from the reference program's by a relative error of at most 0.0003.
Values may be sent and summed in bfloat16 or wider, within the bound.
No kernel may reach another device: no remote copies, remote signals or barrier semaphores. Data moves between devices by JAX's collectives and lax.ppermute only.
A program may use at most 128 MiB of HBM per device.

```python
import math
import jax
import jax.numpy as jnp
from jax import lax

D = 2048
FF = 16384
CAP = 1024
USERS = 4


def draw_hidden(key, part):
    key_base = jax.random.fold_in(key, 11)
    key_cols = jax.random.fold_in(key, 12)
    key_rows = jax.random.fold_in(key, 13)
    base = jnp.clip(jax.random.normal(key_base, (USERS, CAP, FF), jnp.float32), -6.0, 6.0)
    trend = jnp.exp(math.log(3.0) * jnp.arange(FF, dtype=jnp.float32) / FF)
    column = jnp.exp(jax.random.uniform(key_cols, (FF,), jnp.float32, -1.15, 1.15)) * trend
    row_scale = jnp.exp(jax.random.uniform(key_rows, (USERS, CAP, 1), jnp.float32, math.log(0.3), math.log(3.0)))
    values = base * row_scale * column
    return jnp.clip(values, -256.0, 256.0).astype(jnp.bfloat16)


def with_ends(entries, rng, smallest, largest):
    index_at = [jax.random.randint(jax.random.fold_in(rng, axis), (), 0, length) for axis, length in enumerate(entries.shape)]
    longest = entries.shape.index(max(entries.shape))
    neighbour = index_at[:longest] + [(index_at[longest] + 1) % entries.shape[longest]] + index_at[longest + 1:]
    return entries.at[tuple(index_at)].set(smallest).at[tuple(neighbour)].set(largest)


def levels(stream_key, extent, split, least, largest):
    level, own = 1.0, jax.random.fold_in(stream_key, 6)
    for axis_at, blocks in split:
        steps = jnp.exp(jax.random.uniform(jax.random.fold_in(own, axis_at), (blocks,), jnp.float32, least / len(split), largest / len(split)))
        level = level * jnp.repeat(steps, extent[axis_at] // blocks).reshape([-1 if axis == axis_at else 1 for axis in range(len(extent))])
    return level


def normal_values(own_key, shape, scale, reach, pieces=(), kind=jnp.bfloat16):
    array = scale * jax.random.normal(own_key, shape, jnp.float32)
    if pieces:
        array = array * levels(own_key, shape, pieces, -0.22, 0.18)
    return jnp.clip(array, -reach, reach).astype(kind)


def setup_inputs(seed: int = 0) -> dict:
    seeds = jax.random.split(jax.random.key(seed), 4)
    return {
        "hidden": draw_hidden(jax.random.fold_in(seeds[3], 71), 0),
        "cotangent": normal_values(seeds[1], (USERS, CAP, D), 1.0, 6.0, ((0, 4), (1, 8))),
        "lengths": with_ends(jax.random.randint(seeds[2], (USERS,), CAP // 4, CAP + 1), jax.random.fold_in(seeds[2], 1), CAP // 4, CAP).astype(jnp.int32),
    }


epsilon = 1e-06

def reference(hidden, cotangent, lengths):
    clip_bound = math.sqrt(8.0 * FF * D * CAP)
    scaling = math.sqrt(FF * D) / (USERS * clip_bound)

    def one_user(running, inputs):
        user_rows, user_cot, user_length = inputs
        keep_rows = jnp.arange(CAP, dtype=jnp.int32) < user_length
        masked = jnp.where(keep_rows[:, None], user_cot, jnp.zeros_like(user_cot))
        gradient = jnp.dot(user_rows.astype(jnp.float32).T, masked.astype(jnp.float32), precision=lax.Precision.HIGHEST)
        norm_sq = jnp.sum(gradient * gradient)
        factor = jnp.minimum(1.0, clip_bound / jnp.sqrt(norm_sq + epsilon)) * scaling
        return (running + factor * gradient, None)
    running, unused = lax.scan(one_user, jnp.zeros((FF, D), jnp.float32), (hidden, cotangent, lengths))
    return running
```

```python
import math

import jax
import jax.numpy as jnp
from jax import lax
from jax.sharding import PartitionSpec as P

epsilon = 1e-06
pieces_wanted = 4


def contract(left, right):
    return lax.dot_general(
        left, right, (((0,), (0,)), ((), ())), preferred_element_type=jnp.float32
    )


def exchange(block, distance, user_count):
    return lax.ppermute(block, "user", [(u, u ^ distance) for u in range(user_count)])


def all_users(block, user_count):
    slots = {0: block}
    distance = user_count // 2
    while distance:
        for slot in list(slots):
            slots[slot ^ distance] = exchange(slots[slot], distance, user_count)
        distance //= 2
    return [slots[slot] for slot in range(user_count)]


def body(hidden, cotangent, lengths):
    tok_count = lax.axis_size("tok")
    user_count = lax.axis_size("user")
    tok_rows = hidden.shape[1]
    hidden_width = hidden.shape[2]
    model_width = cotangent.shape[2]
    capacity = tok_rows * tok_count
    own_width = hidden_width // tok_count
    pieces = pieces_wanted if own_width % (128 * pieces_wanted) == 0 else 1
    piece_width = own_width // pieces
    clip_bound = math.sqrt(8.0 * hidden_width * model_width * capacity)
    scaling = math.sqrt(hidden_width * model_width) / (user_count * clip_bound)
    own_user = lax.axis_index("user")
    slot_users = own_user ^ lax.iota(jnp.int32, user_count)

    position = lax.axis_index("tok") * tok_rows + lax.iota(jnp.int32, tok_rows)
    keep_rows = position < lengths[0]
    masked = jnp.where(keep_rows[:, None], cotangent[0], jnp.zeros_like(cotangent[0]))
    by_user = masked.reshape(tok_rows, user_count, model_width // user_count).transpose(1, 0, 2)
    by_user = lax.all_to_all(by_user, "user", split_axis=0, concat_axis=0, tiled=True)
    by_slot = jnp.take(by_user, slot_users, axis=0)
    right = lax.all_gather(by_slot, "tok", axis=1, tiled=True)

    split = hidden[0].reshape(tok_rows, tok_count, pieces, piece_width)
    products = []
    squares = jnp.zeros((user_count,), jnp.float32)
    for piece in range(pieces):
        outgoing = split[:, :, piece, :].transpose(1, 0, 2)
        columns = lax.all_to_all(outgoing, "tok", split_axis=0, concat_axis=0, tiled=True)
        columns = columns.reshape(capacity, piece_width)
        slots = all_users(columns, user_count)
        gradients = [contract(slots[s], right[s]) for s in range(user_count)]
        squares += jnp.stack([jnp.sum(g * g) for g in gradients])
        products.append(gradients)

    norm_sq = lax.psum(jnp.take(squares, slot_users), ("user", "tok"))
    factor = jnp.minimum(1.0, clip_bound / jnp.sqrt(norm_sq + epsilon)) * scaling
    slot_factor = jnp.take(factor, slot_users)
    rows = [sum(slot_factor[s] * g for s, g in enumerate(gradients)) for gradients in products]
    return jnp.concatenate(rows, axis=0)


def solution(mesh):
    return jax.shard_map(
        body,
        mesh=mesh,
        in_specs=(P("user", "tok", None), P("user", "tok", None), P("user")),
        out_specs=P("tok", "user"),
        check_vma=False,
    )
```

```python
import functools
import math

import jax
import jax.numpy as jnp
from jax import lax
from jax.experimental import pallas as pl
from jax.experimental.pallas import tpu as pltpu
from jax.sharding import PartitionSpec as P

epsilon = 1e-06
lanes = 128
edges = (0.0, 0.25, 0.5, 0.75, 0.875, 1.0)
ANY = pl.BlockSpec(memory_space=pl.ANY)


def exchange(block, axis, distance):
    size = lax.axis_size(axis)
    return lax.ppermute(block, axis, [(i, i ^ distance) for i in range(size)])


def doubling(block, axis):
    size = lax.axis_size(axis)
    slots = {0: block}
    distance = size // 2
    while distance:
        for slot in list(slots):
            slots[slot ^ distance] = exchange(slots[slot], axis, distance)
        distance //= 2
    return [slots[slot] for slot in range(size)]


def pack_kernel(start, stride, hidden_ref, *refs):
    out_ref, sems = refs[-2], refs[-1]
    count, _, width = out_ref.shape
    copies = [
        pltpu.make_async_copy(
            hidden_ref.at[0, :, pl.ds(k * stride + start, width)], out_ref.at[k], sems.at[k]
        )
        for k in range(count)
    ]
    for copy in copies:
        copy.start()
    for copy in copies:
        copy.wait()


def pack(hidden, count, start, width, after):
    _, rows, total = hidden.shape
    return pl.pallas_call(
        functools.partial(pack_kernel, start, total // count),
        out_shape=jax.ShapeDtypeStruct((count, rows, width), hidden.dtype),
        in_specs=[ANY] * (1 + len(after)),
        out_specs=ANY,
        scratch_shapes=[pltpu.SemaphoreType.DMA((count,))],
        cost_estimate=pl.CostEstimate(
            flops=0, bytes_accessed=4 * count * rows * width, transcendentals=0
        ),
        name="pack_columns",
    )(hidden, *after)


def mask_kernel(user_count, valid_ref, user_ref, cot_ref, out_ref):
    rows, width = out_ref.shape[1:]
    keep = lax.broadcasted_iota(jnp.int32, (rows, width), 0) < valid_ref[0]
    for slot in range(user_count):
        column = pl.multiple_of((user_ref[0] ^ slot) * width, lanes)
        block = cot_ref[0, :, pl.ds(column, width)]
        out_ref[slot] = jnp.where(keep, block, jnp.zeros_like(block))


def mask(valid, user, cotangent, user_count):
    _, rows, total = cotangent.shape
    smem = pl.BlockSpec(memory_space=pltpu.SMEM)
    return pl.pallas_call(
        functools.partial(mask_kernel, user_count),
        out_shape=jax.ShapeDtypeStruct((user_count, rows, total // user_count), cotangent.dtype),
        in_specs=[smem, smem, pl.BlockSpec(memory_space=pltpu.VMEM)],
        out_specs=pl.BlockSpec(memory_space=pltpu.VMEM),
        name="mask_cotangent",
    )(valid, user, cotangent)


def order_kernel(tok_ref, *refs):
    out_ref, sems = refs[-2], refs[-1]
    slots = refs[:-2]
    copies = [
        pltpu.make_async_copy(slot_ref, out_ref.at[:, tok_ref[0] ^ s], sems.at[s])
        for s, slot_ref in enumerate(slots)
    ]
    for copy in copies:
        copy.start()
    for copy in copies:
        copy.wait()


def order(tok, slots):
    users, rows, width = slots[0].shape
    count = len(slots)
    return pl.pallas_call(
        order_kernel,
        out_shape=jax.ShapeDtypeStruct((users, count, rows, width), slots[0].dtype),
        in_specs=[pl.BlockSpec(memory_space=pltpu.SMEM)] + [ANY] * count,
        out_specs=ANY,
        scratch_shapes=[pltpu.SemaphoreType.DMA((count,))],
        name="order_tokens",
    )(tok, *slots)


def product_kernel(user_count, first, *refs):
    lefts, right_ref = refs[:user_count], refs[user_count]
    sums_in = None if first else refs[user_count + 1]
    product_ref, sums_ref, total = refs[-3:]
    step = pl.program_id(0)

    @pl.when(step == 0)
    def _():
        total[...] = jnp.zeros_like(total) if first else sums_in[0]

    for slot in range(user_count):
        value = lax.dot_general(
            lefts[slot][...],
            right_ref[slot],
            (((0,), (0,)), ((), ())),
            preferred_element_type=jnp.float32,
        )
        product_ref[slot] = value
        row = jnp.sum(value * value, axis=0, keepdims=True)
        for at in range(0, row.shape[1], lanes):
            total[slot : slot + 1, :] += row[:, at : at + lanes]

    @pl.when(step == pl.num_programs(0) - 1)
    def _():
        sums_ref[...] = jnp.broadcast_to(total[...][None], sums_ref.shape)


def product(lefts, right, start, own_width, before, copies):
    user_count, tokens, columns = right.shape
    width = lefts[0].shape[1]
    tile = math.gcd(math.gcd(width, start), 2 * lanes) if tokens <= 1024 else lanes
    first = before is None
    vmem = pl.BlockSpec(memory_space=pltpu.VMEM)
    in_specs = [pl.BlockSpec((tokens, tile), lambda i: (0, i))] * user_count
    in_specs += [
        pl.BlockSpec((user_count, tokens, columns), lambda i: (0, 0, 0), pipeline_mode=pl.Buffered(1))
    ]
    operands = [*lefts, right]
    aliases = {}
    if not first:
        gradients, sums = before
        in_specs += [vmem, ANY]
        operands += [sums, gradients]
        aliases = {user_count + 2: 0}
    return pl.pallas_call(
        functools.partial(product_kernel, user_count, first),
        grid=(width // tile,),
        out_shape=[
            jax.ShapeDtypeStruct((user_count, own_width, columns), jnp.float32),
            jax.ShapeDtypeStruct((copies, 8, lanes), jnp.float32),
        ],
        in_specs=in_specs,
        out_specs=[
            pl.BlockSpec((user_count, tile, columns), lambda i: (0, start // tile + i, 0)),
            vmem,
        ],
        scratch_shapes=[pltpu.VMEM((8, lanes), jnp.float32)],
        input_output_aliases=aliases,
        compiler_params=pltpu.CompilerParams(vmem_limit_bytes=48 * 2**20),
        cost_estimate=pl.CostEstimate(
            flops=2 * user_count * tokens * columns * width,
            bytes_accessed=2 * user_count * tokens * (width + columns) + 4 * user_count * width * columns,
            transcendentals=0,
        ),
        name="product_and_squares",
    )(*operands)


def combine_kernel(user_count, clip_bound, scaling, user_ref, sums_ref, gradient_ref, out_ref):
    per_user = sums_ref.shape[0] // user_count
    by_source = [
        jnp.sum(sums_ref[j * per_user : (j + 1) * per_user], axis=0) for j in range(user_count)
    ]
    factors = []
    for u in range(user_count):
        row = sum(by_source[j][j ^ u : (j ^ u) + 1, :] for j in range(user_count))
        norm_sq = jnp.sum(row, axis=1, keepdims=True)
        factors.append(jnp.minimum(1.0, clip_bound / jnp.sqrt(norm_sq + epsilon)) * scaling)
    result = None
    for slot in range(user_count):
        user = user_ref[0] ^ slot
        factor = sum(jnp.where(user == u, factors[u], 0.0) for u in range(user_count))
        term = factor * gradient_ref[slot]
        result = term if result is None else result + term
    out_ref[...] = result


def combine(user, sums, gradients, clip_bound, scaling):
    user_count, rows, columns = gradients.shape
    tile = min(rows, 256)
    return pl.pallas_call(
        functools.partial(combine_kernel, user_count, clip_bound, scaling),
        grid=(rows // tile,),
        out_shape=jax.ShapeDtypeStruct((rows, columns), jnp.float32),
        in_specs=[
            pl.BlockSpec(memory_space=pltpu.SMEM),
            pl.BlockSpec(memory_space=pltpu.VMEM),
            pl.BlockSpec((user_count, tile, columns), lambda i: (0, i, 0)),
        ],
        out_specs=pl.BlockSpec((tile, columns), lambda i: (i, 0)),
        compiler_params=pltpu.CompilerParams(vmem_limit_bytes=32 * 2**20),
        name="weighted_sum",
    )(user, sums, gradients)


def body(hidden, cotangent, lengths):
    tok_count = lax.axis_size("tok")
    user_count = lax.axis_size("user")
    tok_rows = hidden.shape[1]
    hidden_width = hidden.shape[2]
    model_width = cotangent.shape[2]
    capacity = tok_rows * tok_count
    own_width = hidden_width // tok_count
    columns = model_width // user_count
    clip_bound = math.sqrt(8.0 * hidden_width * model_width * capacity)
    scaling = math.sqrt(hidden_width * model_width) / (user_count * clip_bound)
    user = lax.axis_index("user").astype(jnp.int32).reshape(1)
    tok = lax.axis_index("tok").astype(jnp.int32).reshape(1)
    valid = lengths - tok * tok_rows

    units = own_width // lanes
    starts = sorted({round(edge * units) * lanes for edge in edges})
    bounds = list(zip(starts[:-1], starts[1:]))

    masked = mask(valid, user, cotangent, user_count)
    by_slot = [masked[0]] + [exchange(masked[s], "user", s) for s in range(1, user_count)]
    right = order(tok, doubling(jnp.stack(by_slot), "tok"))
    right = right.reshape(user_count, capacity, columns)

    before = None
    across = []
    done = []
    for at, (start, stop) in enumerate(bounds):
        after = []
        if at >= 2:
            after.append(across[at - 2])
        if at >= 3:
            after.append(done[at - 3])
        outgoing = pack(hidden, tok_count, start, stop - start, after)
        arrived = lax.all_to_all(outgoing, "tok", split_axis=0, concat_axis=0, tiled=True)
        arrived = arrived.reshape(capacity, stop - start)
        lefts = doubling(arrived, "user")
        across.append(lefts[user_count // 2])
        last = at == len(bounds) - 1
        before = product(
            lefts, right, start, own_width, before, tok_count * user_count if last else 1
        )
        done.append(before[1])
    gradients, sums = before
    sums = lax.all_to_all(sums, ("user", "tok"), split_axis=0, concat_axis=0, tiled=True)
    return combine(user, sums, gradients, clip_bound, scaling)


def solution(mesh):
    return jax.shard_map(
        body,
        mesh=mesh,
        in_specs=(P("user", "tok", None), P("user", "tok", None), P("user")),
        out_specs=P("tok", "user"),
        check_vma=False,
    )
```

```python
import functools
import math

import jax
import jax.numpy as jnp
from jax import lax
from jax.experimental import pallas as pl
from jax.experimental.pallas import tpu as pltpu
from jax.sharding import PartitionSpec as P

epsilon = 1e-06
lanes = 128
ANY = pl.BlockSpec(memory_space=pl.ANY)
SMEM = pl.BlockSpec(memory_space=pltpu.SMEM)
VMEM = pl.BlockSpec(memory_space=pltpu.VMEM)
HBM = pl.BlockSpec(memory_space=pltpu.HBM)


def exchange(block, axis, distance):
    size = lax.axis_size(axis)
    return lax.ppermute(block, axis, [(i, i ^ distance) for i in range(size)])


def doubling(block, axis):
    size = lax.axis_size(axis)
    slots = {0: block}
    distance = size // 2
    while distance:
        for slot in list(slots):
            slots[slot ^ distance] = exchange(slots[slot], axis, distance)
        distance //= 2
    return [slots[slot] for slot in range(size)]


def pack_kernel(distances, tok_ref, hidden_ref, *refs):
    out_refs, sems = refs[-1 - len(distances) : -1], refs[-1]
    width = out_refs[0].shape[1]
    copies = []
    for at, distance in enumerate(distances):
        start = pl.multiple_of((tok_ref[0] ^ distance) * width, lanes)
        copies.append(
            pltpu.make_async_copy(
                hidden_ref.at[0, :, pl.ds(start, width)], out_refs[at], sems.at[at]
            )
        )
    for copy in copies:
        copy.start()
    for copy in copies:
        copy.wait()


def pack(tok, hidden, distances, width, after):
    rows = hidden.shape[1]
    count = len(distances)
    return pl.pallas_call(
        functools.partial(pack_kernel, distances),
        out_shape=[jax.ShapeDtypeStruct((rows, width), hidden.dtype)] * count,
        in_specs=[SMEM, HBM] + [ANY] * len(after),
        out_specs=[VMEM] * count,
        scratch_shapes=[pltpu.SemaphoreType.DMA((count,))],
        compiler_params=pltpu.CompilerParams(vmem_limit_bytes=2**20),
        cost_estimate=pl.CostEstimate(
            flops=0, bytes_accessed=4 * count * rows * width, transcendentals=0
        ),
        name="pack_columns",
    )(tok, hidden, *after)


def mask_kernel(valid_ref, user_ref, cot_ref, *out_refs):
    rows, width = out_refs[0].shape
    keep = lax.broadcasted_iota(jnp.int32, (rows, width), 0) < valid_ref[0]
    for slot, out_ref in enumerate(out_refs):
        column = pl.multiple_of((user_ref[0] ^ slot) * width, lanes)
        block = cot_ref[0, :, pl.ds(column, width)]
        out_ref[...] = jnp.where(keep, block, jnp.zeros_like(block))


def mask(valid, user, cotangent, user_count):
    _, rows, total = cotangent.shape
    return pl.pallas_call(
        mask_kernel,
        out_shape=[jax.ShapeDtypeStruct((rows, total // user_count), cotangent.dtype)] * user_count,
        in_specs=[SMEM, SMEM, VMEM],
        out_specs=[VMEM] * user_count,
        compiler_params=pltpu.CompilerParams(vmem_limit_bytes=2 * 2**20),
        name="mask_cotangent",
    )(valid, user, cotangent)


def product_kernel(user_count, sources, first, last, *refs):
    lefts = [refs[i * user_count : (i + 1) * user_count] for i in range(sources)]
    rights = refs[sources * user_count : sources * (user_count + 1)]
    held_ref = None if first else refs[sources * (user_count + 1)]
    product_ref = refs[sources * (user_count + 1) + (0 if first else 1)]
    width = product_ref.shape[1]
    tile = min(width, 2 * lanes)
    squares = []
    for slot in range(user_count):
        right = jnp.concatenate([right_ref[slot] for right_ref in rights], axis=0)

        def step(i, total, slot=slot, right=right):
            at = pl.ds(pl.multiple_of(i * tile, tile), tile)
            left = jnp.concatenate([source[slot][:, at] for source in lefts], axis=0)
            value = lax.dot_general(
                left, right, (((0,), (0,)), ((), ())), preferred_element_type=jnp.float32
            )
            if not first:
                value += held_ref[slot, at, :]
            product_ref[slot, at, :] = value
            if last:
                row = jnp.sum(value * value, axis=0, keepdims=True)
                for start in range(0, row.shape[1], lanes):
                    total += row[:, start : start + lanes]
            return total

        squares.append(lax.fori_loop(0, width // tile, step, jnp.zeros((1, lanes), jnp.float32)))
    if last:
        sums_ref = refs[-1]
        rows = jnp.concatenate(squares + [jnp.zeros((8 - user_count, lanes), jnp.float32)], axis=0)
        sums_ref[...] = jnp.broadcast_to(rows[None], sums_ref.shape)


def product(lefts, rights, held, copies):
    sources = len(rights)
    user_count, tokens, columns = rights[0].shape
    width = lefts[0][0].shape[1]
    first, last = held is None, copies > 0
    operands = [left for source in lefts for left in source] + list(rights)
    aliases = {}
    if not first:
        aliases = {len(operands): 0}
        operands.append(held)
    out_shape = [jax.ShapeDtypeStruct((user_count, width, columns), jnp.float32)]
    if last:
        out_shape.append(jax.ShapeDtypeStruct((copies, 8, lanes), jnp.float32))
    return pl.pallas_call(
        functools.partial(product_kernel, user_count, sources, first, last),
        out_shape=out_shape,
        in_specs=[VMEM] * len(operands),
        out_specs=[VMEM] * len(out_shape),
        input_output_aliases=aliases,
        compiler_params=pltpu.CompilerParams(vmem_limit_bytes=8 * 2**20),
        cost_estimate=pl.CostEstimate(
            flops=2 * user_count * sources * tokens * columns * width,
            bytes_accessed=2 * user_count * sources * tokens * (width + columns),
            transcendentals=0,
        ),
        name="product_and_squares",
    )(*operands)


def combine_kernel(user_count, clip_bound, scaling, user_ref, sums_ref, gradient_ref, out_ref):
    per_user = sums_ref.shape[0] // user_count
    by_source = [
        jnp.sum(sums_ref[j * per_user : (j + 1) * per_user], axis=0) for j in range(user_count)
    ]
    factors = []
    for u in range(user_count):
        row = sum(by_source[j][j ^ u : (j ^ u) + 1, :] for j in range(user_count))
        norm_sq = jnp.sum(row, axis=1, keepdims=True)
        factors.append(jnp.minimum(1.0, clip_bound / jnp.sqrt(norm_sq + epsilon)) * scaling)
    tile = out_ref.shape[0]
    at = pl.ds(pl.multiple_of(pl.program_id(0) * tile, tile), tile)
    result = None
    for slot in range(user_count):
        user = user_ref[0] ^ slot
        factor = sum(jnp.where(user == u, factors[u], 0.0) for u in range(user_count))
        term = factor * gradient_ref[slot, at, :]
        result = term if result is None else result + term
    out_ref[...] = result


def combine(user, sums, gradients, clip_bound, scaling):
    user_count, rows, columns = gradients.shape
    tile = min(rows, 256)
    return pl.pallas_call(
        functools.partial(combine_kernel, user_count, clip_bound, scaling),
        grid=(rows // tile,),
        out_shape=jax.ShapeDtypeStruct((rows, columns), jnp.float32),
        in_specs=[SMEM, VMEM, VMEM],
        out_specs=pl.BlockSpec((tile, columns), lambda i: (i, 0)),
        compiler_params=pltpu.CompilerParams(vmem_limit_bytes=8 * 2**20),
        name="weighted_sum",
    )(user, sums, gradients)


def body(hidden, cotangent, lengths):
    tok_count = lax.axis_size("tok")
    user_count = lax.axis_size("user")
    tok_rows = hidden.shape[1]
    hidden_width = hidden.shape[2]
    model_width = cotangent.shape[2]
    capacity = tok_rows * tok_count
    own_width = hidden_width // tok_count
    clip_bound = math.sqrt(8.0 * hidden_width * model_width * capacity)
    scaling = math.sqrt(hidden_width * model_width) / (user_count * clip_bound)
    user = lax.axis_index("user").astype(jnp.int32).reshape(1)
    tok = lax.axis_index("tok").astype(jnp.int32).reshape(1)
    valid = lengths - tok * tok_rows
    half = tok_count // 2

    masked = mask(valid, user, cotangent, user_count)
    by_slot = [masked[0]] + [exchange(masked[s], "user", s) for s in range(1, user_count)]
    rights = doubling(jnp.stack(by_slot), "tok")

    early = list(range(half + 1))
    outgoing = dict(zip(early, pack(tok, hidden, early, own_width, [masked[0]])))
    arrived = {0: outgoing[0]}
    for d in range(1, tok_count):
        if d not in outgoing:
            after = rights[half] if d == half + 1 else arrived[d - 2]
            outgoing[d] = pack(tok, hidden, [d], own_width, [after])[0]
        arrived[d] = exchange(outgoing[d], "tok", d)

    held = None
    for d in range(0, tok_count, 2):
        last = d == tok_count - 2
        pair = [doubling(arrived[d], "user"), doubling(arrived[d + 1], "user")]
        outs = product(pair, rights[d : d + 2], held, tok_count * user_count if last else 0)
        held = outs[0]
    sums = lax.all_to_all(outs[1], ("user", "tok"), split_axis=0, concat_axis=0, tiled=True)
    return combine(user, sums, held, clip_bound, scaling)


def solution(mesh):
    return jax.shard_map(
        body,
        mesh=mesh,
        in_specs=(P("user", "tok", None), P("user", "tok", None), P("user")),
        out_specs=P("tok", "user"),
        check_vma=False,
    )
```

```python
import functools
import math

import jax
import jax.numpy as jnp
from jax import lax
from jax.experimental import pallas as pl
from jax.experimental.pallas import tpu as pltpu
from jax.sharding import PartitionSpec as P

epsilon = 1e-06
lanes = 128
edges = (0.0, 0.25, 0.5, 0.75, 1.0)
ANY = pl.BlockSpec(memory_space=pl.ANY)
SMEM = pl.BlockSpec(memory_space=pltpu.SMEM)
VMEM = pl.BlockSpec(memory_space=pltpu.VMEM)
HBM = pl.BlockSpec(memory_space=pltpu.HBM)


def exchange(block, axis, distance):
    size = lax.axis_size(axis)
    return lax.ppermute(block, axis, [(i, i ^ distance) for i in range(size)])


def pack_kernel(start, distances, tok_ref, hidden_ref, *refs):
    out_refs, sems = refs[-1 - len(distances) : -1], refs[-1]
    width = out_refs[0].shape[1]
    own_width = hidden_ref.shape[2] // (len(distances))
    copies = []
    for at, distance in enumerate(distances):
        column = pl.multiple_of((tok_ref[0] ^ distance) * own_width + start, lanes)
        copies.append(
            pltpu.make_async_copy(
                hidden_ref.at[0, :, pl.ds(column, width)], out_refs[at], sems.at[at]
            )
        )
    for copy in copies:
        copy.start()
    for copy in copies:
        copy.wait()


def pack(tok, hidden, count, start, width, after):
    rows = hidden.shape[1]
    return pl.pallas_call(
        functools.partial(pack_kernel, start, list(range(count))),
        out_shape=[jax.ShapeDtypeStruct((rows, width), hidden.dtype)] * count,
        in_specs=[SMEM, HBM] + [ANY] * len(after),
        out_specs=[VMEM] * count,
        scratch_shapes=[pltpu.SemaphoreType.DMA((count,))],
        compiler_params=pltpu.CompilerParams(vmem_limit_bytes=2**20),
        cost_estimate=pl.CostEstimate(
            flops=0, bytes_accessed=4 * count * rows * width, transcendentals=0
        ),
        name="pack_columns",
    )(tok, hidden, *after)


def join_kernel(places, *refs):
    out_ref = refs[-1]
    for ref, (row, column, width) in zip(refs, places):
        rows = ref.shape[0]
        out_ref[row : row + rows, column : column + width] = ref[:, -width:]


def join(parts, shape, after=()):
    arrays = [part[0] for part in parts]
    return pl.pallas_call(
        functools.partial(join_kernel, [part[1:] for part in parts]),
        out_shape=jax.ShapeDtypeStruct(shape, arrays[0].dtype),
        in_specs=[VMEM] * len(arrays) + [ANY] * len(after),
        out_specs=VMEM,
        compiler_params=pltpu.CompilerParams(vmem_limit_bytes=2**20),
        cost_estimate=pl.CostEstimate(
            flops=0, bytes_accessed=2 * shape[0] * shape[1], transcendentals=0
        ),
        name="join_blocks",
    )(*arrays, *after)


def stack(arrays, width, after=()):
    rows = arrays[0].shape[0]
    parts = [(array, i * rows, 0, width) for i, array in enumerate(arrays)]
    return join(parts, (rows * len(arrays), width), after)


def mask_kernel(valid_ref, user_ref, cot_ref, *out_refs):
    rows, width = out_refs[0].shape
    keep = lax.broadcasted_iota(jnp.int32, (rows, width), 0) < valid_ref[0]
    for slot, out_ref in enumerate(out_refs):
        column = pl.multiple_of((user_ref[0] ^ slot) * width, lanes)
        block = cot_ref[0, :, pl.ds(column, width)]
        out_ref[...] = jnp.where(keep, block, jnp.zeros_like(block))


def mask(valid, user, cotangent, user_count):
    _, rows, total = cotangent.shape
    return pl.pallas_call(
        mask_kernel,
        out_shape=[jax.ShapeDtypeStruct((rows, total // user_count), cotangent.dtype)] * user_count,
        in_specs=[SMEM, SMEM, VMEM],
        out_specs=[VMEM] * user_count,
        compiler_params=pltpu.CompilerParams(vmem_limit_bytes=2 * 2**20),
        name="mask_cotangent",
    )(valid, user, cotangent)


def product_kernel(user_count, copies, *refs):
    sums_ref, out_ref = refs[-1], refs[-2]
    before_ref, right_ref = refs[-3], refs[-4]
    parts = refs[:-4]
    width, columns = out_ref.shape[1:]
    tile = min(width, 2 * lanes)
    squares = []
    for slot in range(user_count):
        right = right_ref[:, slot * columns : (slot + 1) * columns]

        def step(i, total, slot=slot, right=right):
            rows = pl.ds(pl.multiple_of(i * tile, tile), tile)
            left = jnp.concatenate(
                [
                    ref[at * rows_each : (at + 1) * rows_each, rows]
                    for ref, at, rows_each in split(parts, user_count)[slot]
                ],
                axis=0,
            )
            value = lax.dot_general(
                left, right, (((0,), (0,)), ((), ())), preferred_element_type=jnp.float32
            )
            out_ref[slot, rows, :] = value
            row = jnp.sum(value * value, axis=0, keepdims=True)
            for start in range(0, row.shape[1], lanes):
                total += row[:, start : start + lanes]
            return total

        squares.append(lax.fori_loop(0, width // tile, step, jnp.zeros((1, lanes), jnp.float32)))
    rows = jnp.concatenate(squares + [jnp.zeros((8 - user_count, lanes), jnp.float32)], axis=0)
    rows += before_ref[0]
    sums_ref[...] = jnp.broadcast_to(rows[None], sums_ref.shape)


def split(parts, user_count):
    slots = [[] for _ in range(user_count)]
    levels = user_count.bit_length()
    for first in range(0, len(parts), levels):
        have = [0]
        each = parts[first].shape[0]
        for level, ref in enumerate(parts[first : first + levels]):
            distance = 0 if level == 0 else user_count >> level
            for at, slot in enumerate(have):
                slots[slot ^ distance].append((ref, at, each))
            if level:
                have = have + [slot ^ distance for slot in have]
    return slots


def product(parts, right, before, width, user_count, copies):
    tokens, total = right.shape
    columns = total // user_count
    operands = [*parts, right, before]
    return pl.pallas_call(
        functools.partial(product_kernel, user_count, copies),
        out_shape=[
            jax.ShapeDtypeStruct((user_count, width, columns), jnp.float32),
            jax.ShapeDtypeStruct((copies, 8, lanes), jnp.float32),
        ],
        in_specs=[VMEM] * len(operands),
        out_specs=[VMEM] * 2,
        compiler_params=pltpu.CompilerParams(vmem_limit_bytes=10 * 2**20),
        cost_estimate=pl.CostEstimate(
            flops=2 * user_count * tokens * columns * width,
            bytes_accessed=2 * user_count * tokens * (width + columns),
            transcendentals=0,
        ),
        name="product_and_squares",
    )(*operands)


def combine_kernel(user_count, clip_bound, scaling, starts, user_ref, sums_ref, *refs):
    out_ref = refs[-1]
    per_user = sums_ref.shape[0] // user_count
    by_source = [
        jnp.sum(sums_ref[j * per_user : (j + 1) * per_user], axis=0) for j in range(user_count)
    ]
    factors = []
    for u in range(user_count):
        row = sum(by_source[j][j ^ u : (j ^ u) + 1, :] for j in range(user_count))
        norm_sq = jnp.sum(row, axis=1, keepdims=True)
        factors.append(jnp.minimum(1.0, clip_bound / jnp.sqrt(norm_sq + epsilon)) * scaling)
    by_slot = []
    for slot in range(user_count):
        user = user_ref[0] ^ slot
        by_slot.append(sum(jnp.where(user == u, factors[u], 0.0) for u in range(user_count)))
    tile = out_ref.shape[0]
    row = pl.program_id(0) * tile
    for ref, start in zip(refs, starts):

        @pl.when((row >= start) & (row < start + ref.shape[1]))
        def _(ref=ref, start=start):
            at = pl.ds(pl.multiple_of(row - start, tile), tile)
            result = by_slot[0] * ref[0, at, :]
            for slot in range(1, user_count):
                result += by_slot[slot] * ref[slot, at, :]
            out_ref[...] = result


def combine(user, sums, gradients, clip_bound, scaling):
    user_count, _, columns = gradients[0].shape
    heights = [gradient.shape[1] for gradient in gradients]
    starts = [sum(heights[:i]) for i in range(len(heights))]
    rows = sum(heights)
    tile = math.gcd(256, *heights)
    return pl.pallas_call(
        functools.partial(combine_kernel, user_count, clip_bound, scaling, starts),
        grid=(rows // tile,),
        out_shape=jax.ShapeDtypeStruct((rows, columns), jnp.float32),
        in_specs=[SMEM] + [VMEM] * (1 + len(gradients)),
        out_specs=pl.BlockSpec((tile, columns), lambda i: (i, 0)),
        compiler_params=pltpu.CompilerParams(vmem_limit_bytes=8 * 2**20),
        name="weighted_sum",
    )(user, sums, *gradients)


def body(hidden, cotangent, lengths):
    tok_count = lax.axis_size("tok")
    user_count = lax.axis_size("user")
    tok_rows = hidden.shape[1]
    hidden_width = hidden.shape[2]
    model_width = cotangent.shape[2]
    capacity = tok_rows * tok_count
    own_width = hidden_width // tok_count
    columns = model_width // user_count
    clip_bound = math.sqrt(8.0 * hidden_width * model_width * capacity)
    scaling = math.sqrt(hidden_width * model_width) / (user_count * clip_bound)
    user = lax.axis_index("user").astype(jnp.int32).reshape(1)
    tok = lax.axis_index("tok").astype(jnp.int32).reshape(1)
    valid = lengths - tok * tok_rows
    half = tok_count // 2
    units = own_width // lanes
    bounds = sorted({round(edge * units) * lanes for edge in edges})

    masked = mask(valid, user, cotangent, user_count)
    by_slot = [masked[0]] + [exchange(masked[s], "user", s) for s in range(1, user_count)]
    cots = {
        0: join(
            [(block, 0, s * columns, columns) for s, block in enumerate(by_slot)],
            (tok_rows, model_width),
        )
    }

    def relay(d, after):
        bit = (d & -d) // 2
        while bit:
            message = join([(cots[d], 0, 0, model_width)], (tok_rows, model_width), after)
            cots[d + bit] = exchange(message, "tok", bit)
            bit //= 2

    right = None
    totals = [jnp.zeros((1, 8, lanes), jnp.float32)]
    gradients = []
    crossed = []
    arrived = []
    for q, (start, stop) in enumerate(zip(bounds[:-1], bounds[1:])):
        width = stop - start
        first, last = start == 0, stop == own_width
        after = [masked[0]] if first else [arrived[q - 1][half], arrived[q - 1][half + 1]]
        if q >= 2:
            after.append(crossed[q - 2])
        outgoing = pack(tok, hidden, tok_count, start, width, after)
        blocks = {0: outgoing[0]}
        for d in range(1, tok_count):
            message = outgoing[d]
            rides = first and d & (d - 1) == 0
            if rides:
                message = join(
                    [(cots[0], 0, 0, model_width), (message, 0, model_width, width)],
                    (tok_rows, model_width + width),
                )
            blocks[d] = exchange(message, "tok", d)
            if rides:
                cots[d] = blocks[d][:, :model_width]
        arrived.append(blocks)
        if first:
            for d in range(1, tok_count):
                relay(d, [])
            right = stack([cots[d] for d in range(tok_count)], model_width)
        parts = []
        for sources in (range(half), range(half, tok_count)):
            far = sources[0] > 0
            have = stack([blocks[d] for d in sources], width, totals[q - 1 : q] if far and q >= 2 else [])
            parts.append(have)
            distance = user_count // 2
            while distance:
                came = exchange(have, "user", distance)
                parts.append(came)
                if far and distance == user_count // 2:
                    crossed.append(came)
                distance //= 2
                if distance:
                    have = stack([have, came], width, totals[q : q + 1] if far and q >= 1 else [])
        gradient, sums = product(
            parts, right, totals[-1], width, user_count, tok_count * user_count if last else 1
        )
        gradients.append(gradient)
        totals.append(sums)
    sums = lax.all_to_all(sums, ("user", "tok"), split_axis=0, concat_axis=0, tiled=True)
    return combine(user, sums, gradients, clip_bound, scaling)


def solution(mesh):
    return jax.shard_map(
        body,
        mesh=mesh,
        in_specs=(P("user", "tok", None), P("user", "tok", None), P("user")),
        out_specs=P("tok", "user"),
        check_vma=False,
    )
```

```python
import functools
import math

import jax
import jax.numpy as jnp
from jax import lax
from jax.experimental import pallas as pl
from jax.experimental.pallas import tpu as pltpu
from jax.sharding import PartitionSpec as P

epsilon = 1e-06
lanes = 128
first_part = 0.5
ANY = pl.BlockSpec(memory_space=pl.ANY)
SMEM = pl.BlockSpec(memory_space=pltpu.SMEM)
VMEM = pl.BlockSpec(memory_space=pltpu.VMEM)
HBM = pl.BlockSpec(memory_space=pltpu.HBM)


def exchange(block, axis, distance):
    size = lax.axis_size(axis)
    return lax.ppermute(block, axis, [(i, i ^ distance) for i in range(size)])


def pack_kernel(distances, tok_ref, hidden_ref, *refs):
    out_refs, sems = refs[-1 - len(distances) : -1], refs[-1]
    width = out_refs[0].shape[1]
    copies = []
    for at, distance in enumerate(distances):
        start = pl.multiple_of((tok_ref[0] ^ distance) * width, lanes)
        copies.append(
            pltpu.make_async_copy(
                hidden_ref.at[0, :, pl.ds(start, width)], out_refs[at], sems.at[at]
            )
        )
    for copy in copies:
        copy.start()
    for copy in copies:
        copy.wait()


def pack(tok, hidden, distances, width, after):
    rows = hidden.shape[1]
    count = len(distances)
    return pl.pallas_call(
        functools.partial(pack_kernel, distances),
        out_shape=[jax.ShapeDtypeStruct((rows, width), hidden.dtype)] * count,
        in_specs=[SMEM, HBM] + [ANY] * len(after),
        out_specs=[VMEM] * count,
        scratch_shapes=[pltpu.SemaphoreType.DMA((count,))],
        compiler_params=pltpu.CompilerParams(vmem_limit_bytes=2**20),
        cost_estimate=pl.CostEstimate(
            flops=0, bytes_accessed=4 * count * rows * width, transcendentals=0
        ),
        name="pack_columns",
    )(tok, hidden, *after)


def join_kernel(parts, *refs):
    out_ref = refs[-1]
    to = 0
    for ref, (start, width) in zip(refs, parts):
        out_ref[:, to : to + width] = ref[:, start : start + width]
        to += width


def join(parts, after):
    arrays = [array for array, _, _ in parts]
    rows = arrays[0].shape[0]
    total = sum(width for _, _, width in parts)
    return pl.pallas_call(
        functools.partial(join_kernel, [part[1:] for part in parts]),
        out_shape=jax.ShapeDtypeStruct((rows, total), arrays[0].dtype),
        in_specs=[VMEM] * len(arrays) + [ANY] * len(after),
        out_specs=VMEM,
        compiler_params=pltpu.CompilerParams(vmem_limit_bytes=2**20),
        cost_estimate=pl.CostEstimate(flops=0, bytes_accessed=4 * rows * total, transcendentals=0),
        name="join_columns",
    )(*arrays, *after)


def mask_kernel(valid_ref, user_ref, cot_ref, *out_refs):
    rows, width = out_refs[0].shape
    keep = lax.broadcasted_iota(jnp.int32, (rows, width), 0) < valid_ref[0]
    for slot, out_ref in enumerate(out_refs):
        column = pl.multiple_of((user_ref[0] ^ slot) * width, lanes)
        block = cot_ref[0, :, pl.ds(column, width)]
        out_ref[...] = jnp.where(keep, block, jnp.zeros_like(block))


def mask(valid, user, cotangent, user_count):
    _, rows, total = cotangent.shape
    return pl.pallas_call(
        mask_kernel,
        out_shape=[jax.ShapeDtypeStruct((rows, total // user_count), cotangent.dtype)] * user_count,
        in_specs=[SMEM, SMEM, VMEM],
        out_specs=[VMEM] * user_count,
        compiler_params=pltpu.CompilerParams(vmem_limit_bytes=2 * 2**20),
        name="mask_cotangent",
    )(valid, user, cotangent)


def product_kernel(lefts, rights, tile, has_held, has_sums, copies, *refs):
    outs = refs[-2:] if copies else refs[-1:]
    inputs = list(refs[: -len(outs)])
    sums_in = inputs.pop() if has_sums else None
    held_ref = inputs.pop() if has_held else None
    product_ref = outs[0]
    user_count, width, columns = product_ref.shape
    squares = []
    for slot in range(user_count):
        right = jnp.concatenate(
            [refs[at][:, start : start + columns] for at, start in rights[slot]], axis=0
        )

        def step(i, total, slot=slot, right=right):
            rows = pl.ds(pl.multiple_of(i * tile, tile), tile)
            left = jnp.concatenate(
                [
                    refs[at][:, pl.ds(pl.multiple_of(start + i * tile, lanes), tile)]
                    for at, start in lefts[slot]
                ],
                axis=0,
            )
            value = lax.dot_general(
                left, right, (((0,), (0,)), ((), ())), preferred_element_type=jnp.float32
            )
            if has_held:
                value += held_ref[slot, rows, :]
            product_ref[slot, rows, :] = value
            if copies:
                row = jnp.sum(value * value, axis=0, keepdims=True)
                for start in range(0, columns, lanes):
                    total += row[:, start : start + lanes]
            return total

        squares.append(lax.fori_loop(0, width // tile, step, jnp.zeros((1, lanes), jnp.float32)))
    if copies:
        rows = jnp.concatenate(squares + [jnp.zeros((8 - user_count, lanes), jnp.float32)], axis=0)
        if has_sums:
            rows += sums_in[0]
        outs[1][...] = jnp.broadcast_to(rows[None], outs[1].shape)


def product(lefts, rights, width, columns, held=None, sums=None, copies=0):
    operands, at = [], {}

    def place(part):
        array, start = part
        if id(array) not in at:
            at[id(array)] = len(operands)
            operands.append(array)
        return at[id(array)], start

    user_count, sources = len(lefts), len(lefts[0])
    left_places = [[place(part) for part in slot] for slot in lefts]
    right_places = [[place(part) for part in slot] for slot in rights]
    tokens = sources * lefts[0][0][0].shape[0]
    aliases = {}
    if held is not None:
        aliases = {len(operands): 0}
        operands.append(held)
    if sums is not None:
        operands.append(sums)
    out_shape = [jax.ShapeDtypeStruct((user_count, width, columns), jnp.float32)]
    if copies:
        out_shape.append(jax.ShapeDtypeStruct((copies, 8, lanes), jnp.float32))
    tile = math.gcd(width, 2 * lanes)
    return pl.pallas_call(
        functools.partial(
            product_kernel, left_places, right_places, tile, held is not None, sums is not None, copies
        ),
        out_shape=out_shape,
        in_specs=[VMEM] * len(operands),
        out_specs=[VMEM] * len(out_shape),
        input_output_aliases=aliases,
        compiler_params=pltpu.CompilerParams(vmem_limit_bytes=8 * 2**20),
        cost_estimate=pl.CostEstimate(
            flops=2 * user_count * tokens * columns * width,
            bytes_accessed=2 * user_count * tokens * (width + columns),
            transcendentals=0,
        ),
        name="product_and_squares",
    )(*operands)


def combine_kernel(user_count, clip_bound, scaling, starts, user_ref, sums_ref, *refs):
    out_ref, factor_ref = refs[-2:]

    @pl.when(pl.program_id(0) == 0)
    def _():
        per_user = sums_ref.shape[0] // user_count
        by_source = [
            jnp.sum(sums_ref[j * per_user : (j + 1) * per_user], axis=0) for j in range(user_count)
        ]
        factors = []
        for u in range(user_count):
            row = sum(by_source[j][j ^ u : (j ^ u) + 1, :] for j in range(user_count))
            norm_sq = jnp.sum(row, axis=1, keepdims=True)
            factors.append(jnp.minimum(1.0, clip_bound / jnp.sqrt(norm_sq + epsilon)) * scaling)
        for slot in range(user_count):
            user = user_ref[0] ^ slot
            factor = sum(jnp.where(user == u, factors[u], 0.0) for u in range(user_count))
            factor_ref[slot : slot + 1, :] = jnp.broadcast_to(factor, (1, lanes))

    by_slot = [factor_ref[slot : slot + 1, 0:1] for slot in range(user_count)]
    tile = out_ref.shape[0]
    row = pl.program_id(0) * tile
    for ref, start in zip(refs, starts):

        @pl.when((row >= start) & (row < start + ref.shape[1]))
        def _(ref=ref, start=start):
            at = pl.ds(pl.multiple_of(row - start, tile), tile)
            result = by_slot[0] * ref[0, at, :]
            for slot in range(1, user_count):
                result += by_slot[slot] * ref[slot, at, :]
            out_ref[...] = result


def combine(user, sums, gradients, clip_bound, scaling):
    user_count, _, columns = gradients[0].shape
    heights = [gradient.shape[1] for gradient in gradients]
    starts = [sum(heights[:i]) for i in range(len(heights))]
    rows = sum(heights)
    tile = math.gcd(256, *heights)
    return pl.pallas_call(
        functools.partial(combine_kernel, user_count, clip_bound, scaling, starts),
        grid=(rows // tile,),
        out_shape=jax.ShapeDtypeStruct((rows, columns), jnp.float32),
        in_specs=[SMEM] + [VMEM] * (1 + len(gradients)),
        out_specs=pl.BlockSpec((tile, columns), lambda i: (i, 0)),
        scratch_shapes=[pltpu.VMEM((8, lanes), jnp.float32)],
        compiler_params=pltpu.CompilerParams(vmem_limit_bytes=8 * 2**20),
        name="weighted_sum",
    )(user, sums, *gradients)


def body(hidden, cotangent, lengths):
    tok_count = lax.axis_size("tok")
    user_count = lax.axis_size("user")
    tok_rows = hidden.shape[1]
    hidden_width = hidden.shape[2]
    model_width = cotangent.shape[2]
    capacity = tok_rows * tok_count
    own_width = hidden_width // tok_count
    columns = model_width // user_count
    clip_bound = math.sqrt(8.0 * hidden_width * model_width * capacity)
    scaling = math.sqrt(hidden_width * model_width) / (user_count * clip_bound)
    user = lax.axis_index("user").astype(jnp.int32).reshape(1)
    tok = lax.axis_index("tok").astype(jnp.int32).reshape(1)
    valid = lengths - tok * tok_rows
    half = tok_count // 2
    across, core = user_count // 2, user_count // 4
    slots = range(user_count)
    cut = round(own_width // lanes * first_part) * lanes
    pieces = [(0, cut), (cut, own_width - cut)]

    cots = {}
    lefts = {}
    ready = []
    tick = []

    def send(axis, distance, parts, after=()):
        message = join(parts, [*tick, *after])
        tick[:] = [message]
        return message, exchange(message, axis, distance)

    def cot_parts(d):
        return [(*cots[d][s], columns) for s in slots]

    def cots_at(array, start):
        return [(array, start + s * columns) for s in slots]

    masked = mask(valid, user, cotangent, user_count)
    by_slot = [masked[0]] + [exchange(masked[s], "user", s) for s in range(1, user_count)]
    outgoing = pack(tok, hidden, list(range(tok_count)), own_width, [masked[0]])
    ready += [(0, i, outgoing[0], start) for i, (start, _) in enumerate(pieces)]

    far_steps = []
    for i, (start, width) in enumerate(pieces):
        for d in range(half, tok_count, 2):
            far_steps.append([("block", e, i) for e in (d, d + 1)])
    far_steps.insert(1, [("cots", half, 0), ("cots", half, 1)])
    near = list(range(1, half))
    near_steps = [near[:2]] + [near[i : i + 2] if tok_count > 8 else near[i : i + 1] for i in range(2, len(near), 2)]
    relay_bits = [half >> i for i in range(1, half.bit_length())]

    lanes_before = [None, None]
    near_before, relay_before, cross_before, core_before = [], [], None, None
    gradients = []
    done = set()

    def finish_core():
        nonlocal core_before
        if core_before is None:
            return
        blocks, own, other, both = core_before
        core_before = None
        total = sum(pieces[i][1] for _, i, _, _ in blocks)
        to = 0
        for d, i, _, _ in blocks:
            lefts[d, i] = {0: (own, to), across: (other, to), core: (both, to), across ^ core: (both, total + to)}
            to += pieces[i][1]

    def add_products(step):
        if len(cots) < tok_count:
            return
        for i, (_, width) in enumerate(pieces):
            here = [d for d in range(tok_count) if (d, i) in lefts and (d, i) not in done]
            all_here = all((d, i) in lefts for d in range(tok_count))
            if not here or not (all_here or (i == 1 and step >= len(far_steps))):
                continue
            before = gradients[i] if len(gradients) > i else None
            final = all_here and i == 1
            out = product(
                [[lefts[d, i][s] for d in here] for s in slots],
                [[cots[d][s] for d in here] for s in slots],
                width,
                columns,
                held=before[0] if before else None,
                sums=gradients[0][1] if final else None,
                copies=0 if not all_here else tok_count * user_count if final else 1,
            )
            done.update((d, i) for d in here)
            gradients[i : i + 1] = [out]
            tick[:] = [out[0]]

    for step in range(len(far_steps) + 2):
        arrivals = []
        for lane in (0, 1):
            after = []
            if lanes_before[lane] is not None:
                after.append(lanes_before[lane][1])
                arrivals.append(lanes_before[lane])
                lanes_before[lane] = None
            if step < len(far_steps):
                kind, d, i = far_steps[step][lane]
                if kind == "block":
                    parts = [(outgoing[d], *pieces[i])]
                else:
                    parts = cot_parts(0)[lane * user_count // 2 : (lane + 1) * user_count // 2]
                message = send("tok", d, parts, after)
                lanes_before[lane] = (far_steps[step][lane], message[1])
        for (kind, d, i), array in arrivals:
            if kind == "block":
                ready.append((d, i, array, 0))
            else:
                cots.setdefault(d, [])
                cots[d] = cots[d] + [(array, s * columns) for s in range(user_count // 2)]
        for d, array in near_before:
            ready += [(d, i, array, start) for i, (start, _) in enumerate(pieces)]
            if d & (d - 1) == 0:
                cots[d] = cots_at(array, own_width)
        for bit, sources, array in relay_before:
            for at, d in enumerate(sources):
                cots[d + bit] = cots_at(array, at * model_width)
        near_before, relay_before = [], []
        crossed = cross_before
        cross_before = None
        if ready:
            blocks, ready = ready, []
            parts = [(array, start, pieces[i][1]) for _, i, array, start in blocks]
            own, other = send("user", across, parts, [crossed[2]] if crossed else [])
            cross_before = (blocks, own, other)
        if step == 0:
            cots[0] = [(block, 0) for block in by_slot]
            cots[0] = cots_at(join(cot_parts(0), []), 0)
        if step < len(near_steps):
            for d in near_steps[step]:
                parts = [(outgoing[d], 0, own_width)]
                if d & (d - 1) == 0:
                    parts += cot_parts(0)
                near_before.append((d, send("tok", d, parts)[1]))
        if relay_bits:
            bit = relay_bits[0]
            sources = list(range(2 * bit, tok_count, 2 * bit))
            if all(d in cots and len(cots[d]) == user_count for d in sources):
                relay_bits.pop(0)
                parts = [part for d in sources for part in cot_parts(d)]
                relay_before.append((bit, sources, send("tok", bit, parts)[1]))
        finish_core()
        if crossed:
            blocks, own, other = crossed
            total = sum(pieces[i][1] for _, i, _, _ in blocks)
            both = send("user", core, [(own, 0, total), (other, 0, total)])[1]
            core_before = (blocks, own, other, both)
        if step >= len(far_steps) - 1:
            finish_core()
            if relay_before:
                for bit, sources, array in relay_before:
                    for at, d in enumerate(sources):
                        cots[d + bit] = cots_at(array, at * model_width)
                relay_before = []
            add_products(step)
    sums = lax.all_to_all(gradients[1][1], ("user", "tok"), split_axis=0, concat_axis=0, tiled=True)
    return combine(user, sums, [g[0] for g in gradients], clip_bound, scaling)


def solution(mesh):
    return jax.shard_map(
        body,
        mesh=mesh,
        in_specs=(P("user", "tok", None), P("user", "tok", None), P("user")),
        out_specs=P("tok", "user"),
        check_vma=False,
    )
```

```python
import functools
import math

import jax
import jax.numpy as jnp
from jax import lax
from jax.experimental import pallas as pl
from jax.experimental.pallas import tpu as pltpu
from jax.sharding import PartitionSpec as P

epsilon = 1e-06
lanes = 128
first_part = 0.625
most_flying = 5
start_time = 1.5
latency = 1.0
link_rate = 5e4
product_time = 16.0
ANY = pl.BlockSpec(memory_space=pl.ANY)
SMEM = pl.BlockSpec(memory_space=pltpu.SMEM)
VMEM = pl.BlockSpec(memory_space=pltpu.VMEM)
HBM = pl.BlockSpec(memory_space=pltpu.HBM)


def exchange(block, axis, distance):
    size = lax.axis_size(axis)
    return lax.ppermute(block, axis, [(i, i ^ distance) for i in range(size)])


def pack_kernel(distances, tok_ref, hidden_ref, *refs):
    out_refs, sems = refs[-1 - len(distances) : -1], refs[-1]
    width = out_refs[0].shape[1]
    copies = []
    for at, distance in enumerate(distances):
        start = pl.multiple_of((tok_ref[0] ^ distance) * width, lanes)
        copies.append(
            pltpu.make_async_copy(
                hidden_ref.at[0, :, pl.ds(start, width)], out_refs[at], sems.at[at]
            )
        )
    for copy in copies:
        copy.start()
    for copy in copies:
        copy.wait()


def pack(tok, hidden, distances, width, after):
    rows = hidden.shape[1]
    count = len(distances)
    return pl.pallas_call(
        functools.partial(pack_kernel, distances),
        out_shape=[jax.ShapeDtypeStruct((rows, width), hidden.dtype)] * count,
        in_specs=[SMEM, HBM] + [ANY] * len(after),
        out_specs=[VMEM] * count,
        scratch_shapes=[pltpu.SemaphoreType.DMA((count,))],
        compiler_params=pltpu.CompilerParams(vmem_limit_bytes=2**20),
        cost_estimate=pl.CostEstimate(
            flops=0, bytes_accessed=4 * count * rows * width, transcendentals=0
        ),
        name="pack_columns",
    )(tok, hidden, *after)


def join_kernel(parts, *refs):
    out_ref = refs[-1]
    to = 0
    for at, start, width in parts:
        out_ref[:, to : to + width] = refs[at][:, start : start + width]
        to += width


def join(parts, after):
    arrays, places = [], []
    for array, start, width in parts:
        at = [i for i, other in enumerate(arrays) if other is array]
        if not at:
            arrays.append(array)
        places.append((at[0] if at else len(arrays) - 1, start, width))
    after = [array for array in after if not any(array is other for other in arrays)]
    rows = arrays[0].shape[0]
    total = sum(width for _, _, width in parts)
    return pl.pallas_call(
        functools.partial(join_kernel, places),
        out_shape=jax.ShapeDtypeStruct((rows, total), arrays[0].dtype),
        in_specs=[VMEM] * len(arrays) + [ANY] * len(after),
        out_specs=VMEM,
        compiler_params=pltpu.CompilerParams(vmem_limit_bytes=6 * 2**20),
        cost_estimate=pl.CostEstimate(flops=3 * 10**10, bytes_accessed=0, transcendentals=0),
        name="join_columns",
    )(*arrays, *after)


def mask_kernel(valid_ref, user_ref, cot_ref, *out_refs):
    rows, width = out_refs[0].shape
    keep = lax.broadcasted_iota(jnp.int32, (rows, width), 0) < valid_ref[0]
    for slot, out_ref in enumerate(out_refs):
        column = pl.multiple_of((user_ref[0] ^ slot) * width, lanes)
        block = cot_ref[0, :, pl.ds(column, width)]
        out_ref[...] = jnp.where(keep, block, jnp.zeros_like(block))


def mask(valid, user, cotangent, user_count):
    _, rows, total = cotangent.shape
    return pl.pallas_call(
        mask_kernel,
        out_shape=[jax.ShapeDtypeStruct((rows, total // user_count), cotangent.dtype)] * user_count,
        in_specs=[SMEM, SMEM, VMEM],
        out_specs=[VMEM] * user_count,
        compiler_params=pltpu.CompilerParams(vmem_limit_bytes=2 * 2**20),
        name="mask_cotangent",
    )(valid, user, cotangent)


def product_kernel(lefts, rights, tile, has_held, has_sums, copies, *refs):
    outs = refs[-2:] if copies else refs[-1:]
    inputs = list(refs[: -len(outs)])
    sums_in = inputs.pop() if has_sums else None
    held_ref = inputs.pop() if has_held else None
    product_ref = outs[0]
    user_count, width, columns = product_ref.shape
    squares = []
    for slot in range(user_count):
        right = jnp.concatenate(
            [refs[at][:, start : start + columns] for at, start in rights[slot]], axis=0
        )

        def step(i, total, slot=slot, right=right):
            rows = pl.ds(pl.multiple_of(i * tile, tile), tile)
            left = jnp.concatenate(
                [
                    refs[at][:, pl.ds(pl.multiple_of(start + i * tile, lanes), tile)]
                    for at, start in lefts[slot]
                ],
                axis=0,
            )
            value = lax.dot_general(
                left, right, (((0,), (0,)), ((), ())), preferred_element_type=jnp.float32
            )
            if has_held:
                value += held_ref[slot, rows, :]
            product_ref[slot, rows, :] = value
            if copies:
                row = jnp.sum(value * value, axis=0, keepdims=True)
                for start in range(0, columns, lanes):
                    total += row[:, start : start + lanes]
            return total

        squares.append(lax.fori_loop(0, width // tile, step, jnp.zeros((1, lanes), jnp.float32)))
    if copies:
        rows = jnp.concatenate(squares + [jnp.zeros((8 - user_count, lanes), jnp.float32)], axis=0)
        if has_sums:
            rows += sums_in[0]
        outs[1][...] = jnp.broadcast_to(rows[None], outs[1].shape)


def product(lefts, rights, width, columns, held=None, sums=None, copies=0):
    operands, at = [], {}

    def place(part):
        array, start = part
        if id(array) not in at:
            at[id(array)] = len(operands)
            operands.append(array)
        return at[id(array)], start

    user_count, sources = len(lefts), len(lefts[0])
    left_places = [[place(part) for part in slot] for slot in lefts]
    right_places = [[place(part) for part in slot] for slot in rights]
    tokens = sources * lefts[0][0][0].shape[0]
    aliases = {}
    if held is not None:
        aliases = {len(operands): 0}
        operands.append(held)
    if sums is not None:
        operands.append(sums)
    out_shape = [jax.ShapeDtypeStruct((user_count, width, columns), jnp.float32)]
    if copies:
        out_shape.append(jax.ShapeDtypeStruct((copies, 8, lanes), jnp.float32))
    tile = math.gcd(width, 2 * lanes)
    return pl.pallas_call(
        functools.partial(
            product_kernel, left_places, right_places, tile, held is not None, sums is not None, copies
        ),
        out_shape=out_shape,
        in_specs=[VMEM] * len(operands),
        out_specs=[VMEM] * len(out_shape),
        input_output_aliases=aliases,
        compiler_params=pltpu.CompilerParams(vmem_limit_bytes=8 * 2**20),
        cost_estimate=pl.CostEstimate(
            flops=2 * user_count * tokens * columns * width,
            bytes_accessed=2 * user_count * tokens * (width + columns),
            transcendentals=0,
        ),
        name="product_and_squares",
    )(*operands)


def combine_kernel(user_count, clip_bound, scaling, starts, user_ref, sums_ref, *refs):
    out_ref, factor_ref = refs[-2:]

    @pl.when(pl.program_id(0) == 0)
    def _():
        per_user = sums_ref.shape[0] // user_count
        by_source = [
            jnp.sum(sums_ref[j * per_user : (j + 1) * per_user], axis=0) for j in range(user_count)
        ]
        factors = []
        for u in range(user_count):
            row = sum(by_source[j][j ^ u : (j ^ u) + 1, :] for j in range(user_count))
            norm_sq = jnp.sum(row, axis=1, keepdims=True)
            factors.append(jnp.minimum(1.0, clip_bound / jnp.sqrt(norm_sq + epsilon)) * scaling)
        for slot in range(user_count):
            user = user_ref[0] ^ slot
            factor = sum(jnp.where(user == u, factors[u], 0.0) for u in range(user_count))
            factor_ref[slot : slot + 1, :] = jnp.broadcast_to(factor, (1, lanes))

    by_slot = [factor_ref[slot : slot + 1, 0:1] for slot in range(user_count)]
    tile = out_ref.shape[0]
    row = pl.program_id(0) * tile
    for ref, start in zip(refs, starts):

        @pl.when((row >= start) & (row < start + ref.shape[1]))
        def _(ref=ref, start=start):
            at = pl.ds(pl.multiple_of(row - start, tile), tile)
            result = by_slot[0] * ref[0, at, :]
            for slot in range(1, user_count):
                result += by_slot[slot] * ref[slot, at, :]
            out_ref[...] = result


def combine(user, sums, gradients, clip_bound, scaling):
    user_count, _, columns = gradients[0].shape
    heights = [gradient.shape[1] for gradient in gradients]
    starts = [sum(heights[:i]) for i in range(len(heights))]
    rows = sum(heights)
    tile = math.gcd(256, *heights)
    return pl.pallas_call(
        functools.partial(combine_kernel, user_count, clip_bound, scaling, starts),
        grid=(rows // tile,),
        out_shape=jax.ShapeDtypeStruct((rows, columns), jnp.float32),
        in_specs=[SMEM] + [VMEM] * (1 + len(gradients)),
        out_specs=pl.BlockSpec((tile, columns), lambda i: (i, 0)),
        scratch_shapes=[pltpu.VMEM((8, lanes), jnp.float32)],
        compiler_params=pltpu.CompilerParams(vmem_limit_bytes=8 * 2**20),
        name="weighted_sum",
    )(user, sums, *gradients)


def body(hidden, cotangent, lengths):
    tok_count = lax.axis_size("tok")
    user_count = lax.axis_size("user")
    tok_rows = hidden.shape[1]
    hidden_width = hidden.shape[2]
    model_width = cotangent.shape[2]
    capacity = tok_rows * tok_count
    own_width = hidden_width // tok_count
    columns = model_width // user_count
    clip_bound = math.sqrt(8.0 * hidden_width * model_width * capacity)
    scaling = math.sqrt(hidden_width * model_width) / (user_count * clip_bound)
    user = lax.axis_index("user").astype(jnp.int32).reshape(1)
    tok = lax.axis_index("tok").astype(jnp.int32).reshape(1)
    valid = lengths - tok * tok_rows
    half = tok_count // 2
    across, core = user_count // 2, user_count // 4
    slots = range(user_count)
    cut = round(own_width // lanes * first_part) * lanes
    pieces = [(0, cut), (cut, own_width - cut)]

    cots = {}
    lefts = {}
    ready = []
    crossed = []
    tick = []
    flying = []
    clock, number = [0.0], [0]

    def start(axis, distance, parts, rate, channels, action):
        message = join(parts, tick)
        tick[:] = [message]
        size = 2 * tok_rows * sum(part[2] for part in parts)
        clock[0] += start_time
        number[0] += 1
        end = clock[0] + latency + size / rate
        flying.append((end, number[0], channels, exchange(message, axis, distance), action))
        return message

    def free(*channels):
        busy = {channel for entry in flying for channel in entry[2]}
        return len(flying) < most_flying and not busy & set(channels)

    def cot_parts(d):
        return [(*cots[d][s], columns) for s in slots]

    def cots_at(array, first):
        return [(array, first + s * columns) for s in slots]

    masked = mask(valid, user, cotangent, user_count)
    by_slot = [masked[0]] + [exchange(masked[s], "user", s) for s in range(1, user_count)]
    outgoing = pack(tok, hidden, list(range(tok_count)), own_width, [masked[0]])
    ready += [(0, i, outgoing[0], first) for i, (first, _) in enumerate(pieces)]

    far = {
        "A": [(None, None)] + [(d, None) for d in range(half + 2, tok_count - 1, 2)] + [(half, 1)],
        "B": [(half, 0)]
        + [(d, None) for d in range(half + 1, tok_count - 2, 2)]
        + [(tok_count - 1, 0), (tok_count - 1, 1)],
    }
    near = list(range(1, half))
    relayed = {half}

    def start_far(lane):
        d, i = far[lane].pop(0)
        if d is None:
            parts = cot_parts(0)

            def action(array):
                cots[half] = cots_at(array, 0)

        else:
            first, width = pieces[i] if i is not None else (0, own_width)
            parts = [(outgoing[d], first, width)]

            def action(array):
                for j, (at, _) in enumerate(pieces):
                    if i is None or i == j:
                        ready.append((d, j, array, at - first))

        start("tok", half if d is None else d, parts, link_rate / 4, {lane}, action)

    def start_near():
        for d in near:
            bits = {bit for bit in range(half.bit_length()) if d >> bit & 1}
            if free(*bits):
                near.remove(d)

                def action(array, d=d):
                    ready.extend((d, j, array, at) for j, (at, _) in enumerate(pieces))

                start("tok", d, [(outgoing[d], 0, own_width)], link_rate, bits, action)
                return True
        for bit in range(half.bit_length() - 1):
            step = 1 << bit
            if step in near or not free(bit):
                continue
            sources = [d for d in cots if d % (2 * step) == 0 and d + step not in relayed]
            if sources:
                relayed.update(d + step for d in sources)
                parts = [part for d in sources for part in cot_parts(d)]

                def action(array, sources=sources, step=step):
                    for at, d in enumerate(sources):
                        cots[d + step] = cots_at(array, at * model_width)

                start("tok", step, parts, link_rate, {bit}, action)
                return True
        return False

    def start_across():
        blocks, total = [], 0
        while ready and total < 2 * own_width:
            blocks.append(ready.pop(0))
            total += pieces[blocks[-1][1]][1]
        parts = [(array, first, pieces[i][1]) for _, i, array, first in blocks]
        own = start(
            "user", across, parts, link_rate, {"X"}, lambda other: crossed.append((blocks, own, other))
        )

    def start_core():
        blocks, own, other = crossed.pop(0)
        total = sum(pieces[i][1] for _, i, _, _ in blocks)

        def action(both):
            to = 0
            for d, i, _, _ in blocks:
                lefts[d, i] = {
                    0: (own, to),
                    across: (other, to),
                    core: (both, to),
                    across ^ core: (both, total + to),
                }
                to += pieces[i][1]

        parts = [(own, 0, total), (other, 0, total)]
        start("user", core, parts, 6 * link_rate, {"C"}, action)

    gradients = [None, None]
    added = set()

    def add_products():
        ends = [entry[0] for entry in flying if entry[2] & {"A", "B"}]
        for i, (_, width) in enumerate(pieces):
            here = [d for d in cots if (d, i) in lefts and (d, i) not in added]
            final = len(here) + len([1 for d, j in added if j == i]) == tok_count
            early = gradients[i] is None and len(here) >= tok_count - 2 - i
            if not here or not (final or early) or (final and i == 1 and gradients[0] is None):
                continue
            time = product_time * width / own_width * (len(here) / tok_count + 0.5)
            if not final and ends and min(ends) - clock[0] < time / 2:
                continue
            if final and i == 1 and len([1 for d, j in added if j == 0]) < tok_count:
                continue
            before = gradients[i]
            out = product(
                [[lefts[d, i][s] for d in here] for s in slots],
                [[cots[d][s] for d in here] for s in slots],
                width,
                columns,
                held=before[0] if before else None,
                sums=gradients[0][1] if final and i == 1 else None,
                copies=0 if not final else tok_count * user_count if i == 1 else 1,
            )
            added.update((d, i) for d in here)
            gradients[i] = out
            tick.append(out[0])
            clock[0] += time

    start_far("B")
    cots[0] = [(block, 0) for block in by_slot]
    own_cots = join(cot_parts(0), tick)
    tick[:] = [own_cots]
    cots[0] = cots_at(own_cots, 0)
    clock[0] += latency
    while True:
        for lane in ("B", "A"):
            if far[lane] and free(lane):
                start_far(lane)
        if crossed and free("C"):
            start_core()
        if ready and free("X"):
            start_across()
        while start_near():
            pass
        if not flying:
            break
        entry = min(flying, key=lambda entry: entry[:2])
        flying.remove(entry)
        clock[0] = max(clock[0], entry[0])
        tick.append(entry[3])
        entry[4](entry[3])
        add_products()
    add_products()
    sums = gradients[1][1]
    sums = lax.all_to_all(sums, ("user", "tok"), split_axis=0, concat_axis=0, tiled=True)
    return combine(user, sums, [g[0] for g in gradients], clip_bound, scaling)


def solution(mesh):
    return jax.shard_map(
        body,
        mesh=mesh,
        in_specs=(P("user", "tok", None), P("user", "tok", None), P("user")),
        out_specs=P("tok", "user"),
        check_vma=False,
    )
```

```python
import functools
import math

import jax
import jax.numpy as jnp
from jax import lax
from jax.experimental import pallas as pl
from jax.experimental.pallas import tpu as pltpu
from jax.sharding import PartitionSpec as P

epsilon = 1e-06
lanes = 128
first_part = 0.625
most_flying = 5
dear = 12 * 10**9
dear_per_byte = 2 * 10**4
start_time = 1.5
latency = 1.0
link_rate = 5e4
product_time = 16.0
ANY = pl.BlockSpec(memory_space=pl.ANY)
SMEM = pl.BlockSpec(memory_space=pltpu.SMEM)
VMEM = pl.BlockSpec(memory_space=pltpu.VMEM)
HBM = pl.BlockSpec(memory_space=pltpu.HBM)


def exchange(block, axis, distance):
    size = lax.axis_size(axis)
    return lax.ppermute(block, axis, [(i, i ^ distance) for i in range(size)])


def pack_kernel(distances, tok_ref, hidden_ref, *refs):
    out_refs, sems = refs[-1 - len(distances) : -1], refs[-1]
    width = out_refs[0].shape[1]
    copies = []
    for at, distance in enumerate(distances):
        start = pl.multiple_of((tok_ref[0] ^ distance) * width, lanes)
        copies.append(
            pltpu.make_async_copy(
                hidden_ref.at[0, :, pl.ds(start, width)], out_refs[at], sems.at[at]
            )
        )
    for copy in copies:
        copy.start()
    for copy in copies:
        copy.wait()


def pack(tok, hidden, distances, width, after):
    rows = hidden.shape[1]
    count = len(distances)
    return pl.pallas_call(
        functools.partial(pack_kernel, distances),
        out_shape=[jax.ShapeDtypeStruct((rows, width), hidden.dtype)] * count,
        in_specs=[SMEM, HBM] + [ANY] * len(after),
        out_specs=[VMEM] * count,
        scratch_shapes=[pltpu.SemaphoreType.DMA((count,))],
        compiler_params=pltpu.CompilerParams(vmem_limit_bytes=2**20),
        cost_estimate=pl.CostEstimate(
            flops=0, bytes_accessed=4 * count * rows * width, transcendentals=0
        ),
        name="pack_columns",
    )(tok, hidden, *after)


def join_kernel(parts, *refs):
    out_ref = refs[-1]
    to = 0
    for at, start, width in parts:
        out_ref[:, to : to + width] = refs[at][:, start : start + width]
        to += width


def join(parts, after):
    arrays, places = [], []
    for array, start, width in parts:
        at = [i for i, other in enumerate(arrays) if other is array]
        if not at:
            arrays.append(array)
        places.append((at[0] if at else len(arrays) - 1, start, width))
    after = [array for array in after if not any(array is other for other in arrays)]
    rows = arrays[0].shape[0]
    total = sum(width for _, _, width in parts)
    return pl.pallas_call(
        functools.partial(join_kernel, places),
        out_shape=jax.ShapeDtypeStruct((rows, total), arrays[0].dtype),
        in_specs=[VMEM] * len(arrays) + [ANY] * len(after),
        out_specs=VMEM,
        compiler_params=pltpu.CompilerParams(vmem_limit_bytes=6 * 2**20),
        cost_estimate=pl.CostEstimate(flops=dear, bytes_accessed=0, transcendentals=0),
        name="join_columns",
    )(*arrays, *after)


def hold_kernel(message_ref, out_ref):
    out_ref[...] = message_ref[...]


def hold(message, flops):
    tile = pl.BlockSpec((16, lanes), lambda i: (0, 0))
    return pl.pallas_call(
        hold_kernel,
        grid=(1,),
        out_shape=jax.ShapeDtypeStruct((16, lanes), message.dtype),
        in_specs=[tile],
        out_specs=tile,
        cost_estimate=pl.CostEstimate(flops=flops, bytes_accessed=0, transcendentals=0),
        name="hold",
    )(message)


def mask_kernel(valid_ref, user_ref, cot_ref, *out_refs):
    rows, width = out_refs[0].shape
    keep = lax.broadcasted_iota(jnp.int32, (rows, width), 0) < valid_ref[0]
    for slot, out_ref in enumerate(out_refs):
        column = pl.multiple_of((user_ref[0] ^ slot) * width, lanes)
        block = cot_ref[0, :, pl.ds(column, width)]
        out_ref[...] = jnp.where(keep, block, jnp.zeros_like(block))


def mask(valid, user, cotangent, user_count):
    _, rows, total = cotangent.shape
    return pl.pallas_call(
        mask_kernel,
        out_shape=[jax.ShapeDtypeStruct((rows, total // user_count), cotangent.dtype)] * user_count,
        in_specs=[SMEM, SMEM, VMEM],
        out_specs=[VMEM] * user_count,
        compiler_params=pltpu.CompilerParams(vmem_limit_bytes=2 * 2**20),
        name="mask_cotangent",
    )(valid, user, cotangent)


def product_kernel(lefts, rights, tile, has_held, has_sums, copies, *refs):
    outs = refs[-2:] if copies else refs[-1:]
    inputs = list(refs[: -len(outs)])
    sums_in = inputs.pop() if has_sums else None
    held_ref = inputs.pop() if has_held else None
    product_ref = outs[0]
    user_count, width, columns = product_ref.shape
    squares = []
    for slot in range(user_count):
        right = jnp.concatenate(
            [refs[at][:, start : start + columns] for at, start in rights[slot]], axis=0
        )

        def step(i, total, slot=slot, right=right):
            rows = pl.ds(pl.multiple_of(i * tile, tile), tile)
            left = jnp.concatenate(
                [
                    refs[at][:, pl.ds(pl.multiple_of(start + i * tile, lanes), tile)]
                    for at, start in lefts[slot]
                ],
                axis=0,
            )
            value = lax.dot_general(
                left, right, (((0,), (0,)), ((), ())), preferred_element_type=jnp.float32
            )
            if has_held:
                value += held_ref[slot, rows, :]
            product_ref[slot, rows, :] = value
            if copies:
                row = jnp.sum(value * value, axis=0, keepdims=True)
                for start in range(0, columns, lanes):
                    total += row[:, start : start + lanes]
            return total

        squares.append(lax.fori_loop(0, width // tile, step, jnp.zeros((1, lanes), jnp.float32)))
    if copies:
        rows = jnp.concatenate(squares + [jnp.zeros((8 - user_count, lanes), jnp.float32)], axis=0)
        if has_sums:
            rows += sums_in[0]
        outs[1][...] = jnp.broadcast_to(rows[None], outs[1].shape)


def product(lefts, rights, width, columns, held=None, sums=None, copies=0):
    operands, at = [], {}

    def place(part):
        array, start = part
        if id(array) not in at:
            at[id(array)] = len(operands)
            operands.append(array)
        return at[id(array)], start

    user_count, sources = len(lefts), len(lefts[0])
    left_places = [[place(part) for part in slot] for slot in lefts]
    right_places = [[place(part) for part in slot] for slot in rights]
    tokens = sources * lefts[0][0][0].shape[0]
    aliases = {}
    if held is not None:
        aliases = {len(operands): 0}
        operands.append(held)
    if sums is not None:
        operands.append(sums)
    out_shape = [jax.ShapeDtypeStruct((user_count, width, columns), jnp.float32)]
    if copies:
        out_shape.append(jax.ShapeDtypeStruct((copies, 8, lanes), jnp.float32))
    tile = math.gcd(width, 2 * lanes)
    return pl.pallas_call(
        functools.partial(
            product_kernel, left_places, right_places, tile, held is not None, sums is not None, copies
        ),
        out_shape=out_shape,
        in_specs=[VMEM] * len(operands),
        out_specs=[VMEM] * len(out_shape),
        input_output_aliases=aliases,
        compiler_params=pltpu.CompilerParams(vmem_limit_bytes=8 * 2**20),
        cost_estimate=pl.CostEstimate(
            flops=2 * user_count * tokens * columns * width,
            bytes_accessed=2 * user_count * tokens * (width + columns),
            transcendentals=0,
        ),
        name="product_and_squares",
    )(*operands)


def combine_kernel(user_count, clip_bound, scaling, starts, user_ref, sums_ref, *refs):
    out_ref, factor_ref = refs[-2:]

    @pl.when(pl.program_id(0) == 0)
    def _():
        per_user = sums_ref.shape[0] // user_count
        by_source = [
            jnp.sum(sums_ref[j * per_user : (j + 1) * per_user], axis=0) for j in range(user_count)
        ]
        factors = []
        for u in range(user_count):
            row = sum(by_source[j][j ^ u : (j ^ u) + 1, :] for j in range(user_count))
            norm_sq = jnp.sum(row, axis=1, keepdims=True)
            factors.append(jnp.minimum(1.0, clip_bound / jnp.sqrt(norm_sq + epsilon)) * scaling)
        for slot in range(user_count):
            user = user_ref[0] ^ slot
            factor = sum(jnp.where(user == u, factors[u], 0.0) for u in range(user_count))
            factor_ref[slot : slot + 1, :] = jnp.broadcast_to(factor, (1, lanes))

    by_slot = [factor_ref[slot : slot + 1, 0:1] for slot in range(user_count)]
    tile = out_ref.shape[0]
    row = pl.program_id(0) * tile
    for ref, start in zip(refs, starts):

        @pl.when((row >= start) & (row < start + ref.shape[1]))
        def _(ref=ref, start=start):
            at = pl.ds(pl.multiple_of(row - start, tile), tile)
            result = by_slot[0] * ref[0, at, :]
            for slot in range(1, user_count):
                result += by_slot[slot] * ref[slot, at, :]
            out_ref[...] = result


def combine(user, sums, gradients, clip_bound, scaling):
    user_count, _, columns = gradients[0].shape
    heights = [gradient.shape[1] for gradient in gradients]
    starts = [sum(heights[:i]) for i in range(len(heights))]
    rows = sum(heights)
    tile = math.gcd(256, *heights)
    return pl.pallas_call(
        functools.partial(combine_kernel, user_count, clip_bound, scaling, starts),
        grid=(rows // tile,),
        out_shape=jax.ShapeDtypeStruct((rows, columns), jnp.float32),
        in_specs=[SMEM] + [VMEM] * (1 + len(gradients)),
        out_specs=pl.BlockSpec((tile, columns), lambda i: (i, 0)),
        scratch_shapes=[pltpu.VMEM((8, lanes), jnp.float32)],
        compiler_params=pltpu.CompilerParams(vmem_limit_bytes=8 * 2**20),
        name="weighted_sum",
    )(user, sums, *gradients)


def body(hidden, cotangent, lengths):
    tok_count = lax.axis_size("tok")
    user_count = lax.axis_size("user")
    tok_rows = hidden.shape[1]
    hidden_width = hidden.shape[2]
    model_width = cotangent.shape[2]
    capacity = tok_rows * tok_count
    own_width = hidden_width // tok_count
    columns = model_width // user_count
    clip_bound = math.sqrt(8.0 * hidden_width * model_width * capacity)
    scaling = math.sqrt(hidden_width * model_width) / (user_count * clip_bound)
    user = lax.axis_index("user").astype(jnp.int32).reshape(1)
    tok = lax.axis_index("tok").astype(jnp.int32).reshape(1)
    valid = lengths - tok * tok_rows
    half = tok_count // 2
    across, core = user_count // 2, user_count // 4
    slots = range(user_count)
    cut = round(own_width // lanes * first_part) * lanes
    pieces = [(0, cut), (cut, own_width - cut)]

    cots = {}
    lefts = {}
    ready = []
    crossed = []
    tick = []
    flying = []
    clock, number = [0.0], [0]

    def start(axis, distance, parts, rate, channels, action):
        message = join(parts, tick)
        tick[:] = [message]
        size = 2 * tok_rows * sum(part[2] for part in parts)
        clock[0] += start_time
        number[0] += 1
        end = clock[0] + latency + size / rate
        flying.append((end, number[0], channels, exchange(message, axis, distance), action))
        return message

    def free(*channels):
        busy = {channel for entry in flying for channel in entry[2]}
        return len(flying) < most_flying and not busy & set(channels)

    def cot_parts(d):
        return [(*cots[d][s], columns) for s in slots]

    def cots_at(array, first):
        return [(array, first + s * columns) for s in slots]

    masked = mask(valid, user, cotangent, user_count)
    by_slot = [masked[0]] + [exchange(masked[s], "user", s) for s in range(1, user_count)]
    outgoing = pack(tok, hidden, list(range(tok_count)), own_width, [masked[0]])
    ready += [(0, i, outgoing[0], first) for i, (first, _) in enumerate(pieces)]

    far = {
        "A": [(None, None)] + [(d, None) for d in range(half + 2, tok_count - 1, 2)] + [(half, 1)],
        "B": [(half, 0)]
        + [(d, None) for d in range(half + 1, tok_count - 2, 2)]
        + [(tok_count - 1, 0), (tok_count - 1, 1)],
    }
    near = list(range(1, half))
    relayed = {half}

    def start_far(lane):
        d, i = far[lane].pop(0)
        if d is None:
            parts = cot_parts(0)

            def action(array):
                cots[half] = cots_at(array, 0)

        else:
            first, width = pieces[i] if i is not None else (0, own_width)
            parts = [(outgoing[d], first, width)]

            def action(array):
                for j, (at, _) in enumerate(pieces):
                    if i is None or i == j:
                        ready.append((d, j, array, at - first))

        start("tok", half if d is None else d, parts, link_rate / 4, {lane}, action)

    def start_near():
        for d in near:
            bits = {bit for bit in range(half.bit_length()) if d >> bit & 1}
            if free(*bits):
                near.remove(d)

                def action(array, d=d):
                    ready.extend((d, j, array, at) for j, (at, _) in enumerate(pieces))

                start("tok", d, [(outgoing[d], 0, own_width)], link_rate, bits, action)
                return True
        for bit in range(half.bit_length() - 1):
            step = 1 << bit
            if step in near or not free(bit):
                continue
            sources = [d for d in cots if d % (2 * step) == 0 and d + step not in relayed]
            if sources:
                relayed.update(d + step for d in sources)
                parts = [part for d in sources for part in cot_parts(d)]

                def action(array, sources=sources, step=step):
                    for at, d in enumerate(sources):
                        cots[d + step] = cots_at(array, at * model_width)

                start("tok", step, parts, link_rate, {bit}, action)
                return True
        return False

    def start_across():
        blocks, total = [], 0
        while ready and total < 2 * own_width:
            blocks.append(ready.pop(0))
            total += pieces[blocks[-1][1]][1]
        parts = [(array, first, pieces[i][1]) for _, i, array, first in blocks]
        own = start(
            "user", across, parts, link_rate, {"X"}, lambda other: crossed.append((blocks, own, other))
        )

    def start_core():
        blocks, own, other = crossed.pop(0)
        total = sum(pieces[i][1] for _, i, _, _ in blocks)

        def action(both):
            to = 0
            for d, i, _, _ in blocks:
                lefts[d, i] = {
                    0: (own, to),
                    across: (other, to),
                    core: (both, to),
                    across ^ core: (both, total + to),
                }
                to += pieces[i][1]

        parts = [(own, 0, total), (other, 0, total)]
        message = start("user", core, parts, 6 * link_rate, {"C"}, action)
        tick[:] = [hold(message, dear_per_byte * 4 * tok_rows * total)]

    gradients = [None, None]
    added = set()

    def add_products():
        ends = [entry[0] for entry in flying if entry[2] & {"A", "B"}]
        for i, (_, width) in enumerate(pieces):
            here = [d for d in cots if (d, i) in lefts and (d, i) not in added]
            final = len(here) + len([1 for d, j in added if j == i]) == tok_count
            early = gradients[i] is None and len(here) >= tok_count - 2 - i
            if not here or not (final or early) or (final and i == 1 and gradients[0] is None):
                continue
            time = product_time * width / own_width * (len(here) / tok_count + 0.5)
            if not final and ends and min(ends) - clock[0] < time / 2:
                continue
            if final and i == 1 and len([1 for d, j in added if j == 0]) < tok_count:
                continue
            before = gradients[i]
            out = product(
                [[lefts[d, i][s] for d in here] for s in slots],
                [[cots[d][s] for d in here] for s in slots],
                width,
                columns,
                held=before[0] if before else None,
                sums=gradients[0][1] if final and i == 1 else None,
                copies=0 if not final else tok_count * user_count if i == 1 else 1,
            )
            added.update((d, i) for d in here)
            gradients[i] = out
            tick.append(out[0])
            clock[0] += time

    start_far("B")
    cots[0] = [(block, 0) for block in by_slot]
    own_cots = join(cot_parts(0), tick)
    tick[:] = [own_cots]
    cots[0] = cots_at(own_cots, 0)
    clock[0] += latency
    while True:
        for lane in ("B", "A"):
            if far[lane] and free(lane):
                start_far(lane)
        if crossed and free("C"):
            start_core()
        if ready and free("X"):
            start_across()
        while start_near():
            pass
        if not flying:
            break
        entry = min(flying, key=lambda entry: entry[:2])
        flying.remove(entry)
        clock[0] = max(clock[0], entry[0])
        tick.append(entry[3])
        entry[4](entry[3])
        add_products()
    add_products()
    sums = gradients[1][1]
    sums = lax.all_to_all(sums, ("user", "tok"), split_axis=0, concat_axis=0, tiled=True)
    return combine(user, sums, [g[0] for g in gradients], clip_bound, scaling)


def solution(mesh):
    return jax.shard_map(
        body,
        mesh=mesh,
        in_specs=(P("user", "tok", None), P("user", "tok", None), P("user")),
        out_specs=P("tok", "user"),
        check_vma=False,
    )
```

```python
import functools
import math

import jax
import jax.numpy as jnp
from jax import lax
from jax.experimental import pallas as pl
from jax.experimental.pallas import tpu as pltpu
from jax.sharding import PartitionSpec as P

epsilon = 1e-06
lanes = 128
first_part = 0.5
dear = 3 * 10**10
ANY = pl.BlockSpec(memory_space=pl.ANY)
SMEM = pl.BlockSpec(memory_space=pltpu.SMEM)
VMEM = pl.BlockSpec(memory_space=pltpu.VMEM)
HBM = pl.BlockSpec(memory_space=pltpu.HBM)


def exchange(block, axis, distance):
    size = lax.axis_size(axis)
    return lax.ppermute(block, axis, [(i, i ^ distance) for i in range(size)])


def pack_kernel(distances, tok_ref, hidden_ref, *refs):
    out_refs, sems = refs[-1 - len(distances) : -1], refs[-1]
    width = out_refs[0].shape[1]
    copies = []
    for at, distance in enumerate(distances):
        start = pl.multiple_of((tok_ref[0] ^ distance) * width, lanes)
        copies.append(
            pltpu.make_async_copy(
                hidden_ref.at[0, :, pl.ds(start, width)], out_refs[at], sems.at[at]
            )
        )
    for copy in copies:
        copy.start()
    for copy in copies:
        copy.wait()


def pack(tok, hidden, distances, width, after):
    rows = hidden.shape[1]
    count = len(distances)
    return pl.pallas_call(
        functools.partial(pack_kernel, distances),
        out_shape=[jax.ShapeDtypeStruct((rows, width), hidden.dtype)] * count,
        in_specs=[SMEM, HBM] + [ANY] * len(after),
        out_specs=[VMEM] * count,
        scratch_shapes=[pltpu.SemaphoreType.DMA((count,))],
        compiler_params=pltpu.CompilerParams(vmem_limit_bytes=2**20),
        cost_estimate=pl.CostEstimate(
            flops=0, bytes_accessed=4 * count * rows * width, transcendentals=0
        ),
        name="pack_columns",
    )(tok, hidden, *after)


def join_kernel(parts, *refs):
    out_ref = refs[-1]
    to = 0
    for at, start, width in parts:
        out_ref[:, to : to + width] = refs[at][:, start : start + width]
        to += width


def join(parts, after):
    arrays, places = [], []
    for array, start, width in parts:
        at = [i for i, other in enumerate(arrays) if other is array]
        if not at:
            arrays.append(array)
        places.append((at[0] if at else len(arrays) - 1, start, width))
    after = [array for array in after if not any(array is other for other in arrays)]
    rows = arrays[0].shape[0]
    total = sum(width for _, _, width in parts)
    return pl.pallas_call(
        functools.partial(join_kernel, places),
        out_shape=jax.ShapeDtypeStruct((rows, total), arrays[0].dtype),
        in_specs=[VMEM] * len(arrays) + [ANY] * len(after),
        out_specs=VMEM,
        compiler_params=pltpu.CompilerParams(vmem_limit_bytes=max(2**20, 8 * rows * total - 2**24)),
        cost_estimate=pl.CostEstimate(flops=0, bytes_accessed=4 * rows * total, transcendentals=0),
        name="join_columns",
    )(*arrays, *after)


def hold_kernel(message_ref, out_ref):
    out_ref[...] = jnp.zeros_like(out_ref)


def hold(message):
    return pl.pallas_call(
        hold_kernel,
        out_shape=jax.ShapeDtypeStruct((16, lanes), message.dtype),
        in_specs=[ANY],
        out_specs=VMEM,
        cost_estimate=pl.CostEstimate(flops=dear, bytes_accessed=0, transcendentals=0),
        compiler_params=pltpu.CompilerParams(vmem_limit_bytes=2**20),
        name="hold",
    )(message)


def mask_kernel(valid_ref, user_ref, cot_ref, *out_refs):
    rows, width = out_refs[0].shape
    keep = lax.broadcasted_iota(jnp.int32, (rows, width), 0) < valid_ref[0]
    for slot, out_ref in enumerate(out_refs):
        column = pl.multiple_of((user_ref[0] ^ slot) * width, lanes)
        block = cot_ref[0, :, pl.ds(column, width)]
        out_ref[...] = jnp.where(keep, block, jnp.zeros_like(block))


def mask(valid, user, cotangent, user_count):
    _, rows, total = cotangent.shape
    return pl.pallas_call(
        mask_kernel,
        out_shape=[jax.ShapeDtypeStruct((rows, total // user_count), cotangent.dtype)] * user_count,
        in_specs=[SMEM, SMEM, VMEM],
        out_specs=[VMEM] * user_count,
        compiler_params=pltpu.CompilerParams(vmem_limit_bytes=2 * 2**20),
        name="mask_cotangent",
    )(valid, user, cotangent)


def product_kernel(lefts, rights, tile, has_held, has_sums, copies, *refs):
    outs = refs[-2:] if copies else refs[-1:]
    inputs = list(refs[: -len(outs)])
    sums_in = inputs.pop() if has_sums else None
    held_ref = inputs.pop() if has_held else None
    product_ref = outs[0]
    user_count, width, columns = product_ref.shape
    squares = []
    for slot in range(user_count):
        right = jnp.concatenate(
            [refs[at][:, start : start + columns] for at, start in rights[slot]], axis=0
        )

        def step(i, total, slot=slot, right=right):
            rows = pl.ds(pl.multiple_of(i * tile, tile), tile)
            left = jnp.concatenate(
                [
                    refs[at][:, pl.ds(pl.multiple_of(start + i * tile, lanes), tile)]
                    for at, start in lefts[slot]
                ],
                axis=0,
            )
            value = lax.dot_general(
                left, right, (((0,), (0,)), ((), ())), preferred_element_type=jnp.float32
            )
            if has_held:
                value += held_ref[slot, rows, :]
            product_ref[slot, rows, :] = value
            if copies:
                row = jnp.sum(value * value, axis=0, keepdims=True)
                for start in range(0, columns, lanes):
                    total += row[:, start : start + lanes]
            return total

        squares.append(lax.fori_loop(0, width // tile, step, jnp.zeros((1, lanes), jnp.float32)))
    if copies:
        rows = jnp.concatenate(squares + [jnp.zeros((8 - user_count, lanes), jnp.float32)], axis=0)
        if has_sums:
            rows += sums_in[0]
        outs[1][...] = jnp.broadcast_to(rows[None], outs[1].shape)


def product(lefts, rights, width, columns, held=None, sums=None, copies=0):
    operands, at = [], {}

    def place(part):
        array, start = part
        if id(array) not in at:
            at[id(array)] = len(operands)
            operands.append(array)
        return at[id(array)], start

    user_count, sources = len(lefts), len(lefts[0])
    left_places = [[place(part) for part in slot] for slot in lefts]
    right_places = [[place(part) for part in slot] for slot in rights]
    tokens = sources * lefts[0][0][0].shape[0]
    aliases = {}
    if held is not None:
        aliases = {len(operands): 0}
        operands.append(held)
    if sums is not None:
        operands.append(sums)
    out_shape = [jax.ShapeDtypeStruct((user_count, width, columns), jnp.float32)]
    if copies:
        out_shape.append(jax.ShapeDtypeStruct((copies, 8, lanes), jnp.float32))
    tile = math.gcd(width, 2 * lanes)
    return pl.pallas_call(
        functools.partial(
            product_kernel, left_places, right_places, tile, held is not None, sums is not None, copies
        ),
        out_shape=out_shape,
        in_specs=[VMEM] * len(operands),
        out_specs=[VMEM] * len(out_shape),
        input_output_aliases=aliases,
        compiler_params=pltpu.CompilerParams(vmem_limit_bytes=8 * 2**20),
        cost_estimate=pl.CostEstimate(
            flops=2 * user_count * tokens * columns * width,
            bytes_accessed=2 * user_count * tokens * (width + columns),
            transcendentals=0,
        ),
        name="product_and_squares",
    )(*operands)


def combine_kernel(user_count, clip_bound, scaling, starts, user_ref, sums_ref, *refs):
    out_ref, factor_ref = refs[-2:]

    @pl.when(pl.program_id(0) == 0)
    def _():
        per_user = sums_ref.shape[0] // user_count
        by_source = [
            jnp.sum(sums_ref[j * per_user : (j + 1) * per_user], axis=0) for j in range(user_count)
        ]
        factors = []
        for u in range(user_count):
            row = sum(by_source[j][j ^ u : (j ^ u) + 1, :] for j in range(user_count))
            norm_sq = jnp.sum(row, axis=1, keepdims=True)
            factors.append(jnp.minimum(1.0, clip_bound / jnp.sqrt(norm_sq + epsilon)) * scaling)
        for slot in range(user_count):
            user = user_ref[0] ^ slot
            factor = sum(jnp.where(user == u, factors[u], 0.0) for u in range(user_count))
            factor_ref[slot : slot + 1, :] = jnp.broadcast_to(factor, (1, lanes))

    by_slot = [factor_ref[slot : slot + 1, 0:1] for slot in range(user_count)]
    tile = out_ref.shape[0]
    row = pl.program_id(0) * tile
    for ref, start in zip(refs, starts):

        @pl.when((row >= start) & (row < start + ref.shape[1]))
        def _(ref=ref, start=start):
            at = pl.ds(pl.multiple_of(row - start, tile), tile)
            result = by_slot[0] * ref[0, at, :]
            for slot in range(1, user_count):
                result += by_slot[slot] * ref[slot, at, :]
            out_ref[...] = result


def combine(user, sums, gradients, clip_bound, scaling):
    user_count, _, columns = gradients[0].shape
    heights = [gradient.shape[1] for gradient in gradients]
    starts = [sum(heights[:i]) for i in range(len(heights))]
    rows = sum(heights)
    tile = math.gcd(256, *heights)
    return pl.pallas_call(
        functools.partial(combine_kernel, user_count, clip_bound, scaling, starts),
        grid=(rows // tile,),
        out_shape=jax.ShapeDtypeStruct((rows, columns), jnp.float32),
        in_specs=[SMEM] + [VMEM] * (1 + len(gradients)),
        out_specs=pl.BlockSpec((tile, columns), lambda i: (i, 0)),
        scratch_shapes=[pltpu.VMEM((8, lanes), jnp.float32)],
        compiler_params=pltpu.CompilerParams(vmem_limit_bytes=8 * 2**20),
        name="weighted_sum",
    )(user, sums, *gradients)


def body(hidden, cotangent, lengths):
    tok_count = lax.axis_size("tok")
    user_count = lax.axis_size("user")
    tok_rows = hidden.shape[1]
    hidden_width = hidden.shape[2]
    model_width = cotangent.shape[2]
    capacity = tok_rows * tok_count
    own_width = hidden_width // tok_count
    columns = model_width // user_count
    clip_bound = math.sqrt(8.0 * hidden_width * model_width * capacity)
    scaling = math.sqrt(hidden_width * model_width) / (user_count * clip_bound)
    user = lax.axis_index("user").astype(jnp.int32).reshape(1)
    tok = lax.axis_index("tok").astype(jnp.int32).reshape(1)
    valid = lengths - tok * tok_rows
    half = tok_count // 2
    across, core = user_count // 2, user_count // 4
    slots = range(user_count)
    cut = round(own_width // lanes * first_part) * lanes
    pieces = [(0, cut), (cut, own_width - cut)]

    cots = {}
    lefts = {}
    ready = []
    tick = []

    def send(axis, distance, parts, after=()):
        message = join(parts, [*tick, *after])
        tick[:] = [message]
        return message, exchange(message, axis, distance)

    def cot_parts(d):
        return [(*cots[d][s], columns) for s in slots]

    def cots_at(array, start):
        return [(array, start + s * columns) for s in slots]

    masked = mask(valid, user, cotangent, user_count)
    by_slot = [masked[0]] + [exchange(masked[s], "user", s) for s in range(1, user_count)]
    outgoing = pack(tok, hidden, list(range(tok_count)), own_width, [masked[0]])
    ready += [(0, i, outgoing[0], start) for i, (start, _) in enumerate(pieces)]

    far_steps = []
    for i, (start, width) in enumerate(pieces):
        for d in range(half, tok_count, 2):
            far_steps.append([("block", e, i) for e in (d, d + 1)])
    far_steps.insert(1, [("cots", half, 0), ("cots", half, 1)])
    near = list(range(1, half))
    near_steps = [near[:2]] + [near[i : i + 2] if tok_count > 8 else near[i : i + 1] for i in range(2, len(near), 2)]
    relay_bits = [half >> i for i in range(1, half.bit_length())]

    lanes_before = [None, None]
    near_before, relay_before, cross_before, core_before = [], [], None, None
    gradients = []
    done = set()

    def finish_core():
        nonlocal core_before
        if core_before is None:
            return
        blocks, own, other, both = core_before
        core_before = None
        total = sum(pieces[i][1] for _, i, _, _ in blocks)
        to = 0
        for d, i, _, _ in blocks:
            lefts[d, i] = {0: (own, to), across: (other, to), core: (both, to), across ^ core: (both, total + to)}
            to += pieces[i][1]

    def add_products(step):
        if len(cots) < tok_count:
            return
        for i, (_, width) in enumerate(pieces):
            here = [d for d in range(tok_count) if (d, i) in lefts and (d, i) not in done]
            all_here = all((d, i) in lefts for d in range(tok_count))
            if not here or not (all_here or (i == 1 and step >= len(far_steps))):
                continue
            before = gradients[i] if len(gradients) > i else None
            final = all_here and i == 1
            out = product(
                [[lefts[d, i][s] for d in here] for s in slots],
                [[cots[d][s] for d in here] for s in slots],
                width,
                columns,
                held=before[0] if before else None,
                sums=gradients[0][1] if final else None,
                copies=0 if not all_here else tok_count * user_count if final else 1,
            )
            done.update((d, i) for d in here)
            gradients[i : i + 1] = [out]
            tick.append(out[0])

    for step in range(len(far_steps) + 2):
        arrivals = []
        for lane in (0, 1):
            after = []
            if lanes_before[lane] is not None:
                after.append(lanes_before[lane][1])
                arrivals.append(lanes_before[lane])
                lanes_before[lane] = None
            if step < len(far_steps):
                kind, d, i = far_steps[step][lane]
                if kind == "block":
                    parts = [(outgoing[d], *pieces[i])]
                else:
                    parts = cot_parts(0)[lane * user_count // 2 : (lane + 1) * user_count // 2]
                message = send("tok", d, parts, after)
                lanes_before[lane] = (far_steps[step][lane], message[1])
        for (kind, d, i), array in arrivals:
            if kind == "block":
                ready.append((d, i, array, 0))
            else:
                cots.setdefault(d, [])
                cots[d] = cots[d] + [(array, s * columns) for s in range(user_count // 2)]
        for d, array in near_before:
            ready += [(d, i, array, start) for i, (start, _) in enumerate(pieces)]
            if d & (d - 1) == 0:
                cots[d] = cots_at(array, own_width)
        for bit, sources, array in relay_before:
            for at, d in enumerate(sources):
                cots[d + bit] = cots_at(array, at * model_width)
        near_before, relay_before = [], []
        crossed = cross_before
        cross_before = None
        if ready:
            blocks = []
            while ready and sum(pieces[i][1] for _, i, _, _ in blocks) < 2 * own_width:
                blocks.append(ready.pop(0))
            parts = [(array, start, pieces[i][1]) for _, i, array, start in blocks]
            own, other = send("user", across, parts, [crossed[2]] if crossed else [])
            cross_before = (blocks, own, other)
        if step == 0:
            cots[0] = [(block, 0) for block in by_slot]
            cots[0] = cots_at(join(cot_parts(0), []), 0)
        if step < len(near_steps):
            for d in near_steps[step]:
                parts = [(outgoing[d], 0, own_width)]
                if d & (d - 1) == 0:
                    parts += cot_parts(0)
                near_before.append((d, send("tok", d, parts)[1]))
        if relay_bits:
            bit = relay_bits[0]
            sources = list(range(2 * bit, tok_count, 2 * bit))
            if all(d in cots and len(cots[d]) == user_count for d in sources):
                relay_bits.pop(0)
                parts = [part for d in sources for part in cot_parts(d)]
                relay_before.append((bit, sources, send("tok", bit, parts)[1]))
        earlier = [core_before[3]] if core_before else []
        finish_core()
        if crossed:
            blocks, own, other = crossed
            total = sum(pieces[i][1] for _, i, _, _ in blocks)
            both = send("user", core, [(own, 0, total), (other, 0, total)], earlier)[1]
            core_before = (blocks, own, other, both)
        if step < len(far_steps):
            tick[:] = [hold(tick[0])]
        if step >= len(far_steps) - 1:
            finish_core()
            if relay_before:
                for bit, sources, array in relay_before:
                    for at, d in enumerate(sources):
                        cots[d + bit] = cots_at(array, at * model_width)
                relay_before = []
            add_products(step)
    sums = lax.all_to_all(gradients[1][1], ("user", "tok"), split_axis=0, concat_axis=0, tiled=True)
    return combine(user, sums, [g[0] for g in gradients], clip_bound, scaling)


def solution(mesh):
    return jax.shard_map(
        body,
        mesh=mesh,
        in_specs=(P("user", "tok", None), P("user", "tok", None), P("user")),
        out_specs=P("tok", "user"),
        check_vma=False,
    )
```

```python
import functools
import math

import jax
import jax.numpy as jnp
from jax import lax
from jax.experimental import pallas as pl
from jax.experimental.pallas import tpu as pltpu
from jax.sharding import PartitionSpec as P

epsilon = 1e-06
lanes = 128
first_part = 0.5
dear = 24 * 10**10
dear_per_byte = 2 * 10**5
ANY = pl.BlockSpec(memory_space=pl.ANY)
SMEM = pl.BlockSpec(memory_space=pltpu.SMEM)
VMEM = pl.BlockSpec(memory_space=pltpu.VMEM)
HBM = pl.BlockSpec(memory_space=pltpu.HBM)


def exchange(block, axis, distance):
    size = lax.axis_size(axis)
    return lax.ppermute(block, axis, [(i, i ^ distance) for i in range(size)])


def pack_kernel(distances, tok_ref, hidden_ref, *refs):
    out_refs, sems = refs[-1 - len(distances) : -1], refs[-1]
    width = out_refs[0].shape[1]
    copies = []
    for at, distance in enumerate(distances):
        start = pl.multiple_of((tok_ref[0] ^ distance) * width, lanes)
        copies.append(
            pltpu.make_async_copy(
                hidden_ref.at[0, :, pl.ds(start, width)], out_refs[at], sems.at[at]
            )
        )
    for copy in copies:
        copy.start()
    for copy in copies:
        copy.wait()


def pack(tok, hidden, distances, width, after):
    rows = hidden.shape[1]
    count = len(distances)
    return pl.pallas_call(
        functools.partial(pack_kernel, distances),
        out_shape=[jax.ShapeDtypeStruct((rows, width), hidden.dtype)] * count,
        in_specs=[SMEM, HBM] + [ANY] * len(after),
        out_specs=[VMEM] * count,
        scratch_shapes=[pltpu.SemaphoreType.DMA((count,))],
        compiler_params=pltpu.CompilerParams(vmem_limit_bytes=2**20),
        cost_estimate=pl.CostEstimate(
            flops=0, bytes_accessed=4 * count * rows * width, transcendentals=0
        ),
        name="pack_columns",
    )(tok, hidden, *after)


def join_kernel(parts, *refs):
    out_ref = refs[-1]
    to = 0
    for at, start, width in parts:
        out_ref[:, to : to + width] = refs[at][:, start : start + width]
        to += width


def join(parts, after):
    arrays, places = [], []
    for array, start, width in parts:
        at = [i for i, other in enumerate(arrays) if other is array]
        if not at:
            arrays.append(array)
        places.append((at[0] if at else len(arrays) - 1, start, width))
    after = [array for array in after if not any(array is other for other in arrays)]
    rows = arrays[0].shape[0]
    total = sum(width for _, _, width in parts)
    return pl.pallas_call(
        functools.partial(join_kernel, places),
        out_shape=jax.ShapeDtypeStruct((rows, total), arrays[0].dtype),
        in_specs=[VMEM] * len(arrays) + [ANY] * len(after),
        out_specs=VMEM,
        compiler_params=pltpu.CompilerParams(vmem_limit_bytes=max(2**20, 8 * rows * total - 2**24)),
        cost_estimate=pl.CostEstimate(flops=0, bytes_accessed=4 * rows * total, transcendentals=0),
        name="join_columns",
    )(*arrays, *after)


def hold_kernel(*refs):
    out_ref = refs[-1]
    out_ref[...] = jnp.zeros_like(out_ref)


def hold(message, after, size):
    return pl.pallas_call(
        hold_kernel,
        out_shape=jax.ShapeDtypeStruct((16, lanes), message.dtype),
        in_specs=[ANY] * (1 + len(after)),
        out_specs=VMEM,
        cost_estimate=pl.CostEstimate(flops=max(dear, dear_per_byte * size) // lax.axis_size("tok"), bytes_accessed=0, transcendentals=0),
        compiler_params=pltpu.CompilerParams(vmem_limit_bytes=2**20),
        name="hold",
    )(message, *after)


def mask_kernel(valid_ref, user_ref, cot_ref, *out_refs):
    rows, width = out_refs[0].shape
    keep = lax.broadcasted_iota(jnp.int32, (rows, width), 0) < valid_ref[0]
    for slot, out_ref in enumerate(out_refs):
        column = pl.multiple_of((user_ref[0] ^ slot) * width, lanes)
        block = cot_ref[0, :, pl.ds(column, width)]
        out_ref[...] = jnp.where(keep, block, jnp.zeros_like(block))


def mask(valid, user, cotangent, user_count):
    _, rows, total = cotangent.shape
    return pl.pallas_call(
        mask_kernel,
        out_shape=[jax.ShapeDtypeStruct((rows, total // user_count), cotangent.dtype)] * user_count,
        in_specs=[SMEM, SMEM, VMEM],
        out_specs=[VMEM] * user_count,
        compiler_params=pltpu.CompilerParams(vmem_limit_bytes=2 * 2**20),
        name="mask_cotangent",
    )(valid, user, cotangent)


def product_kernel(lefts, rights, tile, has_held, has_sums, copies, *refs):
    outs = refs[-2:] if copies else refs[-1:]
    inputs = list(refs[: -len(outs)])
    sums_in = inputs.pop() if has_sums else None
    held_ref = inputs.pop() if has_held else None
    product_ref = outs[0]
    user_count, width, columns = product_ref.shape
    squares = []
    for slot in range(user_count):
        right = jnp.concatenate(
            [refs[at][:, start : start + columns] for at, start in rights[slot]], axis=0
        )

        def step(i, total, slot=slot, right=right):
            rows = pl.ds(pl.multiple_of(i * tile, tile), tile)
            left = jnp.concatenate(
                [
                    refs[at][:, pl.ds(pl.multiple_of(start + i * tile, lanes), tile)]
                    for at, start in lefts[slot]
                ],
                axis=0,
            )
            value = lax.dot_general(
                left, right, (((0,), (0,)), ((), ())), preferred_element_type=jnp.float32
            )
            if has_held:
                value += held_ref[slot, rows, :]
            product_ref[slot, rows, :] = value
            if copies:
                row = jnp.sum(value * value, axis=0, keepdims=True)
                for start in range(0, columns, lanes):
                    total += row[:, start : start + lanes]
            return total

        squares.append(lax.fori_loop(0, width // tile, step, jnp.zeros((1, lanes), jnp.float32)))
    if copies:
        rows = jnp.concatenate(squares + [jnp.zeros((8 - user_count, lanes), jnp.float32)], axis=0)
        if has_sums:
            rows += sums_in[0]
        outs[1][...] = jnp.broadcast_to(rows[None], outs[1].shape)


def product(lefts, rights, width, columns, held=None, sums=None, copies=0):
    operands, at = [], {}

    def place(part):
        array, start = part
        if id(array) not in at:
            at[id(array)] = len(operands)
            operands.append(array)
        return at[id(array)], start

    user_count, sources = len(lefts), len(lefts[0])
    left_places = [[place(part) for part in slot] for slot in lefts]
    right_places = [[place(part) for part in slot] for slot in rights]
    tokens = sources * lefts[0][0][0].shape[0]
    aliases = {}
    if held is not None:
        aliases = {len(operands): 0}
        operands.append(held)
    if sums is not None:
        operands.append(sums)
    out_shape = [jax.ShapeDtypeStruct((user_count, width, columns), jnp.float32)]
    if copies:
        out_shape.append(jax.ShapeDtypeStruct((copies, 8, lanes), jnp.float32))
    tile = math.gcd(width, 2 * lanes)
    return pl.pallas_call(
        functools.partial(
            product_kernel, left_places, right_places, tile, held is not None, sums is not None, copies
        ),
        out_shape=out_shape,
        in_specs=[VMEM] * len(operands),
        out_specs=[VMEM] * len(out_shape),
        input_output_aliases=aliases,
        compiler_params=pltpu.CompilerParams(vmem_limit_bytes=8 * 2**20),
        cost_estimate=pl.CostEstimate(
            flops=2 * user_count * tokens * columns * width,
            bytes_accessed=2 * user_count * tokens * (width + columns),
            transcendentals=0,
        ),
        name="product_and_squares",
    )(*operands)


def combine_kernel(user_count, clip_bound, scaling, starts, user_ref, sums_ref, *refs):
    out_ref, factor_ref = refs[-2:]

    @pl.when(pl.program_id(0) == 0)
    def _():
        per_user = sums_ref.shape[0] // user_count
        by_source = [
            jnp.sum(sums_ref[j * per_user : (j + 1) * per_user], axis=0) for j in range(user_count)
        ]
        factors = []
        for u in range(user_count):
            row = sum(by_source[j][j ^ u : (j ^ u) + 1, :] for j in range(user_count))
            norm_sq = jnp.sum(row, axis=1, keepdims=True)
            factors.append(jnp.minimum(1.0, clip_bound / jnp.sqrt(norm_sq + epsilon)) * scaling)
        for slot in range(user_count):
            user = user_ref[0] ^ slot
            factor = sum(jnp.where(user == u, factors[u], 0.0) for u in range(user_count))
            factor_ref[slot : slot + 1, :] = jnp.broadcast_to(factor, (1, lanes))

    by_slot = [factor_ref[slot : slot + 1, 0:1] for slot in range(user_count)]
    tile = out_ref.shape[0]
    row = pl.program_id(0) * tile
    for ref, start in zip(refs, starts):

        @pl.when((row >= start) & (row < start + ref.shape[1]))
        def _(ref=ref, start=start):
            at = pl.ds(pl.multiple_of(row - start, tile), tile)
            result = by_slot[0] * ref[0, at, :]
            for slot in range(1, user_count):
                result += by_slot[slot] * ref[slot, at, :]
            out_ref[...] = result


def combine(user, sums, gradients, clip_bound, scaling):
    user_count, _, columns = gradients[0].shape
    heights = [gradient.shape[1] for gradient in gradients]
    starts = [sum(heights[:i]) for i in range(len(heights))]
    rows = sum(heights)
    tile = math.gcd(256, *heights)
    return pl.pallas_call(
        functools.partial(combine_kernel, user_count, clip_bound, scaling, starts),
        grid=(rows // tile,),
        out_shape=jax.ShapeDtypeStruct((rows, columns), jnp.float32),
        in_specs=[SMEM] + [VMEM] * (1 + len(gradients)),
        out_specs=pl.BlockSpec((tile, columns), lambda i: (i, 0)),
        scratch_shapes=[pltpu.VMEM((8, lanes), jnp.float32)],
        compiler_params=pltpu.CompilerParams(vmem_limit_bytes=8 * 2**20),
        name="weighted_sum",
    )(user, sums, *gradients)


def body(hidden, cotangent, lengths):
    tok_count = lax.axis_size("tok")
    user_count = lax.axis_size("user")
    tok_rows = hidden.shape[1]
    hidden_width = hidden.shape[2]
    model_width = cotangent.shape[2]
    capacity = tok_rows * tok_count
    own_width = hidden_width // tok_count
    columns = model_width // user_count
    clip_bound = math.sqrt(8.0 * hidden_width * model_width * capacity)
    scaling = math.sqrt(hidden_width * model_width) / (user_count * clip_bound)
    user = lax.axis_index("user").astype(jnp.int32).reshape(1)
    tok = lax.axis_index("tok").astype(jnp.int32).reshape(1)
    valid = lengths - tok * tok_rows
    half = tok_count // 2
    across, core = user_count // 2, user_count // 4
    slots = range(user_count)
    cut = round(own_width // lanes * first_part) * lanes
    pieces = [(0, cut), (cut, own_width - cut)]

    cots = {}
    lefts = {}
    ready = []
    tick = []

    sizes = [0]

    def send(axis, distance, parts, after=()):
        message = join(parts, [*tick, *after])
        sizes.append(2 * message.size)
        tick[:] = [message]
        return message, exchange(message, axis, distance)

    def cot_parts(d):
        return [(*cots[d][s], columns) for s in slots]

    def cots_at(array, start):
        return [(array, start + s * columns) for s in slots]

    masked = mask(valid, user, cotangent, user_count)
    by_slot = [masked[0]] + [exchange(masked[s], "user", s) for s in range(1, user_count)]
    outgoing = pack(tok, hidden, list(range(tok_count)), own_width, [masked[0]])
    ready += [(0, i, outgoing[0], start) for i, (start, _) in enumerate(pieces)]

    far = list(range(half + 1, tok_count))
    far_steps = [[(half, None), ("cots", None)], [None, None]]
    while len(far) > 1:
        far_steps += [[(far.pop(0), None), (far.pop(0), None)], [None, None]]
    far_steps += [[(far[0], 0), ("wait", None)], [(far[0], 1), None]]
    last_pair = len(far_steps) - 3
    near = list(range(1, half))
    near_steps = [near[:2]] + [[d] for d in near[2:]]
    relayed = set()

    def bits_below(d):
        return [1 << i for i in range(((d & -d) or 1).bit_length() - 1)]


    lanes_before = [None, None]
    near_before, relay_before, cross_before, core_before = [], [], None, None
    crossed = []
    gradients = [None, None]
    done = set()

    def finish_core():
        nonlocal core_before
        if core_before is not None:
            units, both = core_before
            core_before = None
            to = 0
            for blocks, own, other in units:
                total = sum(pieces[i][1] for _, i, _, _ in blocks)
                at = 0
                for d, i, _, _ in blocks:
                    lefts[d, i] = {
                        0: (own, at),
                        across: (other, at),
                        core: (both, to + at),
                        across ^ core: (both, to + total + at),
                    }
                    at += pieces[i][1]
                to += 2 * total

    def finish_relays():
        for bit, sources, array in relay_before:
            for at, d in enumerate(sources):
                cots[d + bit] = cots_at(array, at * model_width)
        relay_before.clear()

    def add_products(i):
        width = pieces[i][1]
        here = [d for d in range(tok_count) if d in cots and (d, i) in lefts and (d, i) not in done]
        if not here:
            return
        done.update((d, i) for d in here)
        full = all((d, i) in done for d in range(tok_count))
        out = product(
            [[lefts[d, i][s] for d in here] for s in slots],
            [[cots[d][s] for d in here] for s in slots],
            width,
            columns,
            held=gradients[i][0] if gradients[i] else None,
            sums=gradients[0][1] if full and i == 1 else None,
            copies=0 if not full else tok_count * user_count if i == 1 else 1,
        )
        gradients[i] = out
        tick.append(out[0])

    for step in range(len(far_steps) + 2):
        flying = 0
        now = far_steps[step] if step < len(far_steps) else [None, ("wait", None)]
        if step == len(far_steps):
            now = [("wait", None), None]
        for lane in (0, 1):
            if lane == 1 and now[1] == ("cots", None):
                continue
            if now[lane] is not None:
                after = []
                if lanes_before[lane] is not None:
                    (d, i), array = lanes_before[lane]
                    lanes_before[lane] = None
                    after.append(array)
                    if d == "cots":
                        cots[half] = cots_at(array, 0)
                    else:
                        first = pieces[i][0] if i is not None else 0
                        ready += [
                            (d, j, array, at - first) for j, (at, _) in enumerate(pieces) if i is None or i == j
                        ]
                d, i = now[lane]
                if d != "wait":
                    first, width = pieces[i] if i is not None else (0, own_width)
                    array = send("tok", d, [(outgoing[d], first, width)], after)[1]
                    lanes_before[lane] = (now[lane], array)
            flying += lanes_before[lane] is not None
        for d, array in near_before:
            ready += [(d, i, array, first) for i, (first, _) in enumerate(pieces)]
            if d & (d - 1) == 0:
                cots[d] = cots_at(array, own_width)
        near_before.clear()
        arrivals = [array for _, _, array in relay_before]
        finish_relays()
        if cross_before is not None:
            crossed.append(cross_before)
        earlier = [cross_before[2]] if cross_before is not None else []
        cross_before = None
        if ready:
            blocks = []
            while ready and sum(pieces[i][1] for _, i, _, _ in blocks) < 2 * own_width:
                blocks.append(ready.pop(0))
            parts = [(array, first, pieces[i][1]) for _, i, array, first in blocks]
            own, other = send("user", across, parts, earlier)
            cross_before = (blocks, own, other)
            flying += 1
        if step == 0:
            cots[0] = [(block, 0) for block in by_slot]
            cots[0] = cots_at(join(cot_parts(0), tick), 0)
            lanes_before[1] = (("cots", None), send("tok", half, cot_parts(0))[1])
            flying += 1
        if step < len(near_steps):
            for d in near_steps[step]:
                parts = [(outgoing[d], 0, own_width)]
                if d & (d - 1) == 0:
                    parts += cot_parts(0)
                near_before.append((d, send("tok", d, parts)[1]))
                flying += 1
        before = [core_before[1]] if core_before else []
        finish_core()
        relays_wait = any(
            d and d + bit not in relayed for d in cots for bit in bits_below(d)
        )
        if crossed and (flying < 5 - relays_wait or step > last_pair):
            parts = []
            for blocks, own, other in crossed:
                total = sum(pieces[i][1] for _, i, _, _ in blocks)
                parts += [(own, 0, total), (other, 0, total)]
            core_before = (list(crossed), send("user", core, parts, before)[1])
            crossed.clear()
            flying += 1
        bit = half // 2
        while bit:
            sources = [d for d in sorted(cots) if bit in bits_below(d) and d + bit not in relayed]
            if sources and flying < 5:
                relayed.update(d + bit for d in sources)
                parts = [part for d in sources for part in cot_parts(d)]
                relay_before.append((bit, sources, send("tok", bit, parts)[1]))
                flying += 1
            bit //= 2
        if step < len(far_steps):
            tick[:] = [hold(tick[0], arrivals, max(sizes))]
            sizes[:] = [0]
        if step == last_pair:
            finish_core()
            add_products(0)
            add_products(1)
    finish_core()
    add_products(0)
    add_products(1)
    sums = lax.all_to_all(gradients[1][1], ("user", "tok"), split_axis=0, concat_axis=0, tiled=True)
    return combine(user, sums, [g[0] for g in gradients], clip_bound, scaling)


def solution(mesh):
    return jax.shard_map(
        body,
        mesh=mesh,
        in_specs=(P("user", "tok", None), P("user", "tok", None), P("user")),
        out_specs=P("tok", "user"),
        check_vma=False,
    )
```

```python
import functools
import math

import jax
import jax.numpy as jnp
from jax import lax
from jax.experimental import pallas as pl
from jax.experimental.pallas import tpu as pltpu
from jax.sharding import PartitionSpec as P

epsilon = 1e-06
lanes = 128
first_part = 0.5
dear = 24 * 10**10
dear_per_byte = 2 * 10**5
ANY = pl.BlockSpec(memory_space=pl.ANY)
SMEM = pl.BlockSpec(memory_space=pltpu.SMEM)
VMEM = pl.BlockSpec(memory_space=pltpu.VMEM)
HBM = pl.BlockSpec(memory_space=pltpu.HBM)


def exchange(block, axis, distance):
    size = lax.axis_size(axis)
    return lax.ppermute(block, axis, [(i, i ^ distance) for i in range(size)])


def pack_kernel(distances, tok_ref, hidden_ref, *refs):
    out_refs, sems = refs[-1 - len(distances) : -1], refs[-1]
    width = out_refs[0].shape[1]
    copies = []
    for at, distance in enumerate(distances):
        start = pl.multiple_of((tok_ref[0] ^ distance) * width, lanes)
        copies.append(
            pltpu.make_async_copy(
                hidden_ref.at[0, :, pl.ds(start, width)], out_refs[at], sems.at[at]
            )
        )
    for copy in copies:
        copy.start()
    for copy in copies:
        copy.wait()


def pack(tok, hidden, distances, width, after):
    rows = hidden.shape[1]
    count = len(distances)
    return pl.pallas_call(
        functools.partial(pack_kernel, distances),
        out_shape=[jax.ShapeDtypeStruct((rows, width), hidden.dtype)] * count,
        in_specs=[SMEM, HBM] + [ANY] * len(after),
        out_specs=[VMEM] * count,
        scratch_shapes=[pltpu.SemaphoreType.DMA((count,))],
        compiler_params=pltpu.CompilerParams(vmem_limit_bytes=2**20),
        cost_estimate=pl.CostEstimate(
            flops=0, bytes_accessed=4 * count * rows * width, transcendentals=0
        ),
        name="pack_columns",
    )(tok, hidden, *after)


def join_kernel(parts, *refs):
    out_ref = refs[-1]
    to = 0
    for at, start, width in parts:
        out_ref[:, to : to + width] = refs[at][:, start : start + width]
        to += width


def join(parts, after):
    arrays, places = [], []
    for array, start, width in parts:
        at = [i for i, other in enumerate(arrays) if other is array]
        if not at:
            arrays.append(array)
        places.append((at[0] if at else len(arrays) - 1, start, width))
    after = [array for array in after if not any(array is other for other in arrays)]
    rows = arrays[0].shape[0]
    total = sum(width for _, _, width in parts)
    return pl.pallas_call(
        functools.partial(join_kernel, places),
        out_shape=jax.ShapeDtypeStruct((rows, total), arrays[0].dtype),
        in_specs=[VMEM] * len(arrays) + [ANY] * len(after),
        out_specs=VMEM,
        compiler_params=pltpu.CompilerParams(vmem_limit_bytes=max(2**20, 8 * rows * total - 2**24)),
        cost_estimate=pl.CostEstimate(flops=0, bytes_accessed=4 * rows * total, transcendentals=0),
        name="join_columns",
    )(*arrays, *after)


def hold_kernel(*refs):
    out_ref = refs[-1]
    out_ref[...] = jnp.zeros_like(out_ref)


def hold(message, after, size):
    return pl.pallas_call(
        hold_kernel,
        out_shape=jax.ShapeDtypeStruct((16, lanes), message.dtype),
        in_specs=[ANY] * (1 + len(after)),
        out_specs=VMEM,
        cost_estimate=pl.CostEstimate(flops=max(dear, dear_per_byte * size) // lax.axis_size("tok"), bytes_accessed=0, transcendentals=0),
        compiler_params=pltpu.CompilerParams(vmem_limit_bytes=2**20),
        name="hold",
    )(message, *after)


def mask_kernel(valid_ref, user_ref, cot_ref, *out_refs):
    rows, width = out_refs[0].shape
    keep = lax.broadcasted_iota(jnp.int32, (rows, width), 0) < valid_ref[0]
    for slot, out_ref in enumerate(out_refs):
        column = pl.multiple_of((user_ref[0] ^ slot) * width, lanes)
        block = cot_ref[0, :, pl.ds(column, width)]
        out_ref[...] = jnp.where(keep, block, jnp.zeros_like(block))


def mask(valid, user, cotangent, user_count):
    _, rows, total = cotangent.shape
    return pl.pallas_call(
        mask_kernel,
        out_shape=[jax.ShapeDtypeStruct((rows, total // user_count), cotangent.dtype)] * user_count,
        in_specs=[SMEM, SMEM, VMEM],
        out_specs=[VMEM] * user_count,
        compiler_params=pltpu.CompilerParams(vmem_limit_bytes=2 * 2**20),
        name="mask_cotangent",
    )(valid, user, cotangent)


def product_kernel(lefts, rights, tile, has_held, has_sums, copies, *refs):
    outs = refs[-2:] if copies else refs[-1:]
    inputs = list(refs[: -len(outs)])
    sums_in = inputs.pop() if has_sums else None
    held_ref = inputs.pop() if has_held else None
    product_ref = outs[0]
    user_count, width, columns = product_ref.shape
    squares = []
    for slot in range(user_count):
        right = jnp.concatenate(
            [refs[at][:, start : start + columns] for at, start in rights[slot]], axis=0
        )

        def step(i, total, slot=slot, right=right):
            rows = pl.ds(pl.multiple_of(i * tile, tile), tile)
            left = jnp.concatenate(
                [
                    refs[at][:, pl.ds(pl.multiple_of(start + i * tile, lanes), tile)]
                    for at, start in lefts[slot]
                ],
                axis=0,
            )
            value = lax.dot_general(
                left, right, (((0,), (0,)), ((), ())), preferred_element_type=jnp.float32
            )
            if has_held:
                value += held_ref[slot, rows, :]
            product_ref[slot, rows, :] = value
            if copies:
                row = jnp.sum(value * value, axis=0, keepdims=True)
                for start in range(0, columns, lanes):
                    total += row[:, start : start + lanes]
            return total

        squares.append(lax.fori_loop(0, width // tile, step, jnp.zeros((1, lanes), jnp.float32)))
    if copies:
        rows = jnp.concatenate(squares + [jnp.zeros((8 - user_count, lanes), jnp.float32)], axis=0)
        if has_sums:
            rows += sums_in[0]
        outs[1][...] = jnp.broadcast_to(rows[None], outs[1].shape)


def product(lefts, rights, width, columns, held=None, sums=None, copies=0):
    operands, at = [], {}

    def place(part):
        array, start = part
        if id(array) not in at:
            at[id(array)] = len(operands)
            operands.append(array)
        return at[id(array)], start

    user_count, sources = len(lefts), len(lefts[0])
    left_places = [[place(part) for part in slot] for slot in lefts]
    right_places = [[place(part) for part in slot] for slot in rights]
    tokens = sources * lefts[0][0][0].shape[0]
    aliases = {}
    if held is not None:
        aliases = {len(operands): 0}
        operands.append(held)
    if sums is not None:
        operands.append(sums)
    out_shape = [jax.ShapeDtypeStruct((user_count, width, columns), jnp.float32)]
    if copies:
        out_shape.append(jax.ShapeDtypeStruct((copies, 8, lanes), jnp.float32))
    tile = math.gcd(width, 2 * lanes)
    return pl.pallas_call(
        functools.partial(
            product_kernel, left_places, right_places, tile, held is not None, sums is not None, copies
        ),
        out_shape=out_shape,
        in_specs=[VMEM] * len(operands),
        out_specs=[VMEM] * len(out_shape),
        input_output_aliases=aliases,
        compiler_params=pltpu.CompilerParams(vmem_limit_bytes=8 * 2**20),
        cost_estimate=pl.CostEstimate(
            flops=2 * user_count * tokens * columns * width,
            bytes_accessed=2 * user_count * tokens * (width + columns),
            transcendentals=0,
        ),
        name="product_and_squares",
    )(*operands)


def combine_kernel(user_count, clip_bound, scaling, starts, user_ref, sums_ref, *refs):
    out_ref, factor_ref = refs[-2:]

    @pl.when(pl.program_id(0) == 0)
    def _():
        per_user = sums_ref.shape[0] // user_count
        by_source = [
            jnp.sum(sums_ref[j * per_user : (j + 1) * per_user], axis=0) for j in range(user_count)
        ]
        factors = []
        for u in range(user_count):
            row = sum(by_source[j][j ^ u : (j ^ u) + 1, :] for j in range(user_count))
            norm_sq = jnp.sum(row, axis=1, keepdims=True)
            factors.append(jnp.minimum(1.0, clip_bound / jnp.sqrt(norm_sq + epsilon)) * scaling)
        for slot in range(user_count):
            user = user_ref[0] ^ slot
            factor = sum(jnp.where(user == u, factors[u], 0.0) for u in range(user_count))
            factor_ref[slot : slot + 1, :] = jnp.broadcast_to(factor, (1, lanes))

    by_slot = [factor_ref[slot : slot + 1, 0:1] for slot in range(user_count)]
    tile = out_ref.shape[0]
    row = pl.program_id(0) * tile
    for ref, start in zip(refs, starts):

        @pl.when((row >= start) & (row < start + ref.shape[1]))
        def _(ref=ref, start=start):
            at = pl.ds(pl.multiple_of(row - start, tile), tile)
            result = by_slot[0] * ref[0, at, :]
            for slot in range(1, user_count):
                result += by_slot[slot] * ref[slot, at, :]
            out_ref[...] = result


def combine(user, sums, gradients, clip_bound, scaling):
    user_count, _, columns = gradients[0].shape
    heights = [gradient.shape[1] for gradient in gradients]
    starts = [sum(heights[:i]) for i in range(len(heights))]
    rows = sum(heights)
    tile = math.gcd(256, *heights)
    return pl.pallas_call(
        functools.partial(combine_kernel, user_count, clip_bound, scaling, starts),
        grid=(rows // tile,),
        out_shape=jax.ShapeDtypeStruct((rows, columns), jnp.float32),
        in_specs=[SMEM] + [VMEM] * (1 + len(gradients)),
        out_specs=pl.BlockSpec((tile, columns), lambda i: (i, 0)),
        scratch_shapes=[pltpu.VMEM((8, lanes), jnp.float32)],
        compiler_params=pltpu.CompilerParams(vmem_limit_bytes=8 * 2**20),
        name="weighted_sum",
    )(user, sums, *gradients)


def body(hidden, cotangent, lengths):
    tok_count = lax.axis_size("tok")
    user_count = lax.axis_size("user")
    tok_rows = hidden.shape[1]
    hidden_width = hidden.shape[2]
    model_width = cotangent.shape[2]
    capacity = tok_rows * tok_count
    own_width = hidden_width // tok_count
    columns = model_width // user_count
    clip_bound = math.sqrt(8.0 * hidden_width * model_width * capacity)
    scaling = math.sqrt(hidden_width * model_width) / (user_count * clip_bound)
    user = lax.axis_index("user").astype(jnp.int32).reshape(1)
    tok = lax.axis_index("tok").astype(jnp.int32).reshape(1)
    valid = lengths - tok * tok_rows
    half = tok_count // 2
    across, core = user_count // 2, user_count // 4
    slots = range(user_count)
    cut = round(own_width // lanes * first_part) * lanes
    pieces = [(0, cut), (cut, own_width - cut)]

    cots = {}
    lefts = {}
    ready = []
    tick = []

    sizes = [0]

    def send(axis, distance, parts, after=()):
        message = join(parts, [*tick, *after])
        sizes.append(2 * message.size)
        tick[:] = [message]
        return message, exchange(message, axis, distance)

    def cot_parts(d):
        return [(*cots[d][s], columns) for s in slots]

    def cots_at(array, start):
        return [(array, start + s * columns) for s in slots]

    masked = mask(valid, user, cotangent, user_count)
    by_slot = [masked[0]] + [exchange(masked[s], "user", s) for s in range(1, user_count)]
    outgoing = pack(tok, hidden, list(range(tok_count)), own_width, [masked[0]])
    ready += [(0, i, outgoing[0], start) for i, (start, _) in enumerate(pieces)]

    far = list(range(half + 1, tok_count))
    far_steps = [[(half, None), ("cots", None)], [None, None]]
    while len(far) > 1:
        far_steps += [[(far.pop(0), None), (far.pop(0), None)], [None, None]]
    far_steps += [[(far[0], 0), ("wait", None)], [(far[0], 1), None]]
    last_pair = len(far_steps) - 3
    near = list(range(1, half))
    near_steps = [near[:2]] + [[d] for d in near[2:]]
    relayed = set()

    def bits_below(d):
        return [1 << i for i in range(((d & -d) or 1).bit_length() - 1)]


    lanes_before = [None, None]
    near_before, relay_before, cross_before, core_before = [], [], None, None
    crossed = []
    gradients = [None, None]
    done = set()

    def finish_core():
        nonlocal core_before
        if core_before is not None:
            units, both = core_before
            core_before = None
            to = 0
            for blocks, own, other in units:
                total = sum(pieces[i][1] for _, i, _, _ in blocks)
                at = 0
                for d, i, _, _ in blocks:
                    lefts[d, i] = {
                        0: (own, at),
                        across: (other, at),
                        core: (both, to + at),
                        across ^ core: (both, to + total + at),
                    }
                    at += pieces[i][1]
                to += 2 * total

    def finish_relays(step):
        arrived = []
        for entry in list(relay_before):
            due, bit, sources, array = entry
            if due <= step:
                relay_before.remove(entry)
                arrived.append(array)
                for at, d in enumerate(sources):
                    cots[d + bit] = cots_at(array, at * model_width)
        return arrived

    def add_products(i):
        width = pieces[i][1]
        here = [d for d in range(tok_count) if d in cots and (d, i) in lefts and (d, i) not in done]
        if not here:
            return
        done.update((d, i) for d in here)
        full = all((d, i) in done for d in range(tok_count))
        out = product(
            [[lefts[d, i][s] for d in here] for s in slots],
            [[cots[d][s] for d in here] for s in slots],
            width,
            columns,
            held=gradients[i][0] if gradients[i] else None,
            sums=gradients[0][1] if full and i == 1 else None,
            copies=0 if not full else tok_count * user_count if i == 1 else 1,
        )
        gradients[i] = out
        tick.append(out[0])

    for step in range(len(far_steps) + 2):
        flying = 0
        now = far_steps[step] if step < len(far_steps) else [None, ("wait", None)]
        if step == len(far_steps):
            now = [("wait", None), None]
        for lane in (0, 1):
            if lane == 1 and now[1] == ("cots", None):
                continue
            if now[lane] is not None:
                after = []
                if lanes_before[lane] is not None:
                    (d, i), array = lanes_before[lane]
                    lanes_before[lane] = None
                    after.append(array)
                    if d == "cots":
                        cots[half] = cots_at(array, 0)
                    else:
                        first = pieces[i][0] if i is not None else 0
                        ready += [
                            (d, j, array, at - first) for j, (at, _) in enumerate(pieces) if i is None or i == j
                        ]
                d, i = now[lane]
                if d != "wait":
                    first, width = pieces[i] if i is not None else (0, own_width)
                    array = send("tok", d, [(outgoing[d], first, width)], after)[1]
                    lanes_before[lane] = (now[lane], array)
            flying += lanes_before[lane] is not None
        for d, array in near_before:
            ready += [(d, i, array, first) for i, (first, _) in enumerate(pieces)]
            if d & (d - 1) == 0:
                cots[d] = cots_at(array, own_width)
        near_before.clear()
        arrivals = finish_relays(step)
        if cross_before is not None:
            crossed.append(cross_before)
        earlier = [cross_before[2]] if cross_before is not None else []
        cross_before = None
        if ready:
            blocks = []
            while ready and sum(pieces[i][1] for _, i, _, _ in blocks) < 2 * own_width:
                blocks.append(ready.pop(0))
            parts = [(array, first, pieces[i][1]) for _, i, array, first in blocks]
            own, other = send("user", across, parts, earlier)
            cross_before = (blocks, own, other)
            flying += 1
        if step == 0:
            cots[0] = [(block, 0) for block in by_slot]
            cots[0] = cots_at(join(cot_parts(0), tick), 0)
            lanes_before[1] = (("cots", None), send("tok", half, cot_parts(0))[1])
            flying += 1
        if step < len(near_steps):
            for d in near_steps[step]:
                parts = [(outgoing[d], 0, own_width)]
                if d & (d - 1) == 0:
                    parts += cot_parts(0)
                near_before.append((d, send("tok", d, parts)[1]))
                flying += 1
        before = [core_before[1]] if core_before else []
        finish_core()
        relays_wait = any(
            d and d + bit not in relayed for d in cots for bit in bits_below(d)
        )
        if crossed and (flying < 5 - relays_wait or step > last_pair):
            parts = []
            for blocks, own, other in crossed:
                total = sum(pieces[i][1] for _, i, _, _ in blocks)
                parts += [(own, 0, total), (other, 0, total)]
            core_before = (list(crossed), send("user", core, parts, before)[1])
            crossed.clear()
            flying += 1
        bit = half // 2
        while bit:
            sources = [d for d in sorted(cots) if bit in bits_below(d) and d + bit not in relayed]
            if sources and flying < 5:
                relayed.update(d + bit for d in sources)
                parts = [part for d in sources for part in cot_parts(d)]
                relay_before.append((step + (2 if step >= last_pair else 1), bit, sources, send("tok", bit, parts)[1]))
                flying += 1
            bit //= 2
        if step < len(far_steps):
            tick[:] = [hold(tick[0], arrivals, max(sizes))]
            sizes[:] = [0]
        if step == last_pair + 1:
            add_products(0)
            add_products(1)
    finish_core()
    add_products(0)
    add_products(1)
    sums = lax.all_to_all(gradients[1][1], ("user", "tok"), split_axis=0, concat_axis=0, tiled=True)
    return combine(user, sums, [g[0] for g in gradients], clip_bound, scaling)


def solution(mesh):
    return jax.shard_map(
        body,
        mesh=mesh,
        in_specs=(P("user", "tok", None), P("user", "tok", None), P("user")),
        out_specs=P("tok", "user"),
        check_vma=False,
    )
```

```python
import functools
import math

import jax
import jax.numpy as jnp
from jax import lax
from jax.experimental import pallas as pl
from jax.experimental.pallas import tpu as pltpu
from jax.sharding import PartitionSpec as P

epsilon = 1e-06
lanes = 128
first_part = 0.625
dear = 24 * 10**10
dear_per_byte = 2 * 10**5
ANY = pl.BlockSpec(memory_space=pl.ANY)
SMEM = pl.BlockSpec(memory_space=pltpu.SMEM)
VMEM = pl.BlockSpec(memory_space=pltpu.VMEM)
HBM = pl.BlockSpec(memory_space=pltpu.HBM)


def exchange(block, axis, distance):
    size = lax.axis_size(axis)
    return lax.ppermute(block, axis, [(i, i ^ distance) for i in range(size)])


def pack_kernel(distances, tok_ref, hidden_ref, *refs):
    out_refs, sems = refs[-1 - len(distances) : -1], refs[-1]
    width = out_refs[0].shape[1]
    copies = []
    for at, distance in enumerate(distances):
        start = pl.multiple_of((tok_ref[0] ^ distance) * width, lanes)
        copies.append(
            pltpu.make_async_copy(
                hidden_ref.at[0, :, pl.ds(start, width)], out_refs[at], sems.at[at]
            )
        )
    for copy in copies:
        copy.start()
    for copy in copies:
        copy.wait()


def pack(tok, hidden, distances, width, after):
    rows = hidden.shape[1]
    count = len(distances)
    return pl.pallas_call(
        functools.partial(pack_kernel, distances),
        out_shape=[jax.ShapeDtypeStruct((rows, width), hidden.dtype)] * count,
        in_specs=[SMEM, HBM] + [ANY] * len(after),
        out_specs=[VMEM] * count,
        scratch_shapes=[pltpu.SemaphoreType.DMA((count,))],
        compiler_params=pltpu.CompilerParams(vmem_limit_bytes=2**20),
        cost_estimate=pl.CostEstimate(
            flops=0, bytes_accessed=4 * count * rows * width, transcendentals=0
        ),
        name="pack_columns",
    )(tok, hidden, *after)


def join_kernel(parts, *refs):
    out_ref = refs[-1]
    to = 0
    for at, start, width in parts:
        out_ref[:, to : to + width] = refs[at][:, start : start + width]
        to += width


def join(parts, after):
    arrays, places = [], []
    for array, start, width in parts:
        at = [i for i, other in enumerate(arrays) if other is array]
        if not at:
            arrays.append(array)
        places.append((at[0] if at else len(arrays) - 1, start, width))
    after = [array for array in after if not any(array is other for other in arrays)]
    rows = arrays[0].shape[0]
    total = sum(width for _, _, width in parts)
    return pl.pallas_call(
        functools.partial(join_kernel, places),
        out_shape=jax.ShapeDtypeStruct((rows, total), arrays[0].dtype),
        in_specs=[VMEM] * len(arrays) + [ANY] * len(after),
        out_specs=VMEM,
        compiler_params=pltpu.CompilerParams(vmem_limit_bytes=max(2**20, 8 * rows * total - 2**24)),
        cost_estimate=pl.CostEstimate(flops=0, bytes_accessed=4 * rows * total, transcendentals=0),
        name="join_columns",
    )(*arrays, *after)


def hold_kernel(*refs):
    out_ref = refs[-1]
    out_ref[...] = jnp.zeros_like(out_ref)


def hold(message, after, size):
    return pl.pallas_call(
        hold_kernel,
        out_shape=jax.ShapeDtypeStruct((16, lanes), message.dtype),
        in_specs=[ANY] * (1 + len(after)),
        out_specs=VMEM,
        cost_estimate=pl.CostEstimate(flops=max(dear, dear_per_byte * size) // lax.axis_size("tok"), bytes_accessed=0, transcendentals=0),
        compiler_params=pltpu.CompilerParams(vmem_limit_bytes=2**20),
        name="hold",
    )(message, *after)


def mask_kernel(valid_ref, user_ref, cot_ref, *out_refs):
    rows, width = out_refs[0].shape
    keep = lax.broadcasted_iota(jnp.int32, (rows, width), 0) < valid_ref[0]
    for slot, out_ref in enumerate(out_refs):
        column = pl.multiple_of((user_ref[0] ^ slot) * width, lanes)
        block = cot_ref[0, :, pl.ds(column, width)]
        out_ref[...] = jnp.where(keep, block, jnp.zeros_like(block))


def mask(valid, user, cotangent, user_count):
    _, rows, total = cotangent.shape
    return pl.pallas_call(
        mask_kernel,
        out_shape=[jax.ShapeDtypeStruct((rows, total // user_count), cotangent.dtype)] * user_count,
        in_specs=[SMEM, SMEM, VMEM],
        out_specs=[VMEM] * user_count,
        compiler_params=pltpu.CompilerParams(vmem_limit_bytes=2 * 2**20),
        name="mask_cotangent",
    )(valid, user, cotangent)


def product_kernel(lefts, rights, tile, has_held, has_sums, copies, *refs):
    outs = refs[-2:] if copies else refs[-1:]
    inputs = list(refs[: -len(outs)])
    sums_in = inputs.pop() if has_sums else None
    held_ref = inputs.pop() if has_held else None
    product_ref = outs[0]
    user_count, width, columns = product_ref.shape
    squares = []
    for slot in range(user_count):
        right = jnp.concatenate(
            [refs[at][:, start : start + columns] for at, start in rights[slot]], axis=0
        )

        def step(i, total, slot=slot, right=right):
            rows = pl.ds(pl.multiple_of(i * tile, tile), tile)
            left = jnp.concatenate(
                [
                    refs[at][:, pl.ds(pl.multiple_of(start + i * tile, lanes), tile)]
                    for at, start in lefts[slot]
                ],
                axis=0,
            )
            value = lax.dot_general(
                left, right, (((0,), (0,)), ((), ())), preferred_element_type=jnp.float32
            )
            if has_held:
                value += held_ref[slot, rows, :]
            product_ref[slot, rows, :] = value
            if copies:
                row = jnp.sum(value * value, axis=0, keepdims=True)
                for start in range(0, columns, lanes):
                    total += row[:, start : start + lanes]
            return total

        squares.append(lax.fori_loop(0, width // tile, step, jnp.zeros((1, lanes), jnp.float32)))
    if copies:
        rows = jnp.concatenate(squares + [jnp.zeros((8 - user_count, lanes), jnp.float32)], axis=0)
        if has_sums:
            rows += sums_in[0]
        outs[1][...] = jnp.broadcast_to(rows[None], outs[1].shape)


def product(lefts, rights, width, columns, held=None, sums=None, copies=0):
    operands, at = [], {}

    def place(part):
        array, start = part
        if id(array) not in at:
            at[id(array)] = len(operands)
            operands.append(array)
        return at[id(array)], start

    user_count, sources = len(lefts), len(lefts[0])
    left_places = [[place(part) for part in slot] for slot in lefts]
    right_places = [[place(part) for part in slot] for slot in rights]
    tokens = sources * lefts[0][0][0].shape[0]
    aliases = {}
    if held is not None:
        aliases = {len(operands): 0}
        operands.append(held)
    if sums is not None:
        operands.append(sums)
    out_shape = [jax.ShapeDtypeStruct((user_count, width, columns), jnp.float32)]
    if copies:
        out_shape.append(jax.ShapeDtypeStruct((copies, 8, lanes), jnp.float32))
    tile = math.gcd(width, 2 * lanes)
    return pl.pallas_call(
        functools.partial(
            product_kernel, left_places, right_places, tile, held is not None, sums is not None, copies
        ),
        out_shape=out_shape,
        in_specs=[VMEM] * len(operands),
        out_specs=[VMEM] * len(out_shape),
        input_output_aliases=aliases,
        compiler_params=pltpu.CompilerParams(vmem_limit_bytes=8 * 2**20),
        cost_estimate=pl.CostEstimate(
            flops=2 * user_count * tokens * columns * width,
            bytes_accessed=2 * user_count * tokens * (width + columns),
            transcendentals=0,
        ),
        name="product_and_squares",
    )(*operands)


def combine_kernel(user_count, clip_bound, scaling, starts, user_ref, sums_ref, *refs):
    out_ref, factor_ref = refs[-2:]

    @pl.when(pl.program_id(0) == 0)
    def _():
        per_user = sums_ref.shape[0] // user_count
        by_source = [
            jnp.sum(sums_ref[j * per_user : (j + 1) * per_user], axis=0) for j in range(user_count)
        ]
        factors = []
        for u in range(user_count):
            row = sum(by_source[j][j ^ u : (j ^ u) + 1, :] for j in range(user_count))
            norm_sq = jnp.sum(row, axis=1, keepdims=True)
            factors.append(jnp.minimum(1.0, clip_bound / jnp.sqrt(norm_sq + epsilon)) * scaling)
        for slot in range(user_count):
            user = user_ref[0] ^ slot
            factor = sum(jnp.where(user == u, factors[u], 0.0) for u in range(user_count))
            factor_ref[slot : slot + 1, :] = jnp.broadcast_to(factor, (1, lanes))

    by_slot = [factor_ref[slot : slot + 1, 0:1] for slot in range(user_count)]
    tile = out_ref.shape[0]
    row = pl.program_id(0) * tile
    for ref, start in zip(refs, starts):

        @pl.when((row >= start) & (row < start + ref.shape[1]))
        def _(ref=ref, start=start):
            at = pl.ds(pl.multiple_of(row - start, tile), tile)
            result = by_slot[0] * ref[0, at, :]
            for slot in range(1, user_count):
                result += by_slot[slot] * ref[slot, at, :]
            out_ref[...] = result


def combine(user, sums, gradients, clip_bound, scaling):
    user_count, _, columns = gradients[0].shape
    heights = [gradient.shape[1] for gradient in gradients]
    starts = [sum(heights[:i]) for i in range(len(heights))]
    rows = sum(heights)
    tile = math.gcd(256, *heights)
    return pl.pallas_call(
        functools.partial(combine_kernel, user_count, clip_bound, scaling, starts),
        grid=(rows // tile,),
        out_shape=jax.ShapeDtypeStruct((rows, columns), jnp.float32),
        in_specs=[SMEM] + [VMEM] * (1 + len(gradients)),
        out_specs=pl.BlockSpec((tile, columns), lambda i: (i, 0)),
        scratch_shapes=[pltpu.VMEM((8, lanes), jnp.float32)],
        compiler_params=pltpu.CompilerParams(vmem_limit_bytes=8 * 2**20),
        name="weighted_sum",
    )(user, sums, *gradients)


def body(hidden, cotangent, lengths):
    tok_count = lax.axis_size("tok")
    user_count = lax.axis_size("user")
    tok_rows = hidden.shape[1]
    hidden_width = hidden.shape[2]
    model_width = cotangent.shape[2]
    capacity = tok_rows * tok_count
    own_width = hidden_width // tok_count
    columns = model_width // user_count
    clip_bound = math.sqrt(8.0 * hidden_width * model_width * capacity)
    scaling = math.sqrt(hidden_width * model_width) / (user_count * clip_bound)
    user = lax.axis_index("user").astype(jnp.int32).reshape(1)
    tok = lax.axis_index("tok").astype(jnp.int32).reshape(1)
    valid = lengths - tok * tok_rows
    half = tok_count // 2
    across, core = user_count // 2, user_count // 4
    slots = range(user_count)
    cut = round(own_width // lanes * first_part) * lanes
    pieces = [(0, cut), (cut, own_width - cut)]

    cots = {}
    lefts = {}
    ready = []
    tick = []

    sizes = [0]

    def send(axis, distance, parts, after=()):
        message = join(parts, [*tick, *after])
        sizes.append(2 * message.size)
        tick[:] = [message]
        return message, exchange(message, axis, distance)

    def cot_parts(d):
        return [(*cots[d][s], columns) for s in slots]

    def cots_at(array, start):
        return [(array, start + s * columns) for s in slots]

    masked = mask(valid, user, cotangent, user_count)
    by_slot = [masked[0]] + [exchange(masked[s], "user", s) for s in range(1, user_count)]
    outgoing = pack(tok, hidden, list(range(tok_count)), own_width, [])
    ready += [(0, i, outgoing[0], start) for i, (start, _) in enumerate(pieces)]

    far = list(range(half + 1, tok_count))
    far_steps = [[(half, None), ("cots", None)], [None, None]]
    while len(far) > 1:
        far_steps += [[(far.pop(0), None), (far.pop(0), None)], [None, None]]
    far_steps += [[(far[0], 0), ("wait", None)], [(far[0], 1), None]]
    last_pair = len(far_steps) - 3
    near = list(range(1, half))
    near_steps = [near[:2]] + [[d] for d in near[2:]]
    relayed = set()

    def bits_below(d):
        return [1 << i for i in range(((d & -d) or 1).bit_length() - 1)]


    lanes_before = [None, None]
    near_before, relay_before, cross_before, core_before = [], [], None, None
    crossed = []
    gradients = [None, None]
    done = set()

    def finish_core():
        nonlocal core_before
        if core_before is not None:
            units, both = core_before
            core_before = None
            to = 0
            for blocks, own, other in units:
                total = sum(pieces[i][1] for _, i, _, _ in blocks)
                at = 0
                for d, i, _, _ in blocks:
                    lefts[d, i] = {
                        0: (own, at),
                        across: (other, at),
                        core: (both, to + at),
                        across ^ core: (both, to + total + at),
                    }
                    at += pieces[i][1]
                to += 2 * total

    def finish_relays(step):
        arrived = []
        for entry in list(relay_before):
            due, bit, sources, array = entry
            if due <= step:
                relay_before.remove(entry)
                arrived.append(array)
                for at, d in enumerate(sources):
                    cots[d + bit] = cots_at(array, at * model_width)
        return arrived

    def add_products(i):
        width = pieces[i][1]
        here = [d for d in range(tok_count) if d in cots and (d, i) in lefts and (d, i) not in done]
        if not here:
            return
        done.update((d, i) for d in here)
        full = all((d, i) in done for d in range(tok_count))
        out = product(
            [[lefts[d, i][s] for d in here] for s in slots],
            [[cots[d][s] for d in here] for s in slots],
            width,
            columns,
            held=gradients[i][0] if gradients[i] else None,
            sums=gradients[0][1] if full and i == 1 else None,
            copies=0 if not full else tok_count * user_count if i == 1 else 1,
        )
        gradients[i] = out
        tick.append(out[0])

    for step in range(len(far_steps) + 2):
        flying = 0
        now = far_steps[step] if step < len(far_steps) else [None, ("wait", None)]
        if step == len(far_steps):
            now = [("wait", None), None]
        for lane in (0, 1):
            if lane == 1 and now[1] == ("cots", None):
                continue
            if now[lane] is not None:
                after = []
                if lanes_before[lane] is not None:
                    (d, i), array = lanes_before[lane]
                    lanes_before[lane] = None
                    after.append(array)
                    if d == "cots":
                        cots[half] = cots_at(array, 0)
                    else:
                        first = pieces[i][0] if i is not None else 0
                        ready += [
                            (d, j, array, at - first) for j, (at, _) in enumerate(pieces) if i is None or i == j
                        ]
                d, i = now[lane]
                if d != "wait":
                    first, width = pieces[i] if i is not None else (0, own_width)
                    array = send("tok", d, [(outgoing[d], first, width)], after)[1]
                    lanes_before[lane] = (now[lane], array)
            flying += lanes_before[lane] is not None
        for d, array in near_before:
            ready += [(d, i, array, first) for i, (first, _) in enumerate(pieces)]
            if d & (d - 1) == 0:
                cots[d] = cots_at(array, own_width)
        near_before.clear()
        arrivals = finish_relays(step)
        bit = half // 2
        while bit:
            sources = [d for d in sorted(cots) if bit in bits_below(d) and d + bit not in relayed]
            if sources and flying < 3:
                relayed.update(d + bit for d in sources)
                parts = [part for d in sources for part in cot_parts(d)]
                relay_before.append((step + (2 if step >= last_pair else 1), bit, sources, send("tok", bit, parts)[1]))
                flying += 1
            bit //= 2
        if cross_before is not None:
            crossed.append(cross_before)
        earlier = [cross_before[2]] if cross_before is not None else []
        cross_before = None
        if ready:
            blocks = []
            while ready and sum(pieces[i][1] for _, i, _, _ in blocks) < 2 * own_width:
                blocks.append(ready.pop(0))
            parts = [(array, first, pieces[i][1]) for _, i, array, first in blocks]
            own, other = send("user", across, parts, earlier)
            cross_before = (blocks, own, other)
            flying += 1
        if step == 0:
            cots[0] = [(block, 0) for block in by_slot]
            cots[0] = cots_at(join(cot_parts(0), tick), 0)
            lanes_before[1] = (("cots", None), send("tok", half, cot_parts(0))[1])
            flying += 1
        if step < len(near_steps):
            for d in near_steps[step]:
                parts = [(outgoing[d], 0, own_width)]
                if d & (d - 1) == 0:
                    parts += cot_parts(0)
                near_before.append((d, send("tok", d, parts)[1]))
                flying += 1
        before = [core_before[1]] if core_before else []
        finish_core()
        if crossed and (flying < 5 or step >= last_pair):
            parts = []
            for blocks, own, other in crossed:
                total = sum(pieces[i][1] for _, i, _, _ in blocks)
                parts += [(own, 0, total), (other, 0, total)]
            core_before = (list(crossed), send("user", core, parts, before)[1])
            crossed.clear()
            flying += 1
        if step < len(far_steps):
            tick[:] = [hold(tick[0], arrivals, max(sizes))]
            sizes[:] = [0]
        if step == last_pair + 1:
            add_products(0)
        elif step == last_pair + 2:
            add_products(1)
        elif step == len(far_steps):
            finish_core()
            add_products(0)
    finish_core()
    add_products(0)
    add_products(1)
    sums = lax.all_to_all(gradients[1][1], ("user", "tok"), split_axis=0, concat_axis=0, tiled=True)
    return combine(user, sums, [g[0] for g in gradients], clip_bound, scaling)


def solution(mesh):
    return jax.shard_map(
        body,
        mesh=mesh,
        in_specs=(P("user", "tok", None), P("user", "tok", None), P("user")),
        out_specs=P("tok", "user"),
        check_vma=False,
    )
```

```python
import functools
import math

import jax
import jax.numpy as jnp
from jax import lax
from jax.experimental import pallas as pl
from jax.experimental.pallas import tpu as pltpu
from jax.sharding import PartitionSpec as P

epsilon = 1e-06
lanes = 128
first_part = 0.625
dear = 24 * 10**10
dear_per_byte = 2 * 10**5
ANY = pl.BlockSpec(memory_space=pl.ANY)
SMEM = pl.BlockSpec(memory_space=pltpu.SMEM)
VMEM = pl.BlockSpec(memory_space=pltpu.VMEM)
HBM = pl.BlockSpec(memory_space=pltpu.HBM)


def exchange(block, axis, distance):
    size = lax.axis_size(axis)
    return lax.ppermute(block, axis, [(i, i ^ distance) for i in range(size)])


def pack_kernel(distances, tok_ref, hidden_ref, *refs):
    out_refs, sems = refs[-1 - len(distances) : -1], refs[-1]
    width = out_refs[0].shape[1]
    copies = []
    for at, distance in enumerate(distances):
        start = pl.multiple_of((tok_ref[0] ^ distance) * width, lanes)
        copies.append(
            pltpu.make_async_copy(
                hidden_ref.at[0, :, pl.ds(start, width)], out_refs[at], sems.at[at]
            )
        )
    for copy in copies:
        copy.start()
    for copy in copies:
        copy.wait()


def pack(tok, hidden, distances, width, after):
    rows = hidden.shape[1]
    count = len(distances)
    return pl.pallas_call(
        functools.partial(pack_kernel, distances),
        out_shape=[jax.ShapeDtypeStruct((rows, width), hidden.dtype)] * count,
        in_specs=[SMEM, HBM] + [ANY] * len(after),
        out_specs=[VMEM] * count,
        scratch_shapes=[pltpu.SemaphoreType.DMA((count,))],
        compiler_params=pltpu.CompilerParams(vmem_limit_bytes=2**20),
        cost_estimate=pl.CostEstimate(
            flops=0, bytes_accessed=4 * count * rows * width, transcendentals=0
        ),
        name="pack_columns",
    )(tok, hidden, *after)


def join_kernel(parts, *refs):
    out_ref = refs[-1]
    to = 0
    for at, start, width in parts:
        out_ref[:, to : to + width] = refs[at][:, start : start + width]
        to += width


def join(parts, after):
    arrays, places = [], []
    for array, start, width in parts:
        at = [i for i, other in enumerate(arrays) if other is array]
        if not at:
            arrays.append(array)
        places.append((at[0] if at else len(arrays) - 1, start, width))
    after = [array for array in after if not any(array is other for other in arrays)]
    rows = arrays[0].shape[0]
    total = sum(width for _, _, width in parts)
    return pl.pallas_call(
        functools.partial(join_kernel, places),
        out_shape=jax.ShapeDtypeStruct((rows, total), arrays[0].dtype),
        in_specs=[VMEM] * len(arrays) + [ANY] * len(after),
        out_specs=VMEM,
        compiler_params=pltpu.CompilerParams(vmem_limit_bytes=max(2**20, 8 * rows * total - 2**24)),
        cost_estimate=pl.CostEstimate(flops=0, bytes_accessed=4 * rows * total, transcendentals=0),
        name="join_columns",
    )(*arrays, *after)


def hold_kernel(*refs):
    out_ref = refs[-1]
    out_ref[...] = jnp.zeros_like(out_ref)


def hold(message, after, size):
    return pl.pallas_call(
        hold_kernel,
        out_shape=jax.ShapeDtypeStruct((16, lanes), message.dtype),
        in_specs=[ANY] * (1 + len(after)),
        out_specs=VMEM,
        cost_estimate=pl.CostEstimate(flops=max(dear, dear_per_byte * size) // lax.axis_size("tok"), bytes_accessed=0, transcendentals=0),
        compiler_params=pltpu.CompilerParams(vmem_limit_bytes=2**20),
        name="hold",
    )(message, *after)


def mask_kernel(valid_ref, user_ref, cot_ref, *out_refs):
    rows, width = out_refs[0].shape
    keep = lax.broadcasted_iota(jnp.int32, (rows, width), 0) < valid_ref[0]
    for slot, out_ref in enumerate(out_refs):
        column = pl.multiple_of((user_ref[0] ^ slot) * width, lanes)
        block = cot_ref[0, :, pl.ds(column, width)]
        out_ref[...] = jnp.where(keep, block, jnp.zeros_like(block))


def mask(valid, user, cotangent, user_count):
    _, rows, total = cotangent.shape
    return pl.pallas_call(
        mask_kernel,
        out_shape=[jax.ShapeDtypeStruct((rows, total // user_count), cotangent.dtype)] * user_count,
        in_specs=[SMEM, SMEM, VMEM],
        out_specs=[VMEM] * user_count,
        compiler_params=pltpu.CompilerParams(vmem_limit_bytes=2 * 2**20),
        name="mask_cotangent",
    )(valid, user, cotangent)


def product_kernel(lefts, rights, tile, has_held, has_sums, copies, *refs):
    outs = refs[-2:] if copies else refs[-1:]
    inputs = list(refs[: -len(outs)])
    sums_in = inputs.pop() if has_sums else None
    held_ref = inputs.pop() if has_held else None
    product_ref = outs[0]
    user_count, width, columns = product_ref.shape
    squares = []
    for slot in range(user_count):
        right = jnp.concatenate(
            [refs[at][:, start : start + columns] for at, start in rights[slot]], axis=0
        )

        def step(i, total, slot=slot, right=right):
            rows = pl.ds(pl.multiple_of(i * tile, tile), tile)
            left = jnp.concatenate(
                [
                    refs[at][:, pl.ds(pl.multiple_of(start + i * tile, lanes), tile)]
                    for at, start in lefts[slot]
                ],
                axis=0,
            )
            value = lax.dot_general(
                left, right, (((0,), (0,)), ((), ())), preferred_element_type=jnp.float32
            )
            if has_held:
                value += held_ref[slot, rows, :]
            product_ref[slot, rows, :] = value
            if copies:
                row = jnp.sum(value * value, axis=0, keepdims=True)
                for start in range(0, columns, lanes):
                    total += row[:, start : start + lanes]
            return total

        squares.append(lax.fori_loop(0, width // tile, step, jnp.zeros((1, lanes), jnp.float32)))
    if copies:
        rows = jnp.concatenate(squares + [jnp.zeros((8 - user_count, lanes), jnp.float32)], axis=0)
        if has_sums:
            rows += sums_in[0]
        outs[1][...] = jnp.broadcast_to(rows[None], outs[1].shape)


def product(lefts, rights, width, columns, held=None, sums=None, copies=0):
    operands, at = [], {}

    def place(part):
        array, start = part
        if id(array) not in at:
            at[id(array)] = len(operands)
            operands.append(array)
        return at[id(array)], start

    user_count, sources = len(lefts), len(lefts[0])
    left_places = [[place(part) for part in slot] for slot in lefts]
    right_places = [[place(part) for part in slot] for slot in rights]
    tokens = sources * lefts[0][0][0].shape[0]
    aliases = {}
    if held is not None:
        aliases = {len(operands): 0}
        operands.append(held)
    if sums is not None:
        operands.append(sums)
    out_shape = [jax.ShapeDtypeStruct((user_count, width, columns), jnp.float32)]
    if copies:
        out_shape.append(jax.ShapeDtypeStruct((copies, 8, lanes), jnp.float32))
    tile = math.gcd(width, 2 * lanes)
    return pl.pallas_call(
        functools.partial(
            product_kernel, left_places, right_places, tile, held is not None, sums is not None, copies
        ),
        out_shape=out_shape,
        in_specs=[VMEM] * len(operands),
        out_specs=[VMEM] * len(out_shape),
        input_output_aliases=aliases,
        compiler_params=pltpu.CompilerParams(vmem_limit_bytes=8 * 2**20),
        cost_estimate=pl.CostEstimate(
            flops=2 * user_count * tokens * columns * width,
            bytes_accessed=2 * user_count * tokens * (width + columns),
            transcendentals=0,
        ),
        name="product_and_squares",
    )(*operands)


def combine_kernel(user_count, clip_bound, scaling, starts, user_ref, sums_ref, *refs):
    out_ref, factor_ref = refs[-2:]

    @pl.when(pl.program_id(0) == 0)
    def _():
        per_user = sums_ref.shape[0] // user_count
        by_source = [
            jnp.sum(sums_ref[j * per_user : (j + 1) * per_user], axis=0) for j in range(user_count)
        ]
        factors = []
        for u in range(user_count):
            row = sum(by_source[j][j ^ u : (j ^ u) + 1, :] for j in range(user_count))
            norm_sq = jnp.sum(row, axis=1, keepdims=True)
            factors.append(jnp.minimum(1.0, clip_bound / jnp.sqrt(norm_sq + epsilon)) * scaling)
        for slot in range(user_count):
            user = user_ref[0] ^ slot
            factor = sum(jnp.where(user == u, factors[u], 0.0) for u in range(user_count))
            factor_ref[slot : slot + 1, :] = jnp.broadcast_to(factor, (1, lanes))

    by_slot = [factor_ref[slot : slot + 1, 0:1] for slot in range(user_count)]
    tile = out_ref.shape[0]
    row = pl.program_id(0) * tile
    for ref, start in zip(refs, starts):

        @pl.when((row >= start) & (row < start + ref.shape[1]))
        def _(ref=ref, start=start):
            at = pl.ds(pl.multiple_of(row - start, tile), tile)
            result = by_slot[0] * ref[0, at, :]
            for slot in range(1, user_count):
                result += by_slot[slot] * ref[slot, at, :]
            out_ref[...] = result


def combine(user, sums, gradients, clip_bound, scaling):
    user_count, _, columns = gradients[0].shape
    heights = [gradient.shape[1] for gradient in gradients]
    starts = [sum(heights[:i]) for i in range(len(heights))]
    rows = sum(heights)
    tile = math.gcd(256, *heights)
    return pl.pallas_call(
        functools.partial(combine_kernel, user_count, clip_bound, scaling, starts),
        grid=(rows // tile,),
        out_shape=jax.ShapeDtypeStruct((rows, columns), jnp.float32),
        in_specs=[SMEM] + [VMEM] * (1 + len(gradients)),
        out_specs=pl.BlockSpec((tile, columns), lambda i: (i, 0)),
        scratch_shapes=[pltpu.VMEM((8, lanes), jnp.float32)],
        compiler_params=pltpu.CompilerParams(vmem_limit_bytes=8 * 2**20),
        name="weighted_sum",
    )(user, sums, *gradients)


def body(hidden, cotangent, lengths):
    tok_count = lax.axis_size("tok")
    user_count = lax.axis_size("user")
    tok_rows = hidden.shape[1]
    hidden_width = hidden.shape[2]
    model_width = cotangent.shape[2]
    capacity = tok_rows * tok_count
    own_width = hidden_width // tok_count
    columns = model_width // user_count
    clip_bound = math.sqrt(8.0 * hidden_width * model_width * capacity)
    scaling = math.sqrt(hidden_width * model_width) / (user_count * clip_bound)
    user = lax.axis_index("user").astype(jnp.int32).reshape(1)
    tok = lax.axis_index("tok").astype(jnp.int32).reshape(1)
    valid = lengths - tok * tok_rows
    half = tok_count // 2
    across, core = user_count // 2, user_count // 4
    slots = range(user_count)
    cut = round(own_width // lanes * first_part) * lanes
    pieces = [(0, cut), (cut, own_width - cut)]

    cots = {}
    lefts = {}
    ready = []
    tick = []

    sizes = [0]

    def send(axis, distance, parts, after=()):
        message = join(parts, [*tick, *after])
        sizes.append(2 * message.size)
        tick[:] = [message]
        return message, exchange(message, axis, distance)

    def cot_parts(d):
        return [(*cots[d][s], columns) for s in slots]

    def cots_at(array, start):
        return [(array, start + s * columns) for s in slots]

    masked = mask(valid, user, cotangent, user_count)
    by_slot = [masked[0]] + [exchange(masked[s], "user", s) for s in range(1, user_count)]
    outgoing = pack(tok, hidden, list(range(tok_count)), own_width, [])
    ready += [(0, i, outgoing[0], start) for i, (start, _) in enumerate(pieces)]

    far_steps = [[(half, None), ("cots", None)], [None, None]]
    far = [(d, None) for d in range(half + 1, tok_count - 1)] + [(tok_count - 1, 0), (tok_count - 1, 1)]
    for at, block in enumerate(far):
        far_steps.append([block, None] if at % 2 == 0 else [None, block])
    far_steps += [[("wait", None), None], [None, ("wait", None)]]
    near = list(range(1, half))
    near_steps = [near[:2]] + [[d] for d in near[2:]]
    relayed = set()

    def rides(d):
        return d & (d - 1) == 0 and d < half // 2

    def bits_below(d):
        if d == 0:
            return [half // 2]
        return [1 << i for i in range((d & -d).bit_length() - 1)]


    lanes_before = [None, None]
    near_before, relay_before, cross_before, core_before = [], [], None, None
    crossed = []
    gradients = [None, None]
    done = set()

    def finish_core():
        nonlocal core_before
        if core_before is not None:
            units, both = core_before
            core_before = None
            to = 0
            for blocks, own, other in units:
                total = sum(pieces[i][1] for _, i, _, _ in blocks)
                at = 0
                for d, i, _, _ in blocks:
                    lefts[d, i] = {
                        0: (own, at),
                        across: (other, at),
                        core: (both, to + at),
                        across ^ core: (both, to + total + at),
                    }
                    at += pieces[i][1]
                to += 2 * total

    def finish_relays(step):
        arrived = []
        for entry in list(relay_before):
            due, bit, sources, array = entry
            if due <= step:
                relay_before.remove(entry)
                arrived.append(array)
                for at, d in enumerate(sources):
                    cots[d + bit] = cots_at(array, at * model_width)
        return arrived

    def add_products(i):
        width = pieces[i][1]
        here = [d for d in range(tok_count) if d in cots and (d, i) in lefts and (d, i) not in done]
        if not here:
            return
        done.update((d, i) for d in here)
        full = all((d, i) in done for d in range(tok_count))
        out = product(
            [[lefts[d, i][s] for d in here] for s in slots],
            [[cots[d][s] for d in here] for s in slots],
            width,
            columns,
            held=gradients[i][0] if gradients[i] else None,
            sums=gradients[0][1] if full and i == 1 else None,
            copies=0 if not full else tok_count * user_count if i == 1 else 1,
        )
        gradients[i] = out
        tick.append(out[0])

    for step in range(len(far_steps) + 1):
        flying = 0
        now = far_steps[step] if step < len(far_steps) else [None, None]
        for lane in (0, 1):
            if lane == 1 and now[1] == ("cots", None):
                continue
            if now[lane] is not None:
                after = []
                if lanes_before[lane] is not None:
                    (d, i), array = lanes_before[lane]
                    lanes_before[lane] = None
                    after.append(array)
                    if d == "cots":
                        cots[half] = cots_at(array, 0)
                    else:
                        first = pieces[i][0] if i is not None else 0
                        ready += [
                            (d, j, array, at - first) for j, (at, _) in enumerate(pieces) if i is None or i == j
                        ]
                d, i = now[lane]
                if d != "wait":
                    first, width = pieces[i] if i is not None else (0, own_width)
                    array = send("tok", d, [(outgoing[d], first, width)], after)[1]
                    lanes_before[lane] = (now[lane], array)
            flying += lanes_before[lane] is not None
        for d, array in near_before:
            ready += [(d, i, array, first) for i, (first, _) in enumerate(pieces)]
            if rides(d):
                cots[d] = cots_at(array, own_width)
        near_before.clear()
        arrivals = finish_relays(step)
        bit = half // 2
        while bit:
            sources = [d for d in sorted(cots) if bit in bits_below(d) and d + bit not in relayed]
            if sources and flying < 4 and step > 0:
                relayed.update(d + bit for d in sources)
                parts = [part for d in sources for part in cot_parts(d)]
                relay_before.append((step + 2, bit, sources, send("tok", bit, parts)[1]))
                flying += 1
            bit //= 2
        if cross_before is not None:
            crossed.append(cross_before)
        earlier = [cross_before[2]] if cross_before is not None else []
        cross_before = None
        if ready:
            blocks = []
            while ready and sum(pieces[i][1] for _, i, _, _ in blocks) < 2 * own_width:
                blocks.append(ready.pop(0))
            parts = [(array, first, pieces[i][1]) for _, i, array, first in blocks]
            own, other = send("user", across, parts, earlier)
            cross_before = (blocks, own, other)
            flying += 1
        if step == 0:
            cots[0] = [(block, 0) for block in by_slot]
            cots[0] = cots_at(join(cot_parts(0), tick), 0)
            lanes_before[1] = (("cots", None), send("tok", half, cot_parts(0))[1])
            flying += 1
        if step < len(near_steps):
            for d in near_steps[step]:
                parts = [(outgoing[d], 0, own_width)]
                if rides(d):
                    parts += cot_parts(0)
                near_before.append((d, send("tok", d, parts)[1]))
                flying += 1
        before = [core_before[1]] if core_before else []
        finish_core()
        if crossed and (flying < 5 or step >= len(far_steps) - 3):
            parts = []
            for blocks, own, other in crossed:
                total = sum(pieces[i][1] for _, i, _, _ in blocks)
                parts += [(own, 0, total), (other, 0, total)]
            core_before = (list(crossed), send("user", core, parts, before)[1])
            crossed.clear()
            flying += 1
        if step < len(far_steps):
            tick[:] = [hold(tick[0], arrivals, max(sizes))]
            sizes[:] = [0]
        if step == len(far_steps) - 3:
            add_products(0)
        elif step == len(far_steps) - 2:
            add_products(1)
        elif step == len(far_steps) - 1:
            finish_core()
            add_products(0)
    finish_core()
    add_products(0)
    add_products(1)
    sums = lax.all_to_all(gradients[1][1], ("user", "tok"), split_axis=0, concat_axis=0, tiled=True)
    return combine(user, sums, [g[0] for g in gradients], clip_bound, scaling)


def solution(mesh):
    return jax.shard_map(
        body,
        mesh=mesh,
        in_specs=(P("user", "tok", None), P("user", "tok", None), P("user")),
        out_specs=P("tok", "user"),
        check_vma=False,
    )
```

```python
import functools
import math

import jax
import jax.numpy as jnp
from jax import lax
from jax.experimental import pallas as pl
from jax.experimental.pallas import tpu as pltpu
from jax.sharding import PartitionSpec as P

epsilon = 1e-06
lanes = 128
first_part = 0.625
dear = 24 * 10**10
dear_per_byte = 2 * 10**5
ANY = pl.BlockSpec(memory_space=pl.ANY)
SMEM = pl.BlockSpec(memory_space=pltpu.SMEM)
VMEM = pl.BlockSpec(memory_space=pltpu.VMEM)
HBM = pl.BlockSpec(memory_space=pltpu.HBM)


def exchange(block, axis, distance):
    size = lax.axis_size(axis)
    return lax.ppermute(block, axis, [(i, i ^ distance) for i in range(size)])


def pack_kernel(distances, tok_ref, hidden_ref, *refs):
    out_refs, sems = refs[-1 - len(distances) : -1], refs[-1]
    width = out_refs[0].shape[1]
    copies = []
    for at, distance in enumerate(distances):
        start = pl.multiple_of((tok_ref[0] ^ distance) * width, lanes)
        copies.append(
            pltpu.make_async_copy(
                hidden_ref.at[0, :, pl.ds(start, width)], out_refs[at], sems.at[at]
            )
        )
    for copy in copies:
        copy.start()
    for copy in copies:
        copy.wait()


def pack(tok, hidden, distances, width, after):
    rows = hidden.shape[1]
    count = len(distances)
    return pl.pallas_call(
        functools.partial(pack_kernel, distances),
        out_shape=[jax.ShapeDtypeStruct((rows, width), hidden.dtype)] * count,
        in_specs=[SMEM, HBM] + [ANY] * len(after),
        out_specs=[VMEM] * count,
        scratch_shapes=[pltpu.SemaphoreType.DMA((count,))],
        compiler_params=pltpu.CompilerParams(vmem_limit_bytes=2**20),
        cost_estimate=pl.CostEstimate(
            flops=0, bytes_accessed=4 * count * rows * width, transcendentals=0
        ),
        name="pack_columns",
    )(tok, hidden, *after)


def join_kernel(parts, *refs):
    out_ref = refs[-1]
    to = 0
    for at, start, width in parts:
        out_ref[:, to : to + width] = refs[at][:, start : start + width]
        to += width


def join(parts, after):
    arrays, places = [], []
    for array, start, width in parts:
        at = [i for i, other in enumerate(arrays) if other is array]
        if not at:
            arrays.append(array)
        places.append((at[0] if at else len(arrays) - 1, start, width))
    after = [array for array in after if not any(array is other for other in arrays)]
    rows = arrays[0].shape[0]
    total = sum(width for _, _, width in parts)
    return pl.pallas_call(
        functools.partial(join_kernel, places),
        out_shape=jax.ShapeDtypeStruct((rows, total), arrays[0].dtype),
        in_specs=[VMEM] * len(arrays) + [ANY] * len(after),
        out_specs=VMEM,
        compiler_params=pltpu.CompilerParams(vmem_limit_bytes=max(2**20, 8 * rows * total - 2**24)),
        cost_estimate=pl.CostEstimate(flops=0, bytes_accessed=4 * rows * total, transcendentals=0),
        name="join_columns",
    )(*arrays, *after)


def hold_kernel(*refs):
    out_ref = refs[-1]
    out_ref[...] = jnp.zeros_like(out_ref)


def hold(message, after, size):
    return pl.pallas_call(
        hold_kernel,
        out_shape=jax.ShapeDtypeStruct((16, lanes), message.dtype),
        in_specs=[ANY] * (1 + len(after)),
        out_specs=VMEM,
        cost_estimate=pl.CostEstimate(flops=max(dear, dear_per_byte * size) // lax.axis_size("tok"), bytes_accessed=0, transcendentals=0),
        compiler_params=pltpu.CompilerParams(vmem_limit_bytes=2**20),
        name="hold",
    )(message, *after)


def mask_kernel(valid_ref, user_ref, cot_ref, *out_refs):
    rows, width = out_refs[0].shape
    keep = lax.broadcasted_iota(jnp.int32, (rows, width), 0) < valid_ref[0]
    for slot, out_ref in enumerate(out_refs):
        column = pl.multiple_of((user_ref[0] ^ slot) * width, lanes)
        block = cot_ref[0, :, pl.ds(column, width)]
        out_ref[...] = jnp.where(keep, block, jnp.zeros_like(block))


def mask(valid, user, cotangent, user_count):
    _, rows, total = cotangent.shape
    return pl.pallas_call(
        mask_kernel,
        out_shape=[jax.ShapeDtypeStruct((rows, total // user_count), cotangent.dtype)] * user_count,
        in_specs=[SMEM, SMEM, VMEM],
        out_specs=[VMEM] * user_count,
        compiler_params=pltpu.CompilerParams(vmem_limit_bytes=2 * 2**20),
        name="mask_cotangent",
    )(valid, user, cotangent)


def product_kernel(lefts, rights, tile, has_held, has_sums, copies, *refs):
    outs = refs[-2:] if copies else refs[-1:]
    inputs = list(refs[: -len(outs)])
    sums_in = inputs.pop() if has_sums else None
    held_ref = inputs.pop() if has_held else None
    product_ref = outs[0]
    user_count, width, columns = product_ref.shape
    squares = []
    for slot in range(user_count):
        right = jnp.concatenate(
            [refs[at][:, start : start + columns] for at, start in rights[slot]], axis=0
        )

        def step(i, total, slot=slot, right=right):
            rows = pl.ds(pl.multiple_of(i * tile, tile), tile)
            left = jnp.concatenate(
                [
                    refs[at][:, pl.ds(pl.multiple_of(start + i * tile, lanes), tile)]
                    for at, start in lefts[slot]
                ],
                axis=0,
            )
            value = lax.dot_general(
                left, right, (((0,), (0,)), ((), ())), preferred_element_type=jnp.float32
            )
            if has_held:
                value += held_ref[slot, rows, :]
            product_ref[slot, rows, :] = value
            if copies:
                row = jnp.sum(value * value, axis=0, keepdims=True)
                for start in range(0, columns, lanes):
                    total += row[:, start : start + lanes]
            return total

        squares.append(lax.fori_loop(0, width // tile, step, jnp.zeros((1, lanes), jnp.float32)))
    if copies:
        rows = jnp.concatenate(squares + [jnp.zeros((8 - user_count, lanes), jnp.float32)], axis=0)
        if has_sums:
            rows += sums_in[0]
        outs[1][...] = jnp.broadcast_to(rows[None], outs[1].shape)


def product(lefts, rights, width, columns, held=None, sums=None, copies=0):
    operands, at = [], {}

    def place(part):
        array, start = part
        if id(array) not in at:
            at[id(array)] = len(operands)
            operands.append(array)
        return at[id(array)], start

    user_count, sources = len(lefts), len(lefts[0])
    left_places = [[place(part) for part in slot] for slot in lefts]
    right_places = [[place(part) for part in slot] for slot in rights]
    tokens = sources * lefts[0][0][0].shape[0]
    aliases = {}
    if held is not None:
        aliases = {len(operands): 0}
        operands.append(held)
    if sums is not None:
        operands.append(sums)
    out_shape = [jax.ShapeDtypeStruct((user_count, width, columns), jnp.float32)]
    if copies:
        out_shape.append(jax.ShapeDtypeStruct((copies, 8, lanes), jnp.float32))
    tile = math.gcd(width, 2 * lanes)
    return pl.pallas_call(
        functools.partial(
            product_kernel, left_places, right_places, tile, held is not None, sums is not None, copies
        ),
        out_shape=out_shape,
        in_specs=[VMEM] * len(operands),
        out_specs=[VMEM] * len(out_shape),
        input_output_aliases=aliases,
        compiler_params=pltpu.CompilerParams(vmem_limit_bytes=8 * 2**20),
        cost_estimate=pl.CostEstimate(
            flops=2 * user_count * tokens * columns * width,
            bytes_accessed=2 * user_count * tokens * (width + columns),
            transcendentals=0,
        ),
        name="product_and_squares",
    )(*operands)


def combine_kernel(user_count, clip_bound, scaling, starts, user_ref, sums_ref, *refs):
    out_ref, factor_ref = refs[-2:]

    @pl.when(pl.program_id(0) == 0)
    def _():
        per_user = sums_ref.shape[0] // user_count
        by_source = [
            jnp.sum(sums_ref[j * per_user : (j + 1) * per_user], axis=0) for j in range(user_count)
        ]
        factors = []
        for u in range(user_count):
            row = sum(by_source[j][j ^ u : (j ^ u) + 1, :] for j in range(user_count))
            norm_sq = jnp.sum(row, axis=1, keepdims=True)
            factors.append(jnp.minimum(1.0, clip_bound / jnp.sqrt(norm_sq + epsilon)) * scaling)
        for slot in range(user_count):
            user = user_ref[0] ^ slot
            factor = sum(jnp.where(user == u, factors[u], 0.0) for u in range(user_count))
            factor_ref[slot : slot + 1, :] = jnp.broadcast_to(factor, (1, lanes))

    by_slot = [factor_ref[slot : slot + 1, 0:1] for slot in range(user_count)]
    tile = out_ref.shape[0]
    row = pl.program_id(0) * tile
    for ref, start in zip(refs, starts):

        @pl.when((row >= start) & (row < start + ref.shape[1]))
        def _(ref=ref, start=start):
            at = pl.ds(pl.multiple_of(row - start, tile), tile)
            result = by_slot[0] * ref[0, at, :]
            for slot in range(1, user_count):
                result += by_slot[slot] * ref[slot, at, :]
            out_ref[...] = result


def combine(user, sums, gradients, clip_bound, scaling):
    user_count, _, columns = gradients[0].shape
    heights = [gradient.shape[1] for gradient in gradients]
    starts = [sum(heights[:i]) for i in range(len(heights))]
    rows = sum(heights)
    tile = math.gcd(256, *heights)
    return pl.pallas_call(
        functools.partial(combine_kernel, user_count, clip_bound, scaling, starts),
        grid=(rows // tile,),
        out_shape=jax.ShapeDtypeStruct((rows, columns), jnp.float32),
        in_specs=[SMEM] + [VMEM] * (1 + len(gradients)),
        out_specs=pl.BlockSpec((tile, columns), lambda i: (i, 0)),
        scratch_shapes=[pltpu.VMEM((8, lanes), jnp.float32)],
        compiler_params=pltpu.CompilerParams(vmem_limit_bytes=8 * 2**20),
        name="weighted_sum",
    )(user, sums, *gradients)


def body(hidden, cotangent, lengths):
    tok_count = lax.axis_size("tok")
    user_count = lax.axis_size("user")
    tok_rows = hidden.shape[1]
    hidden_width = hidden.shape[2]
    model_width = cotangent.shape[2]
    capacity = tok_rows * tok_count
    own_width = hidden_width // tok_count
    columns = model_width // user_count
    clip_bound = math.sqrt(8.0 * hidden_width * model_width * capacity)
    scaling = math.sqrt(hidden_width * model_width) / (user_count * clip_bound)
    user = lax.axis_index("user").astype(jnp.int32).reshape(1)
    tok = lax.axis_index("tok").astype(jnp.int32).reshape(1)
    valid = lengths - tok * tok_rows
    half = tok_count // 2
    across, core = user_count // 2, user_count // 4
    slots = range(user_count)
    cut = round(own_width // lanes * first_part) * lanes
    pieces = [(0, cut), (cut, own_width - cut)]

    cots = {}
    lefts = {}
    ready = []
    tick = []

    sizes = [0]

    def send(axis, distance, parts, after=()):
        message = join(parts, [*tick, *after])
        sizes.append(2 * message.size)
        tick[:] = [message]
        return message, exchange(message, axis, distance)

    def cot_parts(d):
        return [(*cots[d][s], columns) for s in slots]

    def cots_at(array, start):
        return [(array, start + s * columns) for s in slots]

    masked = mask(valid, user, cotangent, user_count)
    by_slot = [masked[0]] + [exchange(masked[s], "user", s) for s in range(1, user_count)]
    outgoing = pack(tok, hidden, list(range(tok_count)), own_width, [])
    ready += [(0, i, outgoing[0], start) for i, (start, _) in enumerate(pieces)]

    far_steps = [[(half, None), ("cots", None)], [None, None]]
    far = [(d, None) for d in range(half + 1, tok_count - 1)] + [(tok_count - 1, 0), (tok_count - 1, 1)]
    for at, block in enumerate(far):
        far_steps.append([block, None] if at % 2 == 0 else [None, block])
    far_steps += [[("wait", None), None], [None, ("wait", None)]]
    near = list(range(1, half))
    near_steps = [near[:2], [], [], []] + [[d] for d in near[2:]]
    relayed = set()

    def rides(d):
        return d & (d - 1) == 0 and d < half // 2

    def bits_below(d):
        if d == 0:
            return [half // 2]
        return [1 << i for i in range((d & -d).bit_length() - 1)]


    lanes_before = [None, None]
    near_before, relay_before, cross_before, core_before = [], [], None, None
    crossed = []
    gradients = [None, None]
    done = set()

    def finish_core():
        nonlocal core_before
        if core_before is not None:
            units, both = core_before
            core_before = None
            to = 0
            for blocks, own, other in units:
                total = sum(pieces[i][1] for _, i, _, _ in blocks)
                at = 0
                for d, i, _, _ in blocks:
                    lefts[d, i] = {
                        0: (own, at),
                        across: (other, at),
                        core: (both, to + at),
                        across ^ core: (both, to + total + at),
                    }
                    at += pieces[i][1]
                to += 2 * total

    def finish_relays(step):
        arrived = []
        for entry in list(relay_before):
            due, bit, sources, array = entry
            if due <= step:
                relay_before.remove(entry)
                arrived.append(array)
                for at, d in enumerate(sources):
                    cots[d + bit] = cots_at(array, at * model_width)
        return arrived

    def add_products(i):
        width = pieces[i][1]
        here = [d for d in range(tok_count) if d in cots and (d, i) in lefts and (d, i) not in done]
        if not here:
            return
        done.update((d, i) for d in here)
        full = all((d, i) in done for d in range(tok_count))
        out = product(
            [[lefts[d, i][s] for d in here] for s in slots],
            [[cots[d][s] for d in here] for s in slots],
            width,
            columns,
            held=gradients[i][0] if gradients[i] else None,
            sums=gradients[0][1] if full and i == 1 else None,
            copies=0 if not full else tok_count * user_count if i == 1 else 1,
        )
        gradients[i] = out
        tick.append(out[0])

    for step in range(len(far_steps) + 1):
        flying = 0
        now = far_steps[step] if step < len(far_steps) else [None, None]
        for lane in (0, 1):
            if lane == 1 and now[1] == ("cots", None):
                continue
            if now[lane] is not None:
                after = []
                if lanes_before[lane] is not None:
                    (d, i), array = lanes_before[lane]
                    lanes_before[lane] = None
                    after.append(array)
                    if d == "cots":
                        cots[half] = cots_at(array, 0)
                    else:
                        first = pieces[i][0] if i is not None else 0
                        ready += [
                            (d, j, array, at - first) for j, (at, _) in enumerate(pieces) if i is None or i == j
                        ]
                d, i = now[lane]
                if d != "wait":
                    first, width = pieces[i] if i is not None else (0, own_width)
                    array = send("tok", d, [(outgoing[d], first, width)], after)[1]
                    lanes_before[lane] = (now[lane], array)
            flying += lanes_before[lane] is not None
        for d, array in near_before:
            ready += [(d, i, array, first) for i, (first, _) in enumerate(pieces)]
            if rides(d):
                cots[d] = cots_at(array, own_width)
        near_before.clear()
        arrivals = finish_relays(step)
        if cross_before is not None:
            crossed.append(cross_before)
        earlier = [cross_before[2]] if cross_before is not None else []
        cross_before = None
        bit = half // 2
        while bit:
            sources = [d for d in sorted(cots) if bit in bits_below(d) and d + bit not in relayed]
            if sources and flying < 4 and step > 0:
                relayed.update(d + bit for d in sources)
                parts = [part for d in sources for part in cot_parts(d)]
                relay_before.append((step + 1, bit, sources, send("tok", bit, parts, earlier)[1]))
                flying += 1
            bit //= 2
        if ready:
            blocks = []
            while ready and sum(pieces[i][1] for _, i, _, _ in blocks) < 2 * own_width:
                blocks.append(ready.pop(0))
            parts = [(array, first, pieces[i][1]) for _, i, array, first in blocks]
            own, other = send("user", across, parts, earlier)
            cross_before = (blocks, own, other)
            flying += 1
        if step == 0:
            cots[0] = [(block, 0) for block in by_slot]
            cots[0] = cots_at(join(cot_parts(0), tick), 0)
            lanes_before[1] = (("cots", None), send("tok", half, cot_parts(0))[1])
            flying += 1
        if step < len(near_steps):
            for d in near_steps[step]:
                parts = [(outgoing[d], 0, own_width)]
                if rides(d):
                    parts += cot_parts(0)
                near_before.append((d, send("tok", d, parts)[1]))
                flying += 1
        before = [core_before[1]] if core_before else []
        finish_core()
        if crossed and (flying < 5 or step >= len(far_steps) - 3):
            parts = []
            for blocks, own, other in crossed:
                total = sum(pieces[i][1] for _, i, _, _ in blocks)
                parts += [(own, 0, total), (other, 0, total)]
            core_before = (list(crossed), send("user", core, parts, before)[1])
            crossed.clear()
            flying += 1
        if step < len(far_steps):
            tick[:] = [hold(tick[0], arrivals, max(sizes))]
            sizes[:] = [0]
        if step == len(far_steps) - 3:
            add_products(0)
        elif step == len(far_steps) - 2:
            add_products(1)
        elif step == len(far_steps) - 1:
            finish_core()
            add_products(0)
    finish_core()
    add_products(0)
    add_products(1)
    sums = lax.all_to_all(gradients[1][1], ("user", "tok"), split_axis=0, concat_axis=0, tiled=True)
    return combine(user, sums, [g[0] for g in gradients], clip_bound, scaling)


def solution(mesh):
    return jax.shard_map(
        body,
        mesh=mesh,
        in_specs=(P("user", "tok", None), P("user", "tok", None), P("user")),
        out_specs=P("tok", "user"),
        check_vma=False,
    )
```

```python
import functools
import math

import jax
import jax.numpy as jnp
from jax import lax
from jax.experimental import pallas as pl
from jax.experimental.pallas import tpu as pltpu
from jax.sharding import PartitionSpec as P

epsilon = 1e-06
lanes = 128
first_part = 0.625
dear = 24 * 10**10
dear_per_byte = 2 * 10**5
ANY = pl.BlockSpec(memory_space=pl.ANY)
SMEM = pl.BlockSpec(memory_space=pltpu.SMEM)
VMEM = pl.BlockSpec(memory_space=pltpu.VMEM)
HBM = pl.BlockSpec(memory_space=pltpu.HBM)


def exchange(block, axis, distance):
    size = lax.axis_size(axis)
    return lax.ppermute(block, axis, [(i, i ^ distance) for i in range(size)])


def pack_kernel(distances, tok_ref, hidden_ref, *refs):
    out_refs, sems = refs[-1 - len(distances) : -1], refs[-1]
    width = out_refs[0].shape[1]
    copies = []
    for at, distance in enumerate(distances):
        start = pl.multiple_of((tok_ref[0] ^ distance) * width, lanes)
        copies.append(
            pltpu.make_async_copy(
                hidden_ref.at[0, :, pl.ds(start, width)], out_refs[at], sems.at[at]
            )
        )
    for copy in copies:
        copy.start()
    for copy in copies:
        copy.wait()


def pack(tok, hidden, distances, width, after):
    rows = hidden.shape[1]
    count = len(distances)
    return pl.pallas_call(
        functools.partial(pack_kernel, distances),
        out_shape=[jax.ShapeDtypeStruct((rows, width), hidden.dtype)] * count,
        in_specs=[SMEM, HBM] + [ANY] * len(after),
        out_specs=[VMEM] * count,
        scratch_shapes=[pltpu.SemaphoreType.DMA((count,))],
        compiler_params=pltpu.CompilerParams(vmem_limit_bytes=2**20),
        cost_estimate=pl.CostEstimate(
            flops=0, bytes_accessed=4 * count * rows * width, transcendentals=0
        ),
        name="pack_columns",
    )(tok, hidden, *after)


def join_kernel(parts, *refs):
    out_ref = refs[-1]
    to = 0
    for at, start, width in parts:
        out_ref[:, to : to + width] = refs[at][:, start : start + width]
        to += width


def join(parts, after):
    arrays, places = [], []
    for array, start, width in parts:
        at = [i for i, other in enumerate(arrays) if other is array]
        if not at:
            arrays.append(array)
        places.append((at[0] if at else len(arrays) - 1, start, width))
    after = [array for array in after if not any(array is other for other in arrays)]
    rows = arrays[0].shape[0]
    total = sum(width for _, _, width in parts)
    return pl.pallas_call(
        functools.partial(join_kernel, places),
        out_shape=jax.ShapeDtypeStruct((rows, total), arrays[0].dtype),
        in_specs=[VMEM] * len(arrays) + [ANY] * len(after),
        out_specs=VMEM,
        compiler_params=pltpu.CompilerParams(vmem_limit_bytes=max(2**20, 8 * rows * total - 2**24)),
        cost_estimate=pl.CostEstimate(flops=0, bytes_accessed=4 * rows * total, transcendentals=0),
        name="join_columns",
    )(*arrays, *after)


def hold_kernel(*refs):
    out_ref = refs[-1]
    out_ref[...] = jnp.zeros_like(out_ref)


def hold(message, after, size):
    return pl.pallas_call(
        hold_kernel,
        out_shape=jax.ShapeDtypeStruct((16, lanes), message.dtype),
        in_specs=[ANY] * (1 + len(after)),
        out_specs=VMEM,
        cost_estimate=pl.CostEstimate(flops=max(dear, dear_per_byte * size) // lax.axis_size("tok"), bytes_accessed=0, transcendentals=0),
        compiler_params=pltpu.CompilerParams(vmem_limit_bytes=2**20),
        name="hold",
    )(message, *after)


def mask_kernel(valid_ref, user_ref, cot_ref, *out_refs):
    rows, width = out_refs[0].shape
    keep = lax.broadcasted_iota(jnp.int32, (rows, width), 0) < valid_ref[0]
    for slot, out_ref in enumerate(out_refs):
        column = pl.multiple_of((user_ref[0] ^ slot) * width, lanes)
        block = cot_ref[0, :, pl.ds(column, width)]
        out_ref[...] = jnp.where(keep, block, jnp.zeros_like(block))


def mask(valid, user, cotangent, user_count):
    _, rows, total = cotangent.shape
    return pl.pallas_call(
        mask_kernel,
        out_shape=[jax.ShapeDtypeStruct((rows, total // user_count), cotangent.dtype)] * user_count,
        in_specs=[SMEM, SMEM, VMEM],
        out_specs=[VMEM] * user_count,
        compiler_params=pltpu.CompilerParams(vmem_limit_bytes=2 * 2**20),
        name="mask_cotangent",
    )(valid, user, cotangent)


def product_kernel(lefts, rights, tile, has_held, has_sums, copies, *refs):
    outs = refs[-2:] if copies else refs[-1:]
    inputs = list(refs[: -len(outs)])
    sums_in = inputs.pop() if has_sums else None
    held_ref = inputs.pop() if has_held else None
    product_ref = outs[0]
    user_count, width, columns = product_ref.shape
    squares = []
    for slot in range(user_count):
        right = jnp.concatenate(
            [refs[at][:, start : start + columns] for at, start in rights[slot]], axis=0
        )

        def step(i, total, slot=slot, right=right):
            rows = pl.ds(pl.multiple_of(i * tile, tile), tile)
            left = jnp.concatenate(
                [
                    refs[at][:, pl.ds(pl.multiple_of(start + i * tile, lanes), tile)]
                    for at, start in lefts[slot]
                ],
                axis=0,
            )
            value = lax.dot_general(
                left, right, (((0,), (0,)), ((), ())), preferred_element_type=jnp.float32
            )
            if has_held:
                value += held_ref[slot, rows, :]
            product_ref[slot, rows, :] = value
            if copies:
                row = jnp.sum(value * value, axis=0, keepdims=True)
                for start in range(0, columns, lanes):
                    total += row[:, start : start + lanes]
            return total

        squares.append(lax.fori_loop(0, width // tile, step, jnp.zeros((1, lanes), jnp.float32)))
    if copies:
        rows = jnp.concatenate(squares + [jnp.zeros((8 - user_count, lanes), jnp.float32)], axis=0)
        if has_sums:
            rows += sums_in[0]
        outs[1][...] = jnp.broadcast_to(rows[None], outs[1].shape)


def product(lefts, rights, width, columns, held=None, sums=None, copies=0):
    operands, at = [], {}

    def place(part):
        array, start = part
        if id(array) not in at:
            at[id(array)] = len(operands)
            operands.append(array)
        return at[id(array)], start

    user_count, sources = len(lefts), len(lefts[0])
    left_places = [[place(part) for part in slot] for slot in lefts]
    right_places = [[place(part) for part in slot] for slot in rights]
    tokens = sources * lefts[0][0][0].shape[0]
    aliases = {}
    if held is not None:
        aliases = {len(operands): 0}
        operands.append(held)
    if sums is not None:
        operands.append(sums)
    out_shape = [jax.ShapeDtypeStruct((user_count, width, columns), jnp.float32)]
    if copies:
        out_shape.append(jax.ShapeDtypeStruct((copies, 8, lanes), jnp.float32))
    tile = math.gcd(width, 2 * lanes)
    return pl.pallas_call(
        functools.partial(
            product_kernel, left_places, right_places, tile, held is not None, sums is not None, copies
        ),
        out_shape=out_shape,
        in_specs=[VMEM] * len(operands),
        out_specs=[VMEM] * len(out_shape),
        input_output_aliases=aliases,
        compiler_params=pltpu.CompilerParams(vmem_limit_bytes=8 * 2**20),
        cost_estimate=pl.CostEstimate(
            flops=2 * user_count * tokens * columns * width,
            bytes_accessed=2 * user_count * tokens * (width + columns),
            transcendentals=0,
        ),
        name="product_and_squares",
    )(*operands)


def combine_kernel(user_count, clip_bound, scaling, starts, user_ref, sums_ref, *refs):
    out_ref, factor_ref = refs[-2:]

    @pl.when(pl.program_id(0) == 0)
    def _():
        per_user = sums_ref.shape[0] // user_count
        by_source = [
            jnp.sum(sums_ref[j * per_user : (j + 1) * per_user], axis=0) for j in range(user_count)
        ]
        factors = []
        for u in range(user_count):
            row = sum(by_source[j][j ^ u : (j ^ u) + 1, :] for j in range(user_count))
            norm_sq = jnp.sum(row, axis=1, keepdims=True)
            factors.append(jnp.minimum(1.0, clip_bound / jnp.sqrt(norm_sq + epsilon)) * scaling)
        for slot in range(user_count):
            user = user_ref[0] ^ slot
            factor = sum(jnp.where(user == u, factors[u], 0.0) for u in range(user_count))
            factor_ref[slot : slot + 1, :] = jnp.broadcast_to(factor, (1, lanes))

    by_slot = [factor_ref[slot : slot + 1, 0:1] for slot in range(user_count)]
    tile = out_ref.shape[0]
    row = pl.program_id(0) * tile
    for ref, start in zip(refs, starts):

        @pl.when((row >= start) & (row < start + ref.shape[1]))
        def _(ref=ref, start=start):
            at = pl.ds(pl.multiple_of(row - start, tile), tile)
            result = by_slot[0] * ref[0, at, :]
            for slot in range(1, user_count):
                result += by_slot[slot] * ref[slot, at, :]
            out_ref[...] = result


def combine(user, sums, gradients, clip_bound, scaling):
    user_count, _, columns = gradients[0].shape
    heights = [gradient.shape[1] for gradient in gradients]
    starts = [sum(heights[:i]) for i in range(len(heights))]
    rows = sum(heights)
    tile = math.gcd(256, *heights)
    return pl.pallas_call(
        functools.partial(combine_kernel, user_count, clip_bound, scaling, starts),
        grid=(rows // tile,),
        out_shape=jax.ShapeDtypeStruct((rows, columns), jnp.float32),
        in_specs=[SMEM] + [VMEM] * (1 + len(gradients)),
        out_specs=pl.BlockSpec((tile, columns), lambda i: (i, 0)),
        scratch_shapes=[pltpu.VMEM((8, lanes), jnp.float32)],
        compiler_params=pltpu.CompilerParams(vmem_limit_bytes=8 * 2**20),
        name="weighted_sum",
    )(user, sums, *gradients)


def body(hidden, cotangent, lengths):
    tok_count = lax.axis_size("tok")
    user_count = lax.axis_size("user")
    tok_rows = hidden.shape[1]
    hidden_width = hidden.shape[2]
    model_width = cotangent.shape[2]
    capacity = tok_rows * tok_count
    own_width = hidden_width // tok_count
    columns = model_width // user_count
    clip_bound = math.sqrt(8.0 * hidden_width * model_width * capacity)
    scaling = math.sqrt(hidden_width * model_width) / (user_count * clip_bound)
    user = lax.axis_index("user").astype(jnp.int32).reshape(1)
    tok = lax.axis_index("tok").astype(jnp.int32).reshape(1)
    valid = lengths - tok * tok_rows
    half = tok_count // 2
    across, core = user_count // 2, user_count // 4
    slots = range(user_count)
    cut = round(own_width // lanes * first_part) * lanes
    pieces = [(0, cut), (cut, own_width - cut)]

    cots = {}
    lefts = {}
    ready = []
    tick = []

    sizes = [0]

    def send(axis, distance, parts, after=()):
        message = join(parts, [*tick, *after])
        sizes.append(2 * message.size)
        tick[:] = [message]
        return message, exchange(message, axis, distance)

    def cot_parts(d):
        return [(*cots[d][s], columns) for s in slots]

    def cots_at(array, start):
        return [(array, start + s * columns) for s in slots]

    masked = mask(valid, user, cotangent, user_count)
    by_slot = [masked[0]] + [exchange(masked[s], "user", s) for s in range(1, user_count)]
    outgoing = pack(tok, hidden, list(range(tok_count)), own_width, [])
    ready += [(0, i, outgoing[0], start) for i, (start, _) in enumerate(pieces)]

    far_steps = [[(half, None), ("cots", None)], [None, None]]
    far = [(d, None) for d in range(half + 1, tok_count - 1)] + [(tok_count - 1, 0), (tok_count - 1, 1)]
    for at, block in enumerate(far):
        far_steps.append([block, None] if at % 2 == 0 else [None, block])
    far_steps += [[("wait", None), None], [None, ("wait", None)]]
    near = list(range(1, half))
    near_steps = [near[:2], []] + [[d] for d in near[2:]]
    relayed = set()

    def rides(d):
        return d & (d - 1) == 0 and d < half // 2

    def bits_below(d):
        if d == 0:
            return [half // 2]
        return [1 << i for i in range((d & -d).bit_length() - 1)]


    lanes_before = [None, None]
    near_before, relay_before, cross_before, core_before = [], [], None, None
    crossed = []
    gradients = [None, None]
    done = set()

    def finish_core():
        nonlocal core_before
        if core_before is not None:
            units, both = core_before
            core_before = None
            to = 0
            for blocks, own, other in units:
                total = sum(pieces[i][1] for _, i, _, _ in blocks)
                at = 0
                for d, i, _, _ in blocks:
                    lefts[d, i] = {
                        0: (own, at),
                        across: (other, at),
                        core: (both, to + at),
                        across ^ core: (both, to + total + at),
                    }
                    at += pieces[i][1]
                to += 2 * total

    def finish_relays(step):
        arrived = []
        for entry in list(relay_before):
            due, bit, sources, array = entry
            if due <= step:
                relay_before.remove(entry)
                arrived.append(array)
                for at, d in enumerate(sources):
                    cots[d + bit] = cots_at(array, at * model_width)
        return arrived

    def add_products(i):
        width = pieces[i][1]
        here = [d for d in range(tok_count) if d in cots and (d, i) in lefts and (d, i) not in done]
        if not here:
            return
        done.update((d, i) for d in here)
        full = all((d, i) in done for d in range(tok_count))
        out = product(
            [[lefts[d, i][s] for d in here] for s in slots],
            [[cots[d][s] for d in here] for s in slots],
            width,
            columns,
            held=gradients[i][0] if gradients[i] else None,
            sums=gradients[0][1] if full and i == 1 else None,
            copies=0 if not full else tok_count * user_count if i == 1 else 1,
        )
        gradients[i] = out
        tick.append(out[0])

    for step in range(len(far_steps) + 1):
        flying = 0
        now = far_steps[step] if step < len(far_steps) else [None, None]
        for lane in (0, 1):
            if lane == 1 and now[1] == ("cots", None):
                continue
            if now[lane] is not None:
                after = []
                if lanes_before[lane] is not None:
                    (d, i), array = lanes_before[lane]
                    lanes_before[lane] = None
                    after.append(array)
                    if d == "cots":
                        cots[half] = cots_at(array, 0)
                    else:
                        first = pieces[i][0] if i is not None else 0
                        ready += [
                            (d, j, array, at - first) for j, (at, _) in enumerate(pieces) if i is None or i == j
                        ]
                d, i = now[lane]
                if d != "wait":
                    first, width = pieces[i] if i is not None else (0, own_width)
                    array = send("tok", d, [(outgoing[d], first, width)], after)[1]
                    lanes_before[lane] = (now[lane], array)
            flying += lanes_before[lane] is not None
        for entry in list(near_before):
            due, d, array = entry
            if due > step:
                flying += 1
                continue
            near_before.remove(entry)
            ready += [(d, i, array, first) for i, (first, _) in enumerate(pieces)]
            if rides(d):
                cots[d] = cots_at(array, own_width)
        arrivals = finish_relays(step)
        if cross_before is not None:
            crossed.append(cross_before)
        earlier = [cross_before[2]] if cross_before is not None else []
        earlier += [core_before[1]] if core_before is not None else []
        cross_before = None
        if ready:
            blocks = []
            while ready and sum(pieces[i][1] for _, i, _, _ in blocks) < 2 * own_width:
                blocks.append(ready.pop(0))
            parts = [(array, first, pieces[i][1]) for _, i, array, first in blocks]
            own, other = send("user", across, parts, earlier)
            earlier = []
            cross_before = (blocks, own, other)
            flying += 1
        bit, sent = half // 2, False
        while bit:
            sources = [d for d in sorted(cots) if bit in bits_below(d) and d + bit not in relayed]
            if sources and flying < 5 and step > 0 and not sent:
                relayed.update(d + bit for d in sources)
                parts = [part for d in sources for part in cot_parts(d)]
                relay_before.append((step + (1 if step < 4 else 2), bit, sources, send("tok", bit, parts, earlier)[1]))
                earlier = []
                flying += 1
                sent = True
            bit //= 2
        if step == 0:
            cots[0] = [(block, 0) for block in by_slot]
            cots[0] = cots_at(join(cot_parts(0), tick), 0)
            lanes_before[1] = (("cots", None), send("tok", half, cot_parts(0))[1])
            flying += 1
        if step < len(near_steps):
            for d in near_steps[step]:
                parts = [(outgoing[d], 0, own_width)]
                if rides(d):
                    parts += cot_parts(0)
                near_before.append((step + (2 if step else 1), d, send("tok", d, parts)[1]))
                flying += 1
        before = [core_before[1]] if core_before else []
        finish_core()
        if crossed and (flying < 5 or step >= len(far_steps) - 3):
            parts = []
            for blocks, own, other in crossed:
                total = sum(pieces[i][1] for _, i, _, _ in blocks)
                parts += [(own, 0, total), (other, 0, total)]
            core_before = (list(crossed), send("user", core, parts, before)[1])
            crossed.clear()
            flying += 1
        if step < len(far_steps):
            tick[:] = [hold(tick[0], arrivals + earlier, max(sizes))]
            sizes[:] = [0]
        if step == len(far_steps) - 3:
            add_products(0)
        elif step == len(far_steps) - 2:
            add_products(1)
        elif step == len(far_steps) - 1:
            finish_core()
            add_products(0)
    finish_core()
    add_products(0)
    add_products(1)
    sums = lax.all_to_all(gradients[1][1], ("user", "tok"), split_axis=0, concat_axis=0, tiled=True)
    return combine(user, sums, [g[0] for g in gradients], clip_bound, scaling)


def solution(mesh):
    return jax.shard_map(
        body,
        mesh=mesh,
        in_specs=(P("user", "tok", None), P("user", "tok", None), P("user")),
        out_specs=P("tok", "user"),
        check_vma=False,
    )
```

```python
import functools
import math

import jax
import jax.numpy as jnp
from jax import lax
from jax.experimental import pallas as pl
from jax.experimental.pallas import tpu as pltpu
from jax.sharding import PartitionSpec as P

epsilon = 1e-06
lanes = 128
first_part = 0.625
dear = 24 * 10**10
dear_per_byte = 2 * 10**5
ANY = pl.BlockSpec(memory_space=pl.ANY)
SMEM = pl.BlockSpec(memory_space=pltpu.SMEM)
VMEM = pl.BlockSpec(memory_space=pltpu.VMEM)
HBM = pl.BlockSpec(memory_space=pltpu.HBM)


def exchange(block, axis, distance):
    size = lax.axis_size(axis)
    return lax.ppermute(block, axis, [(i, i ^ distance) for i in range(size)])


def pack_kernel(distances, tok_ref, hidden_ref, *refs):
    out_refs, sems = refs[-1 - len(distances) : -1], refs[-1]
    width = out_refs[0].shape[1]
    copies = []
    for at, distance in enumerate(distances):
        start = pl.multiple_of((tok_ref[0] ^ distance) * width, lanes)
        copies.append(
            pltpu.make_async_copy(
                hidden_ref.at[0, :, pl.ds(start, width)], out_refs[at], sems.at[at]
            )
        )
    for copy in copies:
        copy.start()
    for copy in copies:
        copy.wait()


def pack(tok, hidden, distances, width, after):
    rows = hidden.shape[1]
    count = len(distances)
    return pl.pallas_call(
        functools.partial(pack_kernel, distances),
        out_shape=[jax.ShapeDtypeStruct((rows, width), hidden.dtype)] * count,
        in_specs=[SMEM, HBM] + [ANY] * len(after),
        out_specs=[VMEM] * count,
        scratch_shapes=[pltpu.SemaphoreType.DMA((count,))],
        compiler_params=pltpu.CompilerParams(vmem_limit_bytes=2**20),
        cost_estimate=pl.CostEstimate(
            flops=0, bytes_accessed=4 * count * rows * width, transcendentals=0
        ),
        name="pack_columns",
    )(tok, hidden, *after)


def join_kernel(parts, *refs):
    out_ref = refs[-1]
    to = 0
    for at, start, width in parts:
        out_ref[:, to : to + width] = refs[at][:, start : start + width]
        to += width


def join(parts, after):
    arrays, places = [], []
    for array, start, width in parts:
        at = [i for i, other in enumerate(arrays) if other is array]
        if not at:
            arrays.append(array)
        places.append((at[0] if at else len(arrays) - 1, start, width))
    after = [array for array in after if not any(array is other for other in arrays)]
    rows = arrays[0].shape[0]
    total = sum(width for _, _, width in parts)
    return pl.pallas_call(
        functools.partial(join_kernel, places),
        out_shape=jax.ShapeDtypeStruct((rows, total), arrays[0].dtype),
        in_specs=[VMEM] * len(arrays) + [ANY] * len(after),
        out_specs=VMEM,
        compiler_params=pltpu.CompilerParams(vmem_limit_bytes=max(2**20, 8 * rows * total - 2**24)),
        cost_estimate=pl.CostEstimate(flops=0, bytes_accessed=4 * rows * total, transcendentals=0),
        name="join_columns",
    )(*arrays, *after)


def hold_kernel(*refs):
    out_ref = refs[-1]
    out_ref[...] = jnp.zeros_like(out_ref)


def hold(message, after, size):
    return pl.pallas_call(
        hold_kernel,
        out_shape=jax.ShapeDtypeStruct((16, lanes), message.dtype),
        in_specs=[ANY] * (1 + len(after)),
        out_specs=VMEM,
        cost_estimate=pl.CostEstimate(flops=max(dear, dear_per_byte * size) // lax.axis_size("tok"), bytes_accessed=0, transcendentals=0),
        compiler_params=pltpu.CompilerParams(vmem_limit_bytes=2**20),
        name="hold",
    )(message, *after)


def mask_kernel(valid_ref, user_ref, cot_ref, *out_refs):
    rows, width = out_refs[0].shape
    keep = lax.broadcasted_iota(jnp.int32, (rows, width), 0) < valid_ref[0]
    for slot, out_ref in enumerate(out_refs):
        column = pl.multiple_of((user_ref[0] ^ slot) * width, lanes)
        block = cot_ref[0, :, pl.ds(column, width)]
        out_ref[...] = jnp.where(keep, block, jnp.zeros_like(block))


def mask(valid, user, cotangent, user_count):
    _, rows, total = cotangent.shape
    return pl.pallas_call(
        mask_kernel,
        out_shape=[jax.ShapeDtypeStruct((rows, total // user_count), cotangent.dtype)] * user_count,
        in_specs=[SMEM, SMEM, VMEM],
        out_specs=[VMEM] * user_count,
        compiler_params=pltpu.CompilerParams(vmem_limit_bytes=2 * 2**20),
        name="mask_cotangent",
    )(valid, user, cotangent)


def product_kernel(lefts, rights, tile, has_held, has_sums, copies, *refs):
    outs = refs[-2:] if copies else refs[-1:]
    inputs = list(refs[: -len(outs)])
    sums_in = inputs.pop() if has_sums else None
    held_ref = inputs.pop() if has_held else None
    product_ref = outs[0]
    user_count, width, columns = product_ref.shape
    squares = []
    for slot in range(user_count):
        right = jnp.concatenate(
            [refs[at][:, start : start + columns] for at, start in rights[slot]], axis=0
        )

        def step(i, total, slot=slot, right=right):
            rows = pl.ds(pl.multiple_of(i * tile, tile), tile)
            left = jnp.concatenate(
                [
                    refs[at][:, pl.ds(pl.multiple_of(start + i * tile, lanes), tile)]
                    for at, start in lefts[slot]
                ],
                axis=0,
            )
            value = lax.dot_general(
                left, right, (((0,), (0,)), ((), ())), preferred_element_type=jnp.float32
            )
            if has_held:
                value += held_ref[slot, rows, :]
            product_ref[slot, rows, :] = value
            if copies:
                row = jnp.sum(value * value, axis=0, keepdims=True)
                for start in range(0, columns, lanes):
                    total += row[:, start : start + lanes]
            return total

        squares.append(lax.fori_loop(0, width // tile, step, jnp.zeros((1, lanes), jnp.float32)))
    if copies:
        rows = jnp.concatenate(squares + [jnp.zeros((8 - user_count, lanes), jnp.float32)], axis=0)
        if has_sums:
            rows += sums_in[0]
        outs[1][...] = jnp.broadcast_to(rows[None], outs[1].shape)


def product(lefts, rights, width, columns, held=None, sums=None, copies=0, after=()):
    operands, at = [], {}

    def place(part):
        array, start = part
        if id(array) not in at:
            at[id(array)] = len(operands)
            operands.append(array)
        return at[id(array)], start

    user_count, sources = len(lefts), len(lefts[0])
    left_places = [[place(part) for part in slot] for slot in lefts]
    right_places = [[place(part) for part in slot] for slot in rights]
    tokens = sources * lefts[0][0][0].shape[0]
    blocks = len(operands)
    operands += [array for array in after if id(array) not in at and array is not held]
    waits = len(operands) - blocks
    aliases = {}
    if held is not None:
        aliases = {len(operands): 0}
        operands.append(held)
    if sums is not None:
        operands.append(sums)
    out_shape = [jax.ShapeDtypeStruct((user_count, width, columns), jnp.float32)]
    if copies:
        out_shape.append(jax.ShapeDtypeStruct((copies, 8, lanes), jnp.float32))
    tile = math.gcd(width, 2 * lanes)
    return pl.pallas_call(
        functools.partial(
            product_kernel, left_places, right_places, tile, held is not None, sums is not None, copies
        ),
        out_shape=out_shape,
        in_specs=[VMEM] * blocks + [ANY] * waits + [VMEM] * (len(operands) - blocks - waits),
        out_specs=[VMEM] * len(out_shape),
        input_output_aliases=aliases,
        compiler_params=pltpu.CompilerParams(vmem_limit_bytes=8 * 2**20),
        cost_estimate=pl.CostEstimate(
            flops=2 * user_count * tokens * columns * width,
            bytes_accessed=2 * user_count * tokens * (width + columns),
            transcendentals=0,
        ),
        name="product_and_squares",
    )(*operands)


def combine_kernel(user_count, clip_bound, scaling, starts, user_ref, sums_ref, *refs):
    out_ref, factor_ref = refs[-2:]

    @pl.when(pl.program_id(0) == 0)
    def _():
        per_user = sums_ref.shape[0] // user_count
        by_source = [
            jnp.sum(sums_ref[j * per_user : (j + 1) * per_user], axis=0) for j in range(user_count)
        ]
        factors = []
        for u in range(user_count):
            row = sum(by_source[j][j ^ u : (j ^ u) + 1, :] for j in range(user_count))
            norm_sq = jnp.sum(row, axis=1, keepdims=True)
            factors.append(jnp.minimum(1.0, clip_bound / jnp.sqrt(norm_sq + epsilon)) * scaling)
        for slot in range(user_count):
            user = user_ref[0] ^ slot
            factor = sum(jnp.where(user == u, factors[u], 0.0) for u in range(user_count))
            factor_ref[slot : slot + 1, :] = jnp.broadcast_to(factor, (1, lanes))

    by_slot = [factor_ref[slot : slot + 1, 0:1] for slot in range(user_count)]
    tile = out_ref.shape[0]
    row = pl.program_id(0) * tile
    for ref, start in zip(refs, starts):

        @pl.when((row >= start) & (row < start + ref.shape[1]))
        def _(ref=ref, start=start):
            at = pl.ds(pl.multiple_of(row - start, tile), tile)
            result = by_slot[0] * ref[0, at, :]
            for slot in range(1, user_count):
                result += by_slot[slot] * ref[slot, at, :]
            out_ref[...] = result


def combine(user, sums, gradients, clip_bound, scaling):
    user_count, _, columns = gradients[0].shape
    heights = [gradient.shape[1] for gradient in gradients]
    starts = [sum(heights[:i]) for i in range(len(heights))]
    rows = sum(heights)
    tile = math.gcd(256, *heights)
    return pl.pallas_call(
        functools.partial(combine_kernel, user_count, clip_bound, scaling, starts),
        grid=(rows // tile,),
        out_shape=jax.ShapeDtypeStruct((rows, columns), jnp.float32),
        in_specs=[SMEM] + [VMEM] * (1 + len(gradients)),
        out_specs=pl.BlockSpec((tile, columns), lambda i: (i, 0)),
        scratch_shapes=[pltpu.VMEM((8, lanes), jnp.float32)],
        compiler_params=pltpu.CompilerParams(vmem_limit_bytes=8 * 2**20),
        name="weighted_sum",
    )(user, sums, *gradients)


def body(hidden, cotangent, lengths):
    tok_count = lax.axis_size("tok")
    user_count = lax.axis_size("user")
    tok_rows = hidden.shape[1]
    hidden_width = hidden.shape[2]
    model_width = cotangent.shape[2]
    capacity = tok_rows * tok_count
    own_width = hidden_width // tok_count
    columns = model_width // user_count
    clip_bound = math.sqrt(8.0 * hidden_width * model_width * capacity)
    scaling = math.sqrt(hidden_width * model_width) / (user_count * clip_bound)
    user = lax.axis_index("user").astype(jnp.int32).reshape(1)
    tok = lax.axis_index("tok").astype(jnp.int32).reshape(1)
    valid = lengths - tok * tok_rows
    half = tok_count // 2
    across, core = user_count // 2, user_count // 4
    slots = range(user_count)
    cut = round(own_width // lanes * first_part) * lanes
    pieces = [(0, cut), (cut, own_width - cut)]

    cots = {}
    lefts = {}
    ready = []
    tick = []

    sizes = [0]

    def send(axis, distance, parts, after=()):
        message = join(parts, [*tick, *after])
        sizes.append(2 * message.size)
        tick[:] = [message]
        return message, exchange(message, axis, distance)

    def cot_parts(d):
        return [(*cots[d][s], columns) for s in slots]

    def cots_at(array, start):
        return [(array, start + s * columns) for s in slots]

    masked = mask(valid, user, cotangent, user_count)
    by_slot = [masked[0]] + [exchange(masked[s], "user", s) for s in range(1, user_count)]
    outgoing = pack(tok, hidden, list(range(tok_count)), own_width, [])
    ready += [(0, i, outgoing[0], start) for i, (start, _) in enumerate(pieces)]

    far_steps = [[(half, None), ("cots", None)], [None, None]]
    far = [(d, None) for d in range(half + 1, tok_count - 1)] + [(tok_count - 1, 0), (tok_count - 1, 1)]
    for at, block in enumerate(far):
        far_steps.append([block, None] if at % 2 == 0 else [None, block])
    far_steps += [[("wait", None), None], [None, ("wait", None)]]
    near = list(range(1, half))
    near_steps = [near[:2], []] + [[d] for d in near[2:]]
    relayed = set()

    def rides(d):
        return d & (d - 1) == 0 and d < half // 2

    def bits_below(d):
        if d == 0:
            return [half // 2]
        return [1 << i for i in range((d & -d).bit_length() - 1)]


    lanes_before = [None, None]
    near_before, relay_before, cross_before, core_before = [], [], None, None
    crossed = []
    gradients = [None, None]
    done = set()

    def finish_core():
        nonlocal core_before
        if core_before is not None:
            units, both = core_before
            core_before = None
            to = 0
            for blocks, own, other in units:
                total = sum(pieces[i][1] for _, i, _, _ in blocks)
                at = 0
                for d, i, _, _ in blocks:
                    lefts[d, i] = {
                        0: (own, at),
                        across: (other, at),
                        core: (both, to + at),
                        across ^ core: (both, to + total + at),
                    }
                    at += pieces[i][1]
                to += 2 * total

    def finish_relays(step):
        arrived = []
        for entry in list(relay_before):
            due, bit, sources, array = entry
            if due <= step:
                relay_before.remove(entry)
                arrived.append(array)
                for at, d in enumerate(sources):
                    cots[d + bit] = cots_at(array, at * model_width)
        return arrived

    def add_products(i):
        width = pieces[i][1]
        here = [d for d in range(tok_count) if d in cots and (d, i) in lefts and (d, i) not in done]
        if not here:
            return
        done.update((d, i) for d in here)
        full = all((d, i) in done for d in range(tok_count))
        out = product(
            [[lefts[d, i][s] for d in here] for s in slots],
            [[cots[d][s] for d in here] for s in slots],
            width,
            columns,
            held=gradients[i][0] if gradients[i] else None,
            sums=gradients[0][1] if full and i == 1 else None,
            copies=0 if not full else tok_count * user_count if i == 1 else 1,
            after=tick[:1] if not full else [],
        )
        gradients[i] = out
        tick.append(out[0])

    for step in range(len(far_steps) + 1):
        flying = 0
        now = far_steps[step] if step < len(far_steps) else [None, None]
        for lane in (0, 1):
            if lane == 1 and now[1] == ("cots", None):
                continue
            if now[lane] is not None:
                after = []
                if lanes_before[lane] is not None:
                    (d, i), array = lanes_before[lane]
                    lanes_before[lane] = None
                    after.append(array)
                    if d == "cots":
                        cots[half] = cots_at(array, 0)
                    else:
                        first = pieces[i][0] if i is not None else 0
                        ready += [
                            (d, j, array, at - first) for j, (at, _) in enumerate(pieces) if i is None or i == j
                        ]
                d, i = now[lane]
                if d != "wait":
                    first, width = pieces[i] if i is not None else (0, own_width)
                    array = send("tok", d, [(outgoing[d], first, width)], after)[1]
                    lanes_before[lane] = (now[lane], array)
            flying += lanes_before[lane] is not None
        for entry in list(near_before):
            due, d, array = entry
            if due > step:
                flying += 1
                continue
            near_before.remove(entry)
            ready += [(d, i, array, first) for i, (first, _) in enumerate(pieces)]
            if rides(d):
                cots[d] = cots_at(array, own_width)
        arrivals = finish_relays(step)
        if cross_before is not None:
            crossed.append(cross_before)
        earlier = [cross_before[2]] if cross_before is not None else []
        earlier += [core_before[1]] if core_before is not None else []
        cross_before = None
        if ready:
            blocks = []
            while ready and sum(pieces[i][1] for _, i, _, _ in blocks) < 2 * own_width:
                blocks.append(ready.pop(0))
            parts = [(array, first, pieces[i][1]) for _, i, array, first in blocks]
            own, other = send("user", across, parts, earlier)
            earlier = []
            cross_before = (blocks, own, other)
            flying += 1
        bit, sent = half // 2, False
        while bit:
            sources = [d for d in sorted(cots) if bit in bits_below(d) and d + bit not in relayed]
            if sources and step > 0 and (step > 5 or (flying < 5 and not sent)):
                relayed.update(d + bit for d in sources)
                parts = [part for d in sources for part in cot_parts(d)]
                relay_before.append((step + (1 if step < 3 else 2), bit, sources, send("tok", bit, parts, earlier)[1]))
                earlier = []
                flying += 1
                sent = True
            bit //= 2
        if step == 0:
            cots[0] = [(block, 0) for block in by_slot]
            cots[0] = cots_at(join(cot_parts(0), tick), 0)
            lanes_before[1] = (("cots", None), send("tok", half, cot_parts(0))[1])
            flying += 1
        if step < len(near_steps):
            for d in near_steps[step]:
                parts = [(outgoing[d], 0, own_width)]
                if rides(d):
                    parts += cot_parts(0)
                near_before.append((step + (3 if step else 1), d, send("tok", d, parts)[1]))
                flying += 1
        before = [core_before[1]] if core_before else []
        finish_core()
        if crossed and (flying < 5 or step >= len(far_steps) - 3):
            parts = []
            for blocks, own, other in crossed:
                total = sum(pieces[i][1] for _, i, _, _ in blocks)
                parts += [(own, 0, total), (other, 0, total)]
            core_before = (list(crossed), send("user", core, parts, before)[1])
            crossed.clear()
            flying += 1
        if step < len(far_steps):
            tick[:] = [hold(tick[0], arrivals + earlier, max(sizes))]
            sizes[:] = [0]
        if step == len(far_steps) - 3:
            add_products(0)
        elif step == len(far_steps) - 2:
            add_products(1)
        elif step == len(far_steps) - 1:
            finish_core()
            add_products(0)
    finish_core()
    add_products(0)
    add_products(1)
    sums = lax.all_to_all(gradients[1][1], ("user", "tok"), split_axis=0, concat_axis=0, tiled=True)
    return combine(user, sums, [g[0] for g in gradients], clip_bound, scaling)


def solution(mesh):
    return jax.shard_map(
        body,
        mesh=mesh,
        in_specs=(P("user", "tok", None), P("user", "tok", None), P("user")),
        out_specs=P("tok", "user"),
        check_vma=False,
    )
```

```python
import functools
import math

import jax
import jax.numpy as jnp
from jax import lax
from jax.experimental import pallas as pl
from jax.experimental.pallas import tpu as pltpu
from jax.sharding import PartitionSpec as P

epsilon = 1e-06
lanes = 128
first_part = 0.625
dear = 24 * 10**10
dear_per_byte = 2 * 10**5
ANY = pl.BlockSpec(memory_space=pl.ANY)
SMEM = pl.BlockSpec(memory_space=pltpu.SMEM)
VMEM = pl.BlockSpec(memory_space=pltpu.VMEM)
HBM = pl.BlockSpec(memory_space=pltpu.HBM)


def exchange(block, axis, distance):
    size = lax.axis_size(axis)
    return lax.ppermute(block, axis, [(i, i ^ distance) for i in range(size)])


def pack_kernel(distances, tok_ref, hidden_ref, *refs):
    out_refs, sems = refs[-1 - len(distances) : -1], refs[-1]
    width = out_refs[0].shape[1]
    copies = []
    for at, distance in enumerate(distances):
        start = pl.multiple_of((tok_ref[0] ^ distance) * width, lanes)
        copies.append(
            pltpu.make_async_copy(
                hidden_ref.at[0, :, pl.ds(start, width)], out_refs[at], sems.at[at]
            )
        )
    for copy in copies:
        copy.start()
    for copy in copies:
        copy.wait()


def pack(tok, hidden, distances, width, after):
    rows = hidden.shape[1]
    count = len(distances)
    return pl.pallas_call(
        functools.partial(pack_kernel, distances),
        out_shape=[jax.ShapeDtypeStruct((rows, width), hidden.dtype)] * count,
        in_specs=[SMEM, HBM] + [ANY] * len(after),
        out_specs=[VMEM] * count,
        scratch_shapes=[pltpu.SemaphoreType.DMA((count,))],
        compiler_params=pltpu.CompilerParams(vmem_limit_bytes=2**20),
        cost_estimate=pl.CostEstimate(
            flops=0, bytes_accessed=4 * count * rows * width, transcendentals=0
        ),
        name="pack_columns",
    )(tok, hidden, *after)


def join_kernel(parts, *refs):
    out_ref = refs[-1]
    to = 0
    for at, start, width in parts:
        out_ref[:, to : to + width] = refs[at][:, start : start + width]
        to += width


def join(parts, after):
    arrays, places = [], []
    for array, start, width in parts:
        at = [i for i, other in enumerate(arrays) if other is array]
        if not at:
            arrays.append(array)
        places.append((at[0] if at else len(arrays) - 1, start, width))
    after = [array for array in after if not any(array is other for other in arrays)]
    rows = arrays[0].shape[0]
    total = sum(width for _, _, width in parts)
    return pl.pallas_call(
        functools.partial(join_kernel, places),
        out_shape=jax.ShapeDtypeStruct((rows, total), arrays[0].dtype),
        in_specs=[VMEM] * len(arrays) + [ANY] * len(after),
        out_specs=VMEM,
        compiler_params=pltpu.CompilerParams(vmem_limit_bytes=max(2**20, 8 * rows * total - 2**24)),
        cost_estimate=pl.CostEstimate(flops=0, bytes_accessed=4 * rows * total, transcendentals=0),
        name="join_columns",
    )(*arrays, *after)


def hold_kernel(*refs):
    out_ref = refs[-1]
    out_ref[...] = jnp.zeros_like(out_ref)


def hold(message, after, size):
    return pl.pallas_call(
        hold_kernel,
        out_shape=jax.ShapeDtypeStruct((16, lanes), message.dtype),
        in_specs=[ANY] * (1 + len(after)),
        out_specs=VMEM,
        cost_estimate=pl.CostEstimate(flops=max(dear, dear_per_byte * size) // lax.axis_size("tok"), bytes_accessed=0, transcendentals=0),
        compiler_params=pltpu.CompilerParams(vmem_limit_bytes=2**20),
        name="hold",
    )(message, *after)


def mask_kernel(valid_ref, user_ref, cot_ref, *out_refs):
    rows, width = out_refs[0].shape
    keep = lax.broadcasted_iota(jnp.int32, (rows, width), 0) < valid_ref[0]
    for slot, out_ref in enumerate(out_refs):
        column = pl.multiple_of((user_ref[0] ^ slot) * width, lanes)
        block = cot_ref[0, :, pl.ds(column, width)]
        out_ref[...] = jnp.where(keep, block, jnp.zeros_like(block))


def mask(valid, user, cotangent, user_count):
    _, rows, total = cotangent.shape
    return pl.pallas_call(
        mask_kernel,
        out_shape=[jax.ShapeDtypeStruct((rows, total // user_count), cotangent.dtype)] * user_count,
        in_specs=[SMEM, SMEM, VMEM],
        out_specs=[VMEM] * user_count,
        compiler_params=pltpu.CompilerParams(vmem_limit_bytes=2 * 2**20),
        name="mask_cotangent",
    )(valid, user, cotangent)


def product_kernel(lefts, rights, tile, has_held, has_sums, copies, *refs):
    outs = refs[-2:] if copies else refs[-1:]
    inputs = list(refs[: -len(outs)])
    sums_in = inputs.pop() if has_sums else None
    held_ref = inputs.pop() if has_held else None
    product_ref = outs[0]
    user_count, width, columns = product_ref.shape
    squares = []
    for slot in range(user_count):
        right = jnp.concatenate(
            [refs[at][:, start : start + columns] for at, start in rights[slot]], axis=0
        )

        def step(i, total, slot=slot, right=right):
            rows = pl.ds(pl.multiple_of(i * tile, tile), tile)
            left = jnp.concatenate(
                [
                    refs[at][:, pl.ds(pl.multiple_of(start + i * tile, lanes), tile)]
                    for at, start in lefts[slot]
                ],
                axis=0,
            )
            value = lax.dot_general(
                left, right, (((0,), (0,)), ((), ())), preferred_element_type=jnp.float32
            )
            if has_held:
                value += held_ref[slot, rows, :]
            product_ref[slot, rows, :] = value
            if copies:
                row = jnp.sum(value * value, axis=0, keepdims=True)
                for start in range(0, columns, lanes):
                    total += row[:, start : start + lanes]
            return total

        squares.append(lax.fori_loop(0, width // tile, step, jnp.zeros((1, lanes), jnp.float32)))
    if copies:
        rows = jnp.concatenate(squares + [jnp.zeros((8 - user_count, lanes), jnp.float32)], axis=0)
        if has_sums:
            rows += sums_in[0]
        outs[1][...] = jnp.broadcast_to(rows[None], outs[1].shape)


def product(lefts, rights, width, columns, held=None, sums=None, copies=0, after=()):
    operands, at = [], {}

    def place(part):
        array, start = part
        if id(array) not in at:
            at[id(array)] = len(operands)
            operands.append(array)
        return at[id(array)], start

    user_count, sources = len(lefts), len(lefts[0])
    left_places = [[place(part) for part in slot] for slot in lefts]
    right_places = [[place(part) for part in slot] for slot in rights]
    tokens = sources * lefts[0][0][0].shape[0]
    blocks = len(operands)
    operands += [array for array in after if id(array) not in at and array is not held]
    waits = len(operands) - blocks
    aliases = {}
    if held is not None:
        aliases = {len(operands): 0}
        operands.append(held)
    if sums is not None:
        operands.append(sums)
    out_shape = [jax.ShapeDtypeStruct((user_count, width, columns), jnp.float32)]
    if copies:
        out_shape.append(jax.ShapeDtypeStruct((copies, 8, lanes), jnp.float32))
    tile = math.gcd(width, 2 * lanes)
    return pl.pallas_call(
        functools.partial(
            product_kernel, left_places, right_places, tile, held is not None, sums is not None, copies
        ),
        out_shape=out_shape,
        in_specs=[VMEM] * blocks + [ANY] * waits + [VMEM] * (len(operands) - blocks - waits),
        out_specs=[VMEM] * len(out_shape),
        input_output_aliases=aliases,
        compiler_params=pltpu.CompilerParams(vmem_limit_bytes=8 * 2**20),
        cost_estimate=pl.CostEstimate(
            flops=2 * user_count * tokens * columns * width,
            bytes_accessed=2 * user_count * tokens * (width + columns),
            transcendentals=0,
        ),
        name="product_and_squares",
    )(*operands)


def combine_kernel(user_count, clip_bound, scaling, starts, user_ref, sums_ref, *refs):
    out_ref, factor_ref = refs[-2:]

    @pl.when(pl.program_id(0) == 0)
    def _():
        per_user = sums_ref.shape[0] // user_count
        by_source = [
            jnp.sum(sums_ref[j * per_user : (j + 1) * per_user], axis=0) for j in range(user_count)
        ]
        factors = []
        for u in range(user_count):
            row = sum(by_source[j][j ^ u : (j ^ u) + 1, :] for j in range(user_count))
            norm_sq = jnp.sum(row, axis=1, keepdims=True)
            factors.append(jnp.minimum(1.0, clip_bound / jnp.sqrt(norm_sq + epsilon)) * scaling)
        for slot in range(user_count):
            user = user_ref[0] ^ slot
            factor = sum(jnp.where(user == u, factors[u], 0.0) for u in range(user_count))
            factor_ref[slot : slot + 1, :] = jnp.broadcast_to(factor, (1, lanes))

    by_slot = [factor_ref[slot : slot + 1, 0:1] for slot in range(user_count)]
    tile = out_ref.shape[0]
    row = pl.program_id(0) * tile
    for ref, start in zip(refs, starts):

        @pl.when((row >= start) & (row < start + ref.shape[1]))
        def _(ref=ref, start=start):
            at = pl.ds(pl.multiple_of(row - start, tile), tile)
            result = by_slot[0] * ref[0, at, :]
            for slot in range(1, user_count):
                result += by_slot[slot] * ref[slot, at, :]
            out_ref[...] = result


def combine(user, sums, gradients, clip_bound, scaling):
    user_count, _, columns = gradients[0].shape
    heights = [gradient.shape[1] for gradient in gradients]
    starts = [sum(heights[:i]) for i in range(len(heights))]
    rows = sum(heights)
    tile = math.gcd(256, *heights)
    return pl.pallas_call(
        functools.partial(combine_kernel, user_count, clip_bound, scaling, starts),
        grid=(rows // tile,),
        out_shape=jax.ShapeDtypeStruct((rows, columns), jnp.float32),
        in_specs=[SMEM] + [VMEM] * (1 + len(gradients)),
        out_specs=pl.BlockSpec((tile, columns), lambda i: (i, 0)),
        scratch_shapes=[pltpu.VMEM((8, lanes), jnp.float32)],
        compiler_params=pltpu.CompilerParams(vmem_limit_bytes=8 * 2**20),
        name="weighted_sum",
    )(user, sums, *gradients)


def body(hidden, cotangent, lengths):
    tok_count = lax.axis_size("tok")
    user_count = lax.axis_size("user")
    tok_rows = hidden.shape[1]
    hidden_width = hidden.shape[2]
    model_width = cotangent.shape[2]
    capacity = tok_rows * tok_count
    own_width = hidden_width // tok_count
    columns = model_width // user_count
    clip_bound = math.sqrt(8.0 * hidden_width * model_width * capacity)
    scaling = math.sqrt(hidden_width * model_width) / (user_count * clip_bound)
    user = lax.axis_index("user").astype(jnp.int32).reshape(1)
    tok = lax.axis_index("tok").astype(jnp.int32).reshape(1)
    valid = lengths - tok * tok_rows
    half = tok_count // 2
    across, core = user_count // 2, user_count // 4
    slots = range(user_count)
    cut = round(own_width // lanes * first_part) * lanes
    pieces = [(0, cut), (cut, own_width - cut)]

    cots = {}
    lefts = {}
    ready = []
    tick = []

    sizes = [0]

    def send(axis, distance, parts, after=()):
        message = join(parts, [*tick, *after])
        sizes.append(2 * message.size)
        tick[:] = [message]
        return message, exchange(message, axis, distance)

    def cot_parts(d):
        return [(*cots[d][s], columns) for s in slots]

    def cots_at(array, start):
        return [(array, start + s * columns) for s in slots]

    masked = mask(valid, user, cotangent, user_count)
    by_slot = [masked[0]] + [exchange(masked[s], "user", s) for s in range(1, user_count)]
    outgoing = pack(tok, hidden, list(range(tok_count)), own_width, [])
    ready += [(0, i, outgoing[0], start) for i, (start, _) in enumerate(pieces)]

    far_steps = [[(half, None), ("cots", None)], [None, None]]
    far = [(d, None) for d in range(half + 1, tok_count - 1)] + [(tok_count - 1, 0), (tok_count - 1, 1)]
    for at, block in enumerate(far):
        far_steps.append([block, None] if at % 2 == 0 else [None, block])
    far_steps += [[("wait", None), None], [None, ("wait", None)]]
    near = list(range(1, half))
    near_steps = [near[:2], [], []] + [[d] for d in near[2:]]
    relayed = set()

    def rides(d):
        return d & (d - 1) == 0 and d < half // 2

    def bits_below(d):
        if d == 0:
            return [half // 2]
        return [1 << i for i in range((d & -d).bit_length() - 1)]


    lanes_before = [None, None]
    near_before, relay_before, cross_before, core_before = [], [], None, None
    crossed = []
    gradients = [None, None]
    done = set()

    def finish_core():
        nonlocal core_before
        if core_before is not None:
            units, both = core_before
            core_before = None
            to = 0
            for blocks, own, other in units:
                total = sum(pieces[i][1] for _, i, _, _ in blocks)
                at = 0
                for d, i, _, _ in blocks:
                    lefts[d, i] = {
                        0: (own, at),
                        across: (other, at),
                        core: (both, to + at),
                        across ^ core: (both, to + total + at),
                    }
                    at += pieces[i][1]
                to += 2 * total

    def finish_relays(step):
        arrived = []
        for entry in list(relay_before):
            due, bit, sources, array = entry
            if due <= step:
                relay_before.remove(entry)
                arrived.append(array)
                for at, d in enumerate(sources):
                    cots[d + bit] = cots_at(array, at * model_width)
        return arrived

    def add_products(i):
        width = pieces[i][1]
        here = [d for d in range(tok_count) if d in cots and (d, i) in lefts and (d, i) not in done]
        if not here:
            return
        done.update((d, i) for d in here)
        full = all((d, i) in done for d in range(tok_count))
        out = product(
            [[lefts[d, i][s] for d in here] for s in slots],
            [[cots[d][s] for d in here] for s in slots],
            width,
            columns,
            held=gradients[i][0] if gradients[i] else None,
            sums=gradients[0][1] if full and i == 1 else None,
            copies=0 if not full else tok_count * user_count if i == 1 else 1,
            after=tick[:1] if not full else [],
        )
        gradients[i] = out
        tick.append(out[0])

    for step in range(len(far_steps) + 1):
        flying = 0
        now = far_steps[step] if step < len(far_steps) else [None, None]
        for lane in (0, 1):
            if lane == 1 and now[1] == ("cots", None):
                continue
            if now[lane] is not None:
                after = []
                if lanes_before[lane] is not None:
                    (d, i), array = lanes_before[lane]
                    lanes_before[lane] = None
                    after.append(array)
                    if d == "cots":
                        cots[half] = cots_at(array, 0)
                    else:
                        first = pieces[i][0] if i is not None else 0
                        ready += [
                            (d, j, array, at - first) for j, (at, _) in enumerate(pieces) if i is None or i == j
                        ]
                d, i = now[lane]
                if d != "wait":
                    first, width = pieces[i] if i is not None else (0, own_width)
                    array = send("tok", d, [(outgoing[d], first, width)], after)[1]
                    lanes_before[lane] = (now[lane], array)
            flying += lanes_before[lane] is not None
        for entry in list(near_before):
            due, d, array = entry
            if due > step:
                flying += 1
                continue
            near_before.remove(entry)
            ready += [(d, i, array, first) for i, (first, _) in enumerate(pieces)]
            if rides(d):
                cots[d] = cots_at(array, own_width)
        arrivals = finish_relays(step)
        if cross_before is not None:
            crossed.append(cross_before)
        earlier = [cross_before[2]] if cross_before is not None else []
        earlier += [core_before[1]] if core_before is not None else []
        if step == 3:
            earlier, arrivals = earlier + arrivals, []
        cross_before = None
        if ready:
            blocks = []
            while ready and sum(pieces[i][1] for _, i, _, _ in blocks) < 2 * own_width:
                blocks.append(ready.pop(0))
            parts = [(array, first, pieces[i][1]) for _, i, array, first in blocks]
            own, other = send("user", across, parts, earlier)
            earlier = []
            cross_before = (blocks, own, other)
            flying += 1
        bit, sent = half // 2, False
        while bit:
            sources = [d for d in sorted(cots) if bit in bits_below(d) and d + bit not in relayed]
            if sources and step > 0 and (step > 5 or (flying < 5 and not sent)):
                relayed.update(d + bit for d in sources)
                parts = [part for d in sources for part in cot_parts(d)]
                relay_before.append((step + (1 if step < 3 else 2), bit, sources, send("tok", bit, parts, earlier)[1]))
                earlier = []
                flying += 1
                sent = True
            bit //= 2
        if step == 0:
            cots[0] = [(block, 0) for block in by_slot]
            cots[0] = cots_at(join(cot_parts(0), tick), 0)
            lanes_before[1] = (("cots", None), send("tok", half, cot_parts(0))[1])
            flying += 1
        if step < len(near_steps):
            for d in near_steps[step]:
                parts = [(outgoing[d], 0, own_width)]
                if rides(d):
                    parts += cot_parts(0)
                near_before.append((step + (2 if step else 1), d, send("tok", d, parts)[1]))
                flying += 1
        before = [core_before[1]] if core_before else []
        finish_core()
        if crossed and (flying < 5 or step >= len(far_steps) - 3):
            parts = []
            for blocks, own, other in crossed:
                total = sum(pieces[i][1] for _, i, _, _ in blocks)
                parts += [(own, 0, total), (other, 0, total)]
            core_before = (list(crossed), send("user", core, parts, before)[1])
            crossed.clear()
            flying += 1
        if step < len(far_steps):
            tick[:] = [hold(tick[0], arrivals + earlier, max(sizes))]
            sizes[:] = [0]
        if step == len(far_steps) - 3:
            add_products(0)
        elif step == len(far_steps) - 2:
            add_products(1)
        elif step == len(far_steps) - 1:
            finish_core()
            add_products(0)
    finish_core()
    add_products(0)
    add_products(1)
    sums = lax.all_to_all(gradients[1][1], ("user", "tok"), split_axis=0, concat_axis=0, tiled=True)
    return combine(user, sums, [g[0] for g in gradients], clip_bound, scaling)


def solution(mesh):
    return jax.shard_map(
        body,
        mesh=mesh,
        in_specs=(P("user", "tok", None), P("user", "tok", None), P("user")),
        out_specs=P("tok", "user"),
        check_vma=False,
    )
```

```python
import functools
import math

import jax
import jax.numpy as jnp
from jax import lax
from jax.experimental import pallas as pl
from jax.experimental.pallas import tpu as pltpu
from jax.sharding import PartitionSpec as P

epsilon = 1e-06
lanes = 128
first_part = 0.625
dear = 24 * 10**10
dear_per_byte = 2 * 10**5
ANY = pl.BlockSpec(memory_space=pl.ANY)
SMEM = pl.BlockSpec(memory_space=pltpu.SMEM)
VMEM = pl.BlockSpec(memory_space=pltpu.VMEM)
HBM = pl.BlockSpec(memory_space=pltpu.HBM)


def exchange(block, axis, distance):
    size = lax.axis_size(axis)
    return lax.ppermute(block, axis, [(i, i ^ distance) for i in range(size)])


def pack_kernel(distances, tok_ref, hidden_ref, *refs):
    out_refs, sems = refs[-1 - len(distances) : -1], refs[-1]
    width = out_refs[0].shape[1]
    copies = []
    for at, distance in enumerate(distances):
        start = pl.multiple_of((tok_ref[0] ^ distance) * width, lanes)
        copies.append(
            pltpu.make_async_copy(
                hidden_ref.at[0, :, pl.ds(start, width)], out_refs[at], sems.at[at]
            )
        )
    for copy in copies:
        copy.start()
    for copy in copies:
        copy.wait()


def pack(tok, hidden, distances, width, after):
    rows = hidden.shape[1]
    count = len(distances)
    return pl.pallas_call(
        functools.partial(pack_kernel, distances),
        out_shape=[jax.ShapeDtypeStruct((rows, width), hidden.dtype)] * count,
        in_specs=[SMEM, HBM] + [ANY] * len(after),
        out_specs=[VMEM] * count,
        scratch_shapes=[pltpu.SemaphoreType.DMA((count,))],
        compiler_params=pltpu.CompilerParams(vmem_limit_bytes=2**20),
        cost_estimate=pl.CostEstimate(
            flops=0, bytes_accessed=4 * count * rows * width, transcendentals=0
        ),
        name="pack_columns",
    )(tok, hidden, *after)


def join_kernel(parts, *refs):
    out_ref = refs[-1]
    to = 0
    for at, start, width in parts:
        out_ref[:, to : to + width] = refs[at][:, start : start + width]
        to += width


def join(parts, after):
    arrays, places = [], []
    for array, start, width in parts:
        at = [i for i, other in enumerate(arrays) if other is array]
        if not at:
            arrays.append(array)
        places.append((at[0] if at else len(arrays) - 1, start, width))
    after = [array for array in after if not any(array is other for other in arrays)]
    rows = arrays[0].shape[0]
    total = sum(width for _, _, width in parts)
    return pl.pallas_call(
        functools.partial(join_kernel, places),
        out_shape=jax.ShapeDtypeStruct((rows, total), arrays[0].dtype),
        in_specs=[VMEM] * len(arrays) + [ANY] * len(after),
        out_specs=VMEM,
        compiler_params=pltpu.CompilerParams(vmem_limit_bytes=max(2**20, 8 * rows * total - 2**24)),
        cost_estimate=pl.CostEstimate(flops=0, bytes_accessed=4 * rows * total, transcendentals=0),
        name="join_columns",
    )(*arrays, *after)


def hold_kernel(*refs):
    out_ref = refs[-1]
    out_ref[...] = jnp.zeros_like(out_ref)


def hold(message, after, size):
    return pl.pallas_call(
        hold_kernel,
        out_shape=jax.ShapeDtypeStruct((16, lanes), message.dtype),
        in_specs=[ANY] * (1 + len(after)),
        out_specs=VMEM,
        cost_estimate=pl.CostEstimate(flops=max(dear, dear_per_byte * size) // lax.axis_size("tok"), bytes_accessed=0, transcendentals=0),
        compiler_params=pltpu.CompilerParams(vmem_limit_bytes=2**20),
        name="hold",
    )(message, *after)


def mask_kernel(valid_ref, user_ref, cot_ref, *out_refs):
    rows, width = out_refs[0].shape
    keep = lax.broadcasted_iota(jnp.int32, (rows, width), 0) < valid_ref[0]
    for slot, out_ref in enumerate(out_refs):
        column = pl.multiple_of((user_ref[0] ^ slot) * width, lanes)
        block = cot_ref[0, :, pl.ds(column, width)]
        out_ref[...] = jnp.where(keep, block, jnp.zeros_like(block))


def mask(valid, user, cotangent, user_count):
    _, rows, total = cotangent.shape
    return pl.pallas_call(
        mask_kernel,
        out_shape=[jax.ShapeDtypeStruct((rows, total // user_count), cotangent.dtype)] * user_count,
        in_specs=[SMEM, SMEM, VMEM],
        out_specs=[VMEM] * user_count,
        compiler_params=pltpu.CompilerParams(vmem_limit_bytes=2 * 2**20),
        name="mask_cotangent",
    )(valid, user, cotangent)


def product_kernel(lefts, rights, tile, has_held, has_sums, copies, *refs):
    outs = refs[-2:] if copies else refs[-1:]
    inputs = list(refs[: -len(outs)])
    sums_in = inputs.pop() if has_sums else None
    held_ref = inputs.pop() if has_held else None
    product_ref = outs[0]
    user_count, width, columns = product_ref.shape
    squares = []
    for slot in range(user_count):
        right = jnp.concatenate(
            [refs[at][:, start : start + columns] for at, start in rights[slot]], axis=0
        )

        def step(i, total, slot=slot, right=right):
            rows = pl.ds(pl.multiple_of(i * tile, tile), tile)
            left = jnp.concatenate(
                [
                    refs[at][:, pl.ds(pl.multiple_of(start + i * tile, lanes), tile)]
                    for at, start in lefts[slot]
                ],
                axis=0,
            )
            value = lax.dot_general(
                left, right, (((0,), (0,)), ((), ())), preferred_element_type=jnp.float32
            )
            if has_held:
                value += held_ref[slot, rows, :]
            product_ref[slot, rows, :] = value
            if copies:
                row = jnp.sum(value * value, axis=0, keepdims=True)
                for start in range(0, columns, lanes):
                    total += row[:, start : start + lanes]
            return total

        squares.append(lax.fori_loop(0, width // tile, step, jnp.zeros((1, lanes), jnp.float32)))
    if copies:
        rows = jnp.concatenate(squares + [jnp.zeros((8 - user_count, lanes), jnp.float32)], axis=0)
        if has_sums:
            rows += sums_in[0]
        outs[1][...] = jnp.broadcast_to(rows[None], outs[1].shape)


def product(lefts, rights, width, columns, held=None, sums=None, copies=0, after=()):
    operands, at = [], {}

    def place(part):
        array, start = part
        if id(array) not in at:
            at[id(array)] = len(operands)
            operands.append(array)
        return at[id(array)], start

    user_count, sources = len(lefts), len(lefts[0])
    left_places = [[place(part) for part in slot] for slot in lefts]
    right_places = [[place(part) for part in slot] for slot in rights]
    tokens = sources * lefts[0][0][0].shape[0]
    blocks = len(operands)
    operands += [array for array in after if id(array) not in at and array is not held]
    waits = len(operands) - blocks
    aliases = {}
    if held is not None:
        aliases = {len(operands): 0}
        operands.append(held)
    if sums is not None:
        operands.append(sums)
    out_shape = [jax.ShapeDtypeStruct((user_count, width, columns), jnp.float32)]
    if copies:
        out_shape.append(jax.ShapeDtypeStruct((copies, 8, lanes), jnp.float32))
    tile = math.gcd(width, 2 * lanes)
    return pl.pallas_call(
        functools.partial(
            product_kernel, left_places, right_places, tile, held is not None, sums is not None, copies
        ),
        out_shape=out_shape,
        in_specs=[VMEM] * blocks + [ANY] * waits + [VMEM] * (len(operands) - blocks - waits),
        out_specs=[VMEM] * len(out_shape),
        input_output_aliases=aliases,
        compiler_params=pltpu.CompilerParams(vmem_limit_bytes=8 * 2**20),
        cost_estimate=pl.CostEstimate(
            flops=2 * user_count * tokens * columns * width,
            bytes_accessed=2 * user_count * tokens * (width + columns),
            transcendentals=0,
        ),
        name="product_and_squares",
    )(*operands)


def combine_kernel(user_count, clip_bound, scaling, starts, user_ref, sums_ref, *refs):
    out_ref, factor_ref = refs[-2:]

    @pl.when(pl.program_id(0) == 0)
    def _():
        per_user = sums_ref.shape[0] // user_count
        by_source = [
            jnp.sum(sums_ref[j * per_user : (j + 1) * per_user], axis=0) for j in range(user_count)
        ]
        factors = []
        for u in range(user_count):
            row = sum(by_source[j][j ^ u : (j ^ u) + 1, :] for j in range(user_count))
            norm_sq = jnp.sum(row, axis=1, keepdims=True)
            factors.append(jnp.minimum(1.0, clip_bound / jnp.sqrt(norm_sq + epsilon)) * scaling)
        for slot in range(user_count):
            user = user_ref[0] ^ slot
            factor = sum(jnp.where(user == u, factors[u], 0.0) for u in range(user_count))
            factor_ref[slot : slot + 1, :] = jnp.broadcast_to(factor, (1, lanes))

    by_slot = [factor_ref[slot : slot + 1, 0:1] for slot in range(user_count)]
    tile = out_ref.shape[0]
    row = pl.program_id(0) * tile
    for ref, start in zip(refs, starts):

        @pl.when((row >= start) & (row < start + ref.shape[1]))
        def _(ref=ref, start=start):
            at = pl.ds(pl.multiple_of(row - start, tile), tile)
            result = by_slot[0] * ref[0, at, :]
            for slot in range(1, user_count):
                result += by_slot[slot] * ref[slot, at, :]
            out_ref[...] = result


def combine(user, sums, gradients, clip_bound, scaling):
    user_count, _, columns = gradients[0].shape
    heights = [gradient.shape[1] for gradient in gradients]
    starts = [sum(heights[:i]) for i in range(len(heights))]
    rows = sum(heights)
    tile = math.gcd(256, *heights)
    return pl.pallas_call(
        functools.partial(combine_kernel, user_count, clip_bound, scaling, starts),
        grid=(rows // tile,),
        out_shape=jax.ShapeDtypeStruct((rows, columns), jnp.float32),
        in_specs=[SMEM] + [VMEM] * (1 + len(gradients)),
        out_specs=pl.BlockSpec((tile, columns), lambda i: (i, 0)),
        scratch_shapes=[pltpu.VMEM((8, lanes), jnp.float32)],
        compiler_params=pltpu.CompilerParams(vmem_limit_bytes=8 * 2**20),
        name="weighted_sum",
    )(user, sums, *gradients)


def body(hidden, cotangent, lengths):
    tok_count = lax.axis_size("tok")
    user_count = lax.axis_size("user")
    tok_rows = hidden.shape[1]
    hidden_width = hidden.shape[2]
    model_width = cotangent.shape[2]
    capacity = tok_rows * tok_count
    own_width = hidden_width // tok_count
    columns = model_width // user_count
    clip_bound = math.sqrt(8.0 * hidden_width * model_width * capacity)
    scaling = math.sqrt(hidden_width * model_width) / (user_count * clip_bound)
    user = lax.axis_index("user").astype(jnp.int32).reshape(1)
    tok = lax.axis_index("tok").astype(jnp.int32).reshape(1)
    valid = lengths - tok * tok_rows
    half = tok_count // 2
    across, core = user_count // 2, user_count // 4
    slots = range(user_count)
    cut = round(own_width // lanes * first_part) * lanes
    pieces = [(0, cut), (cut, own_width - cut)]

    cots = {}
    lefts = {}
    ready = []
    tick = []

    sizes = [0]

    def send(axis, distance, parts, after=()):
        message = join(parts, [*tick, *after])
        sizes.append(2 * message.size)
        tick[:] = [message]
        return message, exchange(message, axis, distance)

    def cot_parts(d):
        return [(*cots[d][s], columns) for s in slots]

    def cots_at(array, start):
        return [(array, start + s * columns) for s in slots]

    masked = mask(valid, user, cotangent, user_count)
    by_slot = [masked[0]] + [exchange(masked[s], "user", s) for s in range(1, user_count)]
    outgoing = pack(tok, hidden, list(range(tok_count)), own_width, [])
    ready += [(0, i, outgoing[0], start) for i, (start, _) in enumerate(pieces)]

    far_steps = [[(half, None), ("cots", None)], [None, None]]
    far = [(d, None) for d in range(half + 1, tok_count - 1)] + [(tok_count - 1, 0), (tok_count - 1, 1)]
    for at, block in enumerate(far):
        far_steps.append([block, None] if at % 2 == 0 else [None, block])
    far_steps += [[("wait", None), None], [None, ("wait", None)]]
    near = list(range(1, half))
    near_steps = [near[:2], []] + [[d] for d in near[2:]]
    relayed = set()

    def rides(d):
        return d & (d - 1) == 0 and d < half // 2

    def bits_below(d):
        if d == 0:
            return [half // 2]
        return [1 << i for i in range((d & -d).bit_length() - 1)]


    lanes_before = [None, None]
    near_before, relay_before, cross_before, core_before = [], [], None, None
    crossed = []
    gradients = [None, None]
    done = set()

    def finish_core():
        nonlocal core_before
        if core_before is not None:
            units, both = core_before
            core_before = None
            to = 0
            for blocks, own, other in units:
                total = sum(pieces[i][1] for _, i, _, _ in blocks)
                at = 0
                for d, i, _, _ in blocks:
                    lefts[d, i] = {
                        0: (own, at),
                        across: (other, at),
                        core: (both, to + at),
                        across ^ core: (both, to + total + at),
                    }
                    at += pieces[i][1]
                to += 2 * total

    def finish_relays(step):
        arrived = []
        for entry in list(relay_before):
            due, bit, sources, array = entry
            if due <= step:
                relay_before.remove(entry)
                arrived.append(array)
                for at, d in enumerate(sources):
                    cots[d + bit] = cots_at(array, at * model_width)
        return arrived

    def add_products(i):
        width = pieces[i][1]
        here = [d for d in range(tok_count) if d in cots and (d, i) in lefts and (d, i) not in done]
        if not here:
            return
        done.update((d, i) for d in here)
        full = all((d, i) in done for d in range(tok_count))
        out = product(
            [[lefts[d, i][s] for d in here] for s in slots],
            [[cots[d][s] for d in here] for s in slots],
            width,
            columns,
            held=gradients[i][0] if gradients[i] else None,
            sums=gradients[0][1] if full and i == 1 else None,
            copies=0 if not full else tok_count * user_count if i == 1 else 1,
            after=tick[:1] if not full else [],
        )
        gradients[i] = out
        tick.append(out[0])

    for step in range(len(far_steps) + 1):
        flying = 0
        now = far_steps[step] if step < len(far_steps) else [None, None]
        for lane in (0, 1):
            if lane == 1 and now[1] == ("cots", None):
                continue
            if now[lane] is not None:
                after = []
                if lanes_before[lane] is not None:
                    (d, i), array = lanes_before[lane]
                    lanes_before[lane] = None
                    after.append(array)
                    if d == "cots":
                        cots[half] = cots_at(array, 0)
                    else:
                        first = pieces[i][0] if i is not None else 0
                        ready += [
                            (d, j, array, at - first) for j, (at, _) in enumerate(pieces) if i is None or i == j
                        ]
                d, i = now[lane]
                if d != "wait":
                    first, width = pieces[i] if i is not None else (0, own_width)
                    array = send("tok", d, [(outgoing[d], first, width)], after)[1]
                    lanes_before[lane] = (now[lane], array)
            flying += lanes_before[lane] is not None
        for entry in list(near_before):
            due, d, array = entry
            if due > step:
                flying += 1
                continue
            near_before.remove(entry)
            ready += [(d, i, array, first) for i, (first, _) in enumerate(pieces)]
            if rides(d):
                cots[d] = cots_at(array, own_width)
        arrivals = finish_relays(step)
        if cross_before is not None:
            crossed.append(cross_before)
        earlier = [cross_before[2]] if cross_before is not None else []
        earlier += [core_before[1]] if core_before is not None else []
        cross_before = None
        if ready:
            blocks = []
            while ready and sum(pieces[i][1] for _, i, _, _ in blocks) < 2 * own_width:
                blocks.append(ready.pop(0))
            parts = [(array, first, pieces[i][1]) for _, i, array, first in blocks]
            own, other = send("user", across, parts, earlier)
            earlier = []
            cross_before = (blocks, own, other)
            flying += 1
        bit, sent = half // 2, False
        while bit:
            sources = [d for d in sorted(cots) if bit in bits_below(d) and d + bit not in relayed]
            if sources and step > 0 and (step > 5 or (flying < 5 and not sent)):
                relayed.update(d + bit for d in sources)
                parts = [part for d in sources for part in cot_parts(d)]
                relay_before.append((step + (1 if step < 3 else 2), bit, sources, send("tok", bit, parts, earlier)[1]))
                earlier = []
                flying += 1
                sent = True
            bit //= 2
        if step == 0:
            cots[0] = [(block, 0) for block in by_slot]
            cots[0] = cots_at(join(cot_parts(0), tick), 0)
            lanes_before[1] = (("cots", None), send("tok", half, cot_parts(0))[1])
            flying += 1
        if step < len(near_steps):
            for d in near_steps[step]:
                parts = [(outgoing[d], 0, own_width)]
                if rides(d):
                    parts += cot_parts(0)
                near_before.append((step + (3 if step else 1), d, send("tok", d, parts)[1]))
                flying += 1
        before = [core_before[1]] if core_before else []
        finish_core()
        if crossed and (flying < 5 or step >= len(far_steps) - 3):
            parts = []
            for blocks, own, other in crossed:
                total = sum(pieces[i][1] for _, i, _, _ in blocks)
                parts += [(own, 0, total), (other, 0, total)]
            core_before = (list(crossed), send("user", core, parts, before)[1])
            crossed.clear()
            flying += 1
        if step < len(far_steps):
            tick[:] = [hold(tick[0], arrivals + earlier, max(sizes))]
            sizes[:] = [0]
        if step == len(far_steps) - 3:
            add_products(0)
            add_products(1)
        elif step == len(far_steps) - 1:
            finish_core()
            add_products(0)
    finish_core()
    add_products(0)
    add_products(1)
    sums = lax.all_to_all(gradients[1][1], ("user", "tok"), split_axis=0, concat_axis=0, tiled=True)
    return combine(user, sums, [g[0] for g in gradients], clip_bound, scaling)


def solution(mesh):
    return jax.shard_map(
        body,
        mesh=mesh,
        in_specs=(P("user", "tok", None), P("user", "tok", None), P("user")),
        out_specs=P("tok", "user"),
        check_vma=False,
    )
```

```python
import functools
import math

import jax
import jax.numpy as jnp
from jax import lax
from jax.experimental import pallas as pl
from jax.experimental.pallas import tpu as pltpu
from jax.sharding import PartitionSpec as P

epsilon = 1e-06
lanes = 128
first_part = 0.5
dear = 24 * 10**10
dear_per_byte = 2 * 10**5
ANY = pl.BlockSpec(memory_space=pl.ANY)
SMEM = pl.BlockSpec(memory_space=pltpu.SMEM)
VMEM = pl.BlockSpec(memory_space=pltpu.VMEM)
HBM = pl.BlockSpec(memory_space=pltpu.HBM)


def exchange(block, axis, distance):
    size = lax.axis_size(axis)
    return lax.ppermute(block, axis, [(i, i ^ distance) for i in range(size)])


def pack_kernel(distances, tok_ref, hidden_ref, *refs):
    out_refs, sems = refs[-1 - len(distances) : -1], refs[-1]
    width = out_refs[0].shape[1]
    copies = []
    for at, distance in enumerate(distances):
        start = pl.multiple_of((tok_ref[0] ^ distance) * width, lanes)
        copies.append(
            pltpu.make_async_copy(
                hidden_ref.at[0, :, pl.ds(start, width)], out_refs[at], sems.at[at]
            )
        )
    for copy in copies:
        copy.start()
    for copy in copies:
        copy.wait()


def pack(tok, hidden, distances, width, after):
    rows = hidden.shape[1]
    count = len(distances)
    return pl.pallas_call(
        functools.partial(pack_kernel, distances),
        out_shape=[jax.ShapeDtypeStruct((rows, width), hidden.dtype)] * count,
        in_specs=[SMEM, HBM] + [ANY] * len(after),
        out_specs=[VMEM] * count,
        scratch_shapes=[pltpu.SemaphoreType.DMA((count,))],
        compiler_params=pltpu.CompilerParams(vmem_limit_bytes=2**20),
        cost_estimate=pl.CostEstimate(
            flops=0, bytes_accessed=4 * count * rows * width, transcendentals=0
        ),
        name="pack_columns",
    )(tok, hidden, *after)


def join_kernel(parts, *refs):
    out_ref = refs[-1]
    to = 0
    for at, start, width in parts:
        out_ref[:, to : to + width] = refs[at][:, start : start + width]
        to += width


def join(parts, after):
    arrays, places = [], []
    for array, start, width in parts:
        at = [i for i, other in enumerate(arrays) if other is array]
        if not at:
            arrays.append(array)
        places.append((at[0] if at else len(arrays) - 1, start, width))
    after = [array for array in after if not any(array is other for other in arrays)]
    rows = arrays[0].shape[0]
    total = sum(width for _, _, width in parts)
    return pl.pallas_call(
        functools.partial(join_kernel, places),
        out_shape=jax.ShapeDtypeStruct((rows, total), arrays[0].dtype),
        in_specs=[VMEM] * len(arrays) + [ANY] * len(after),
        out_specs=VMEM,
        compiler_params=pltpu.CompilerParams(vmem_limit_bytes=max(2**20, 8 * rows * total - 2**24)),
        cost_estimate=pl.CostEstimate(flops=0, bytes_accessed=4 * rows * total, transcendentals=0),
        name="join_columns",
    )(*arrays, *after)


def hold_kernel(*refs):
    out_ref = refs[-1]
    out_ref[...] = jnp.zeros_like(out_ref)


def hold(message, after, size):
    return pl.pallas_call(
        hold_kernel,
        out_shape=jax.ShapeDtypeStruct((16, lanes), message.dtype),
        in_specs=[ANY] * (1 + len(after)),
        out_specs=VMEM,
        cost_estimate=pl.CostEstimate(flops=max(dear, dear_per_byte * size) // lax.axis_size("tok"), bytes_accessed=0, transcendentals=0),
        compiler_params=pltpu.CompilerParams(vmem_limit_bytes=2**20),
        name="hold",
    )(message, *after)


def mask_kernel(valid_ref, user_ref, cot_ref, *out_refs):
    rows, width = out_refs[0].shape
    keep = lax.broadcasted_iota(jnp.int32, (rows, width), 0) < valid_ref[0]
    for slot, out_ref in enumerate(out_refs):
        column = pl.multiple_of((user_ref[0] ^ slot) * width, lanes)
        block = cot_ref[0, :, pl.ds(column, width)]
        out_ref[...] = jnp.where(keep, block, jnp.zeros_like(block))


def mask(valid, user, cotangent, user_count):
    _, rows, total = cotangent.shape
    return pl.pallas_call(
        mask_kernel,
        out_shape=[jax.ShapeDtypeStruct((rows, total // user_count), cotangent.dtype)] * user_count,
        in_specs=[SMEM, SMEM, VMEM],
        out_specs=[VMEM] * user_count,
        compiler_params=pltpu.CompilerParams(vmem_limit_bytes=2 * 2**20),
        name="mask_cotangent",
    )(valid, user, cotangent)


def product_kernel(lefts, rights, tile, has_held, has_sums, copies, *refs):
    outs = refs[-2:] if copies else refs[-1:]
    inputs = list(refs[: -len(outs)])
    sums_in = inputs.pop() if has_sums else None
    held_ref = inputs.pop() if has_held else None
    product_ref = outs[0]
    user_count, width, columns = product_ref.shape
    squares = []
    for slot in range(user_count):
        right = jnp.concatenate(
            [refs[at][:, start : start + columns] for at, start in rights[slot]], axis=0
        )

        def step(i, total, slot=slot, right=right):
            rows = pl.ds(pl.multiple_of(i * tile, tile), tile)
            left = jnp.concatenate(
                [
                    refs[at][:, pl.ds(pl.multiple_of(start + i * tile, lanes), tile)]
                    for at, start in lefts[slot]
                ],
                axis=0,
            )
            value = lax.dot_general(
                left, right, (((0,), (0,)), ((), ())), preferred_element_type=jnp.float32
            )
            if has_held:
                value += held_ref[slot, rows, :]
            product_ref[slot, rows, :] = value
            if copies:
                row = jnp.sum(value * value, axis=0, keepdims=True)
                for start in range(0, columns, lanes):
                    total += row[:, start : start + lanes]
            return total

        squares.append(lax.fori_loop(0, width // tile, step, jnp.zeros((1, lanes), jnp.float32)))
    if copies:
        rows = jnp.concatenate(squares + [jnp.zeros((8 - user_count, lanes), jnp.float32)], axis=0)
        if has_sums:
            rows += sums_in[0]
        outs[1][...] = jnp.broadcast_to(rows[None], outs[1].shape)


def product(lefts, rights, width, columns, held=None, sums=None, copies=0, after=()):
    operands, at = [], {}

    def place(part):
        array, start = part
        if id(array) not in at:
            at[id(array)] = len(operands)
            operands.append(array)
        return at[id(array)], start

    user_count, sources = len(lefts), len(lefts[0])
    left_places = [[place(part) for part in slot] for slot in lefts]
    right_places = [[place(part) for part in slot] for slot in rights]
    tokens = sources * lefts[0][0][0].shape[0]
    blocks = len(operands)
    operands += [array for array in after if id(array) not in at and array is not held]
    waits = len(operands) - blocks
    aliases = {}
    if held is not None:
        aliases = {len(operands): 0}
        operands.append(held)
    if sums is not None:
        operands.append(sums)
    out_shape = [jax.ShapeDtypeStruct((user_count, width, columns), jnp.float32)]
    if copies:
        out_shape.append(jax.ShapeDtypeStruct((copies, 8, lanes), jnp.float32))
    tile = math.gcd(width, 2 * lanes)
    return pl.pallas_call(
        functools.partial(
            product_kernel, left_places, right_places, tile, held is not None, sums is not None, copies
        ),
        out_shape=out_shape,
        in_specs=[VMEM] * blocks + [ANY] * waits + [VMEM] * (len(operands) - blocks - waits),
        out_specs=[VMEM] * len(out_shape),
        input_output_aliases=aliases,
        compiler_params=pltpu.CompilerParams(vmem_limit_bytes=8 * 2**20),
        cost_estimate=pl.CostEstimate(
            flops=2 * user_count * tokens * columns * width,
            bytes_accessed=2 * user_count * tokens * (width + columns),
            transcendentals=0,
        ),
        name="product_and_squares",
    )(*operands)


def combine_kernel(user_count, clip_bound, scaling, starts, user_ref, sums_ref, *refs):
    out_ref, factor_ref = refs[-2:]

    @pl.when(pl.program_id(0) == 0)
    def _():
        per_user = sums_ref.shape[0] // user_count
        by_source = [
            jnp.sum(sums_ref[j * per_user : (j + 1) * per_user], axis=0) for j in range(user_count)
        ]
        factors = []
        for u in range(user_count):
            row = sum(by_source[j][j ^ u : (j ^ u) + 1, :] for j in range(user_count))
            norm_sq = jnp.sum(row, axis=1, keepdims=True)
            factors.append(jnp.minimum(1.0, clip_bound / jnp.sqrt(norm_sq + epsilon)) * scaling)
        for slot in range(user_count):
            user = user_ref[0] ^ slot
            factor = sum(jnp.where(user == u, factors[u], 0.0) for u in range(user_count))
            factor_ref[slot : slot + 1, :] = jnp.broadcast_to(factor, (1, lanes))

    by_slot = [factor_ref[slot : slot + 1, 0:1] for slot in range(user_count)]
    tile = out_ref.shape[0]
    row = pl.program_id(0) * tile
    for ref, start in zip(refs, starts):

        @pl.when((row >= start) & (row < start + ref.shape[1]))
        def _(ref=ref, start=start):
            at = pl.ds(pl.multiple_of(row - start, tile), tile)
            result = by_slot[0] * ref[0, at, :]
            for slot in range(1, user_count):
                result += by_slot[slot] * ref[slot, at, :]
            out_ref[...] = result


def combine(user, sums, gradients, clip_bound, scaling):
    user_count, _, columns = gradients[0].shape
    heights = [gradient.shape[1] for gradient in gradients]
    starts = [sum(heights[:i]) for i in range(len(heights))]
    rows = sum(heights)
    tile = math.gcd(256, *heights)
    return pl.pallas_call(
        functools.partial(combine_kernel, user_count, clip_bound, scaling, starts),
        grid=(rows // tile,),
        out_shape=jax.ShapeDtypeStruct((rows, columns), jnp.float32),
        in_specs=[SMEM] + [VMEM] * (1 + len(gradients)),
        out_specs=pl.BlockSpec((tile, columns), lambda i: (i, 0)),
        scratch_shapes=[pltpu.VMEM((8, lanes), jnp.float32)],
        compiler_params=pltpu.CompilerParams(vmem_limit_bytes=8 * 2**20),
        name="weighted_sum",
    )(user, sums, *gradients)


def body(hidden, cotangent, lengths):
    tok_count = lax.axis_size("tok")
    user_count = lax.axis_size("user")
    tok_rows = hidden.shape[1]
    hidden_width = hidden.shape[2]
    model_width = cotangent.shape[2]
    capacity = tok_rows * tok_count
    own_width = hidden_width // tok_count
    columns = model_width // user_count
    clip_bound = math.sqrt(8.0 * hidden_width * model_width * capacity)
    scaling = math.sqrt(hidden_width * model_width) / (user_count * clip_bound)
    user = lax.axis_index("user").astype(jnp.int32).reshape(1)
    tok = lax.axis_index("tok").astype(jnp.int32).reshape(1)
    valid = lengths - tok * tok_rows
    half = tok_count // 2
    across, core = user_count // 2, user_count // 4
    slots = range(user_count)
    cut = round(own_width // lanes * first_part) * lanes
    pieces = [(0, cut), (cut, own_width - cut)]

    cots = {}
    lefts = {}
    ready = []
    tick = []

    sizes = [0]

    def send(axis, distance, parts, after=()):
        message = join(parts, [*tick, *after])
        sizes.append(2 * message.size)
        tick[:] = [message]
        return message, exchange(message, axis, distance)

    def cot_parts(d):
        return [(*cots[d][s], columns) for s in slots]

    def cots_at(array, start):
        return [(array, start + s * columns) for s in slots]

    masked = mask(valid, user, cotangent, user_count)
    by_slot = [masked[0]] + [exchange(masked[s], "user", s) for s in range(1, user_count)]
    outgoing = pack(tok, hidden, list(range(tok_count)), own_width, [])
    ready += [(0, i, outgoing[0], start) for i, (start, _) in enumerate(pieces)]

    far_steps = [[(half, None), ("cots", None)], [None, None]]
    far = [(d, None) for d in range(half + 1, tok_count - 1)] + [(tok_count - 1, 0), (tok_count - 1, 1)]
    for at, block in enumerate(far):
        far_steps.append([block, None] if at % 2 == 0 else [None, block])
    far_steps += [[("wait", None), None], [None, ("wait", None)]]
    near = list(range(1, half))
    near_steps = [near[:2], []] + [[d] for d in near[2:]]
    relayed = set()

    def rides(d):
        return d & (d - 1) == 0 and d < half // 2

    def bits_below(d):
        if d == 0:
            return [half // 2]
        return [1 << i for i in range((d & -d).bit_length() - 1)]


    lanes_before = [None, None]
    near_before, relay_before, cross_before, core_before = [], [], None, None
    crossed = []
    gradients = [None, None]
    done = set()

    def finish_core():
        nonlocal core_before
        if core_before is not None:
            units, both = core_before
            core_before = None
            to = 0
            for blocks, own, other in units:
                total = sum(pieces[i][1] for _, i, _, _ in blocks)
                at = 0
                for d, i, _, _ in blocks:
                    lefts[d, i] = {
                        0: (own, at),
                        across: (other, at),
                        core: (both, to + at),
                        across ^ core: (both, to + total + at),
                    }
                    at += pieces[i][1]
                to += 2 * total

    def finish_relays(step):
        arrived = []
        for entry in list(relay_before):
            due, bit, sources, array = entry
            if due <= step:
                relay_before.remove(entry)
                arrived.append(array)
                for at, d in enumerate(sources):
                    cots[d + bit] = cots_at(array, at * model_width)
        return arrived

    def add_products(i):
        width = pieces[i][1]
        here = [d for d in range(tok_count) if d in cots and (d, i) in lefts and (d, i) not in done]
        if not here:
            return
        done.update((d, i) for d in here)
        full = all((d, i) in done for d in range(tok_count))
        out = product(
            [[lefts[d, i][s] for d in here] for s in slots],
            [[cots[d][s] for d in here] for s in slots],
            width,
            columns,
            held=gradients[i][0] if gradients[i] else None,
            sums=gradients[0][1] if full and i == 1 else None,
            copies=0 if not full else tok_count * user_count if i == 1 else 1,
            after=tick[:1] if not full else [],
        )
        gradients[i] = out
        tick.append(out[0])

    for step in range(len(far_steps) + 1):
        flying = 0
        now = far_steps[step] if step < len(far_steps) else [None, None]
        for lane in (0, 1):
            if lane == 1 and now[1] == ("cots", None):
                continue
            if now[lane] is not None:
                after = []
                if lanes_before[lane] is not None:
                    (d, i), array = lanes_before[lane]
                    lanes_before[lane] = None
                    after.append(array)
                    if d == "cots":
                        cots[half] = cots_at(array, 0)
                    else:
                        first = pieces[i][0] if i is not None else 0
                        ready += [
                            (d, j, array, at - first) for j, (at, _) in enumerate(pieces) if i is None or i == j
                        ]
                d, i = now[lane]
                if d != "wait":
                    first, width = pieces[i] if i is not None else (0, own_width)
                    array = send("tok", d, [(outgoing[d], first, width)], after)[1]
                    lanes_before[lane] = (now[lane], array)
            flying += lanes_before[lane] is not None
        for entry in list(near_before):
            due, d, array = entry
            if due > step:
                flying += 1
                continue
            near_before.remove(entry)
            ready += [(d, i, array, first) for i, (first, _) in enumerate(pieces)]
            if rides(d):
                cots[d] = cots_at(array, own_width)
        arrivals = finish_relays(step)
        if cross_before is not None:
            crossed.append(cross_before)
        earlier = [cross_before[2]] if cross_before is not None else []
        earlier += [core_before[1]] if core_before is not None else []
        cross_before = None
        if ready:
            blocks = []
            while ready and sum(pieces[i][1] for _, i, _, _ in blocks) < 2 * own_width:
                blocks.append(ready.pop(0))
            parts = [(array, first, pieces[i][1]) for _, i, array, first in blocks]
            own, other = send("user", across, parts, earlier)
            earlier = []
            cross_before = (blocks, own, other)
            flying += 1
        bit, sent = half // 2, False
        while bit:
            sources = [d for d in sorted(cots) if bit in bits_below(d) and d + bit not in relayed]
            if sources and step > 0 and (step > 5 or (flying < 5 and not sent)):
                relayed.update(d + bit for d in sources)
                parts = [part for d in sources for part in cot_parts(d)]
                relay_before.append((step + (1 if step < 3 else 2), bit, sources, send("tok", bit, parts, earlier)[1]))
                earlier = []
                flying += 1
                sent = True
            bit //= 2
        if step == 0:
            cots[0] = [(block, 0) for block in by_slot]
            cots[0] = cots_at(join(cot_parts(0), tick), 0)
            lanes_before[1] = (("cots", None), send("tok", half, cot_parts(0))[1])
            flying += 1
        if step < len(near_steps):
            for d in near_steps[step]:
                parts = [(outgoing[d], 0, own_width)]
                if rides(d):
                    parts += cot_parts(0)
                near_before.append((step + (3 if step else 1), d, send("tok", d, parts)[1]))
                flying += 1
        before = [core_before[1]] if core_before else []
        finish_core()
        if crossed and (flying < 5 or step >= len(far_steps) - 3):
            parts = []
            for blocks, own, other in crossed:
                total = sum(pieces[i][1] for _, i, _, _ in blocks)
                parts += [(own, 0, total), (other, 0, total)]
            core_before = (list(crossed), send("user", core, parts, before)[1])
            crossed.clear()
            flying += 1
        if step < len(far_steps):
            tick[:] = [hold(tick[0], arrivals + earlier, max(sizes))]
            sizes[:] = [0]
        if step == len(far_steps) - 3:
            add_products(0)
        elif step == len(far_steps) - 2:
            add_products(1)
        elif step == len(far_steps) - 1:
            finish_core()
            add_products(0)
    finish_core()
    add_products(0)
    add_products(1)
    sums = lax.all_to_all(gradients[1][1], ("user", "tok"), split_axis=0, concat_axis=0, tiled=True)
    return combine(user, sums, [g[0] for g in gradients], clip_bound, scaling)


def solution(mesh):
    return jax.shard_map(
        body,
        mesh=mesh,
        in_specs=(P("user", "tok", None), P("user", "tok", None), P("user")),
        out_specs=P("tok", "user"),
        check_vma=False,
    )
```

```python
import functools
import math

import jax
import jax.numpy as jnp
from jax import lax
from jax.experimental import pallas as pl
from jax.experimental.pallas import tpu as pltpu
from jax.sharding import PartitionSpec as P

epsilon = 1e-06
lanes = 128
first_part = 0.5
dear = 24 * 10**10
dear_per_byte = 2 * 10**5
ANY = pl.BlockSpec(memory_space=pl.ANY)
SMEM = pl.BlockSpec(memory_space=pltpu.SMEM)
VMEM = pl.BlockSpec(memory_space=pltpu.VMEM)
HBM = pl.BlockSpec(memory_space=pltpu.HBM)


def exchange(block, axis, distance):
    size = lax.axis_size(axis)
    return lax.ppermute(block, axis, [(i, i ^ distance) for i in range(size)])


def pack_kernel(distances, tok_ref, hidden_ref, *refs):
    out_refs, sems = refs[-1 - len(distances) : -1], refs[-1]
    width = out_refs[0].shape[1]
    copies = []
    for at, distance in enumerate(distances):
        start = pl.multiple_of((tok_ref[0] ^ distance) * width, lanes)
        copies.append(
            pltpu.make_async_copy(
                hidden_ref.at[0, :, pl.ds(start, width)], out_refs[at], sems.at[at]
            )
        )
    for copy in copies:
        copy.start()
    for copy in copies:
        copy.wait()


def pack(tok, hidden, distances, width, after):
    rows = hidden.shape[1]
    count = len(distances)
    return pl.pallas_call(
        functools.partial(pack_kernel, distances),
        out_shape=[jax.ShapeDtypeStruct((rows, width), hidden.dtype)] * count,
        in_specs=[SMEM, HBM] + [ANY] * len(after),
        out_specs=[VMEM] * count,
        scratch_shapes=[pltpu.SemaphoreType.DMA((count,))],
        compiler_params=pltpu.CompilerParams(vmem_limit_bytes=2**20),
        cost_estimate=pl.CostEstimate(
            flops=0, bytes_accessed=4 * count * rows * width, transcendentals=0
        ),
        name="pack_columns",
    )(tok, hidden, *after)


def join_kernel(parts, *refs):
    out_ref = refs[-1]
    to = 0
    for at, start, width in parts:
        out_ref[:, to : to + width] = refs[at][:, start : start + width]
        to += width


def join(parts, after):
    arrays, places = [], []
    for array, start, width in parts:
        at = [i for i, other in enumerate(arrays) if other is array]
        if not at:
            arrays.append(array)
        places.append((at[0] if at else len(arrays) - 1, start, width))
    after = [array for array in after if not any(array is other for other in arrays)]
    rows = arrays[0].shape[0]
    total = sum(width for _, _, width in parts)
    return pl.pallas_call(
        functools.partial(join_kernel, places),
        out_shape=jax.ShapeDtypeStruct((rows, total), arrays[0].dtype),
        in_specs=[VMEM] * len(arrays) + [ANY] * len(after),
        out_specs=VMEM,
        compiler_params=pltpu.CompilerParams(vmem_limit_bytes=max(2**20, 8 * rows * total - 2**24)),
        cost_estimate=pl.CostEstimate(flops=0, bytes_accessed=4 * rows * total, transcendentals=0),
        name="join_columns",
    )(*arrays, *after)


def hold_kernel(*refs):
    out_ref = refs[-1]
    out_ref[...] = jnp.zeros_like(out_ref)


def hold(message, after, size):
    return pl.pallas_call(
        hold_kernel,
        out_shape=jax.ShapeDtypeStruct((16, lanes), message.dtype),
        in_specs=[ANY] * (1 + len(after)),
        out_specs=VMEM,
        cost_estimate=pl.CostEstimate(flops=max(dear, dear_per_byte * size) // lax.axis_size("tok"), bytes_accessed=0, transcendentals=0),
        compiler_params=pltpu.CompilerParams(vmem_limit_bytes=2**20),
        name="hold",
    )(message, *after)


def mask_kernel(valid_ref, user_ref, cot_ref, *out_refs):
    rows, width = out_refs[0].shape
    keep = lax.broadcasted_iota(jnp.int32, (rows, width), 0) < valid_ref[0]
    for slot, out_ref in enumerate(out_refs):
        column = pl.multiple_of((user_ref[0] ^ slot) * width, lanes)
        block = cot_ref[0, :, pl.ds(column, width)]
        out_ref[...] = jnp.where(keep, block, jnp.zeros_like(block))


def mask(valid, user, cotangent, user_count):
    _, rows, total = cotangent.shape
    return pl.pallas_call(
        mask_kernel,
        out_shape=[jax.ShapeDtypeStruct((rows, total // user_count), cotangent.dtype)] * user_count,
        in_specs=[SMEM, SMEM, VMEM],
        out_specs=[VMEM] * user_count,
        compiler_params=pltpu.CompilerParams(vmem_limit_bytes=2 * 2**20),
        name="mask_cotangent",
    )(valid, user, cotangent)


def product_kernel(lefts, rights, tile, has_held, has_sums, copies, *refs):
    outs = refs[-2:] if copies else refs[-1:]
    inputs = list(refs[: -len(outs)])
    sums_in = inputs.pop() if has_sums else None
    held_ref = inputs.pop() if has_held else None
    product_ref = outs[0]
    user_count, width, columns = product_ref.shape
    squares = []
    for slot in range(user_count):
        right = jnp.concatenate(
            [refs[at][:, start : start + columns] for at, start in rights[slot]], axis=0
        )

        def step(i, total, slot=slot, right=right):
            rows = pl.ds(pl.multiple_of(i * tile, tile), tile)
            left = jnp.concatenate(
                [
                    refs[at][:, pl.ds(pl.multiple_of(start + i * tile, lanes), tile)]
                    for at, start in lefts[slot]
                ],
                axis=0,
            )
            value = lax.dot_general(
                left, right, (((0,), (0,)), ((), ())), preferred_element_type=jnp.float32
            )
            if has_held:
                value += held_ref[slot, rows, :]
            product_ref[slot, rows, :] = value
            if copies:
                row = jnp.sum(value * value, axis=0, keepdims=True)
                for start in range(0, columns, lanes):
                    total += row[:, start : start + lanes]
            return total

        squares.append(lax.fori_loop(0, width // tile, step, jnp.zeros((1, lanes), jnp.float32)))
    if copies:
        rows = jnp.concatenate(squares + [jnp.zeros((8 - user_count, lanes), jnp.float32)], axis=0)
        if has_sums:
            rows += sums_in[0]
        outs[1][...] = jnp.broadcast_to(rows[None], outs[1].shape)


def product(lefts, rights, width, columns, held=None, sums=None, copies=0, after=()):
    operands, at = [], {}

    def place(part):
        array, start = part
        if id(array) not in at:
            at[id(array)] = len(operands)
            operands.append(array)
        return at[id(array)], start

    user_count, sources = len(lefts), len(lefts[0])
    left_places = [[place(part) for part in slot] for slot in lefts]
    right_places = [[place(part) for part in slot] for slot in rights]
    tokens = sources * lefts[0][0][0].shape[0]
    blocks = len(operands)
    operands += [array for array in after if id(array) not in at and array is not held]
    waits = len(operands) - blocks
    aliases = {}
    if held is not None:
        aliases = {len(operands): 0}
        operands.append(held)
    if sums is not None:
        operands.append(sums)
    out_shape = [jax.ShapeDtypeStruct((user_count, width, columns), jnp.float32)]
    if copies:
        out_shape.append(jax.ShapeDtypeStruct((copies, 8, lanes), jnp.float32))
    tile = math.gcd(width, 2 * lanes)
    return pl.pallas_call(
        functools.partial(
            product_kernel, left_places, right_places, tile, held is not None, sums is not None, copies
        ),
        out_shape=out_shape,
        in_specs=[VMEM] * blocks + [ANY] * waits + [VMEM] * (len(operands) - blocks - waits),
        out_specs=[VMEM] * len(out_shape),
        input_output_aliases=aliases,
        compiler_params=pltpu.CompilerParams(vmem_limit_bytes=8 * 2**20),
        cost_estimate=pl.CostEstimate(
            flops=2 * user_count * tokens * columns * width,
            bytes_accessed=2 * user_count * tokens * (width + columns),
            transcendentals=0,
        ),
        name="product_and_squares",
    )(*operands)


def combine_kernel(user_count, clip_bound, scaling, starts, user_ref, sums_ref, *refs):
    out_ref, factor_ref = refs[-2:]

    @pl.when(pl.program_id(0) == 0)
    def _():
        per_user = sums_ref.shape[0] // user_count
        by_source = [
            jnp.sum(sums_ref[j * per_user : (j + 1) * per_user], axis=0) for j in range(user_count)
        ]
        factors = []
        for u in range(user_count):
            row = sum(by_source[j][j ^ u : (j ^ u) + 1, :] for j in range(user_count))
            norm_sq = jnp.sum(row, axis=1, keepdims=True)
            factors.append(jnp.minimum(1.0, clip_bound / jnp.sqrt(norm_sq + epsilon)) * scaling)
        for slot in range(user_count):
            user = user_ref[0] ^ slot
            factor = sum(jnp.where(user == u, factors[u], 0.0) for u in range(user_count))
            factor_ref[slot : slot + 1, :] = jnp.broadcast_to(factor, (1, lanes))

    by_slot = [factor_ref[slot : slot + 1, 0:1] for slot in range(user_count)]
    tile = out_ref.shape[0]
    row = pl.program_id(0) * tile
    for ref, start in zip(refs, starts):

        @pl.when((row >= start) & (row < start + ref.shape[1]))
        def _(ref=ref, start=start):
            at = pl.ds(pl.multiple_of(row - start, tile), tile)
            result = by_slot[0] * ref[0, at, :]
            for slot in range(1, user_count):
                result += by_slot[slot] * ref[slot, at, :]
            out_ref[...] = result


def combine(user, sums, gradients, clip_bound, scaling):
    user_count, _, columns = gradients[0].shape
    heights = [gradient.shape[1] for gradient in gradients]
    starts = [sum(heights[:i]) for i in range(len(heights))]
    rows = sum(heights)
    tile = math.gcd(512, *heights)
    return pl.pallas_call(
        functools.partial(combine_kernel, user_count, clip_bound, scaling, starts),
        grid=(rows // tile,),
        out_shape=jax.ShapeDtypeStruct((rows, columns), jnp.float32),
        in_specs=[SMEM] + [VMEM] * (1 + len(gradients)),
        out_specs=pl.BlockSpec((tile, columns), lambda i: (i, 0)),
        scratch_shapes=[pltpu.VMEM((8, lanes), jnp.float32)],
        compiler_params=pltpu.CompilerParams(vmem_limit_bytes=8 * 2**20),
        name="weighted_sum",
    )(user, sums, *gradients)


def body(hidden, cotangent, lengths):
    tok_count = lax.axis_size("tok")
    user_count = lax.axis_size("user")
    tok_rows = hidden.shape[1]
    hidden_width = hidden.shape[2]
    model_width = cotangent.shape[2]
    capacity = tok_rows * tok_count
    own_width = hidden_width // tok_count
    columns = model_width // user_count
    clip_bound = math.sqrt(8.0 * hidden_width * model_width * capacity)
    scaling = math.sqrt(hidden_width * model_width) / (user_count * clip_bound)
    user = lax.axis_index("user").astype(jnp.int32).reshape(1)
    tok = lax.axis_index("tok").astype(jnp.int32).reshape(1)
    valid = lengths - tok * tok_rows
    half = tok_count // 2
    across, core = user_count // 2, user_count // 4
    slots = range(user_count)
    cut = round(own_width // lanes * first_part) * lanes
    pieces = [(0, cut), (cut, own_width - cut)]

    cots = {}
    lefts = {}
    ready = []
    tick = []

    sizes = [0]

    def send(axis, distance, parts, after=()):
        message = join(parts, [*tick, *after])
        sizes.append(2 * message.size)
        tick[:] = [message]
        return message, exchange(message, axis, distance)

    def cot_parts(d):
        return [(*cots[d][s], columns) for s in slots]

    def cots_at(array, start):
        return [(array, start + s * columns) for s in slots]

    masked = mask(valid, user, cotangent, user_count)
    by_slot = [masked[0]] + [exchange(masked[s], "user", s) for s in range(1, user_count)]
    outgoing = pack(tok, hidden, list(range(tok_count)), own_width, [])
    ready += [(0, i, outgoing[0], start) for i, (start, _) in enumerate(pieces)]

    far_steps = [[(half, None), ("cots", None)], [None, None]]
    far = [(d, None) for d in range(half + 1, tok_count - 1)] + [(tok_count - 1, 0), (tok_count - 1, 1)]
    for at, block in enumerate(far):
        far_steps.append([block, None] if at % 2 == 0 else [None, block])
    far_steps += [[("wait", None), None], [None, ("wait", None)]]
    near = list(range(1, half))
    near_steps = [near[:2], []] + [[d] for d in near[2:]]
    relayed = set()

    def rides(d):
        return d & (d - 1) == 0 and d < half // 2

    def bits_below(d):
        if d == 0:
            return [half // 2]
        return [1 << i for i in range((d & -d).bit_length() - 1)]


    lanes_before = [None, None]
    near_before, relay_before, cross_before, core_before = [], [], None, None
    crossed = []
    gradients = [None, None]
    done = set()

    def finish_core():
        nonlocal core_before
        if core_before is not None:
            units, both = core_before
            core_before = None
            to = 0
            for blocks, own, other in units:
                total = sum(pieces[i][1] for _, i, _, _ in blocks)
                at = 0
                for d, i, _, _ in blocks:
                    lefts[d, i] = {
                        0: (own, at),
                        across: (other, at),
                        core: (both, to + at),
                        across ^ core: (both, to + total + at),
                    }
                    at += pieces[i][1]
                to += 2 * total

    def finish_relays(step):
        arrived = []
        for entry in list(relay_before):
            due, bit, sources, array = entry
            if due <= step:
                relay_before.remove(entry)
                arrived.append(array)
                for at, d in enumerate(sources):
                    cots[d + bit] = cots_at(array, at * model_width)
        return arrived

    def add_products(i):
        width = pieces[i][1]
        here = [d for d in range(tok_count) if d in cots and (d, i) in lefts and (d, i) not in done]
        if not here:
            return
        done.update((d, i) for d in here)
        full = all((d, i) in done for d in range(tok_count))
        out = product(
            [[lefts[d, i][s] for d in here] for s in slots],
            [[cots[d][s] for d in here] for s in slots],
            width,
            columns,
            held=gradients[i][0] if gradients[i] else None,
            sums=gradients[0][1] if full and i == 1 else None,
            copies=0 if not full else tok_count * user_count if i == 1 else 1,
            after=tick[:1] if not full else [],
        )
        gradients[i] = out
        tick.append(out[0])

    for step in range(len(far_steps) + 1):
        flying = 0
        now = far_steps[step] if step < len(far_steps) else [None, None]
        for lane in (0, 1):
            if lane == 1 and now[1] == ("cots", None):
                continue
            if now[lane] is not None:
                after = []
                if lanes_before[lane] is not None:
                    (d, i), array = lanes_before[lane]
                    lanes_before[lane] = None
                    after.append(array)
                    if d == "cots":
                        cots[half] = cots_at(array, 0)
                    else:
                        first = pieces[i][0] if i is not None else 0
                        ready += [
                            (d, j, array, at - first) for j, (at, _) in enumerate(pieces) if i is None or i == j
                        ]
                d, i = now[lane]
                if d != "wait":
                    first, width = pieces[i] if i is not None else (0, own_width)
                    array = send("tok", d, [(outgoing[d], first, width)], after)[1]
                    lanes_before[lane] = (now[lane], array)
            flying += lanes_before[lane] is not None
        for entry in list(near_before):
            due, d, array = entry
            if due > step:
                flying += 1
                continue
            near_before.remove(entry)
            ready += [(d, i, array, first) for i, (first, _) in enumerate(pieces)]
            if rides(d):
                cots[d] = cots_at(array, own_width)
        arrivals = finish_relays(step)
        if cross_before is not None:
            crossed.append(cross_before)
        earlier = [cross_before[2]] if cross_before is not None else []
        earlier += [core_before[1]] if core_before is not None else []
        cross_before = None
        if ready:
            blocks = []
            while ready and sum(pieces[i][1] for _, i, _, _ in blocks) < 2 * own_width:
                blocks.append(ready.pop(0))
            parts = [(array, first, pieces[i][1]) for _, i, array, first in blocks]
            own, other = send("user", across, parts, earlier)
            earlier = []
            cross_before = (blocks, own, other)
            flying += 1
        bit, sent = half // 2, False
        while bit:
            sources = [d for d in sorted(cots) if bit in bits_below(d) and d + bit not in relayed]
            if sources and step > 0 and (step > 5 or (flying < 5 and not sent)):
                relayed.update(d + bit for d in sources)
                parts = [part for d in sources for part in cot_parts(d)]
                relay_before.append((step + (1 if step < 3 else 2), bit, sources, send("tok", bit, parts, earlier)[1]))
                earlier = []
                flying += 1
                sent = True
            bit //= 2
        if step == 0:
            cots[0] = [(block, 0) for block in by_slot]
            cots[0] = cots_at(join(cot_parts(0), tick), 0)
            lanes_before[1] = (("cots", None), send("tok", half, cot_parts(0))[1])
            flying += 1
        if step < len(near_steps):
            for d in near_steps[step]:
                parts = [(outgoing[d], 0, own_width)]
                if rides(d):
                    parts += cot_parts(0)
                near_before.append((step + (3 if step else 1), d, send("tok", d, parts)[1]))
                flying += 1
        before = [core_before[1]] if core_before else []
        finish_core()
        if crossed and (flying < 5 or step >= len(far_steps) - 3):
            parts = []
            for blocks, own, other in crossed:
                total = sum(pieces[i][1] for _, i, _, _ in blocks)
                parts += [(own, 0, total), (other, 0, total)]
            core_before = (list(crossed), send("user", core, parts, before)[1])
            crossed.clear()
            flying += 1
        if step < len(far_steps):
            tick[:] = [hold(tick[0], arrivals + earlier, max(sizes))]
            sizes[:] = [0]
        if step == len(far_steps) - 3:
            add_products(0)
        elif step == len(far_steps) - 2:
            add_products(1)
        elif step == len(far_steps) - 1:
            finish_core()
            add_products(0)
    finish_core()
    add_products(0)
    add_products(1)
    sums = lax.all_to_all(gradients[1][1], ("user", "tok"), split_axis=0, concat_axis=0, tiled=True)
    return combine(user, sums, [g[0] for g in gradients], clip_bound, scaling)


def solution(mesh):
    return jax.shard_map(
        body,
        mesh=mesh,
        in_specs=(P("user", "tok", None), P("user", "tok", None), P("user")),
        out_specs=P("tok", "user"),
        check_vma=False,
    )
```
